256 devices in a mesh: seq: 32 (over x, z), own: 8 (over y, core).
Axes of the slice: x: 4, y: 4, z: 8, core: 2. Of those that a mesh axis runs over, the one named last changes fastest.
Arguments:
- queries: bfloat16 [8192, 8192], P('seq', 'own'), may hold values from -75 to 75
- key_rows: bfloat16 [8192, 1024], P('seq', 'own'), may hold values from -6 to 6
- value_rows: bfloat16 [8192, 1024], P('seq', 'own'), may hold values from -6 to 6
- out_grad: bfloat16 [8192, 8192], P('seq', 'own'), may hold values from -6 to 6
- inputs: bfloat16 [8192, 8192], P('seq', 'own'), may hold values from -6 to 6
- key_weight: bfloat16 [8192, 1024], P('own', 'seq'), may hold values from -0.0625 to 0.0625
- value_weight: bfloat16 [8192, 1024], P('own', 'seq'), may hold values from -0.0625 to 0.0625
- far_blocks: int32 [64, 4], P('seq'), may hold values from 0 to 60, as said below
- far_count: int32 [64], P('seq'), may hold values from 0 to 4, as said below
Outputs:
- query_grad: bfloat16 [8192, 8192], P('seq', 'own')
- input_grad: bfloat16 [8192, 8192], P('seq', 'own')
- key_weight_grad: float32 [8192, 1024], P('own', 'seq')
- value_weight_grad: float32 [8192, 1024], P('own', 'seq')
The draws below stay inside these ranges and needn't reach their ends.
Inputs may be any that keep to these rules, and one draw needn't show every extreme that they name: `far_blocks`: the first far_count[i] entries of row i are distinct blocks below i - 2; the other entries are 0. far_count[i] is at most min(4, i - 2) and at least 1 where that bound is positive.
All inputs are finite; a program needn't handle non-finite values.
Results may differ from the reference program's by a relative error of at most 0.0095.
Values may be sent and summed in bfloat16 or wider, within the bound.
No kernel may reach another device: no remote copies, remote signals or barrier semaphores. Data moves between devices by JAX's collectives and lax.ppermute only.
A program may use at most 128 MiB of HBM per device.

```python
import math
import jax
import jax.numpy as jnp
from jax import lax

D = 8192
DH = 128
GQ = 8
BLK = 128
WIN = 3
FARS = 4
KV = 8
HEADS = 64
SEQ = 8192
BLOCKS = 64


def far_lists(key):
    row_ids = jnp.arange(BLOCKS, dtype=jnp.int32)
    available = jnp.maximum(row_ids - WIN + 1, 0)
    order_key = jax.random.fold_in(key, 11)
    count_key = jax.random.fold_in(key, 12)
    rank_keys = jax.random.randint(order_key, (BLOCKS, BLOCKS), 0, 4096) * BLOCKS + row_ids[None, :]
    rank_keys = jnp.where(row_ids[None, :] < available[:, None], rank_keys, 4096 * BLOCKS + row_ids[None, :])
    last_top = (row_ids[:, None] == BLOCKS - 1) & (row_ids[None, :] == available[:, None] - 1)
    rank_keys = jnp.where(last_top, -1, rank_keys)
    ordering = jnp.argsort(rank_keys, axis=1, stable=True)[:, :FARS].astype(jnp.int32)
    drawn = jax.random.randint(count_key, (BLOCKS,), 1, FARS + 1)
    wanted = jnp.where(row_ids == WIN - 1 + FARS, FARS, drawn)
    live_count = jnp.minimum(available, wanted).astype(jnp.int32)
    slot_ids = jnp.arange(FARS, dtype=jnp.int32)
    blocks_used = jnp.where(slot_ids[None, :] < live_count[:, None], ordering, 0).astype(jnp.int32)
    return (blocks_used, live_count)


def draw_far_blocks(key, part):
    shared = far_lists(key)
    return shared[0]


def draw_far_count(key, part):
    shared = far_lists(key)
    return shared[1]


def draw_key_rows(key, part):
    key = jax.random.fold_in(key, 4)
    entries = jnp.clip(jax.random.normal(key, (SEQ, KV * DH), jnp.float32), -6.0, 6.0)
    return entries.astype(jnp.bfloat16)


def draw_queries(key, part):
    key = jax.random.fold_in(key, 6)
    entries = jnp.clip(jax.random.normal(key, (SEQ, HEADS * DH), jnp.float32), -6.0, 6.0)
    return entries.astype(jnp.bfloat16)


def level_of(own_key, dims, cuts, low, high):
    gain, own = 1.0, jax.random.fold_in(own_key, 6)
    for axis_at, parts in cuts:
        steps = jnp.exp(jax.random.uniform(jax.random.fold_in(own, axis_at), (parts,), jnp.float32, low / len(cuts), high / len(cuts)))
        gain = gain * jnp.repeat(steps, dims[axis_at] // parts).reshape([-1 if axis == axis_at else 1 for axis in range(len(dims))])
    return gain


def centred(rng, dims, spread, reach, cuts=(), held_as=jnp.bfloat16):
    array = spread * jax.random.normal(rng, dims, jnp.float32)
    if cuts:
        array = array * level_of(rng, dims, cuts, -0.22, 0.18)
    return jnp.clip(array, -reach, reach).astype(held_as)


def setup_inputs(seed: int = 0) -> dict:
    key_of = jax.random.split(jax.random.key(seed), 10)
    queries = draw_queries(jax.random.fold_in(key_of[9], 71), 0)
    key_rows = draw_key_rows(jax.random.fold_in(key_of[9], 71), 0)
    value_rows = centred(key_of[2], (SEQ, KV * DH), 1.0, 6.0, ((0, 32), (1, 8)))
    out_grad = centred(key_of[3], (SEQ, HEADS * DH), 1.0, 6.0, ((0, 32), (1, 8)))
    inputs = centred(key_of[4], (SEQ, D), 1.0, 6.0, ((0, 32), (1, 8)))
    key_weight = centred(key_of[5], (D, KV * DH), D ** -0.5, 0.0625, ((0, 8), (1, 32)))
    value_weight = centred(key_of[6], (D, KV * DH), D ** -0.5, 0.0625, ((0, 8), (1, 32)))
    far_blocks = draw_far_blocks(jax.random.fold_in(key_of[9], 71), 0)
    far_count = draw_far_count(jax.random.fold_in(key_of[9], 71), 0)
    return {"queries": queries, "key_rows": key_rows, "value_rows": value_rows, "out_grad": out_grad, "inputs": inputs, "key_weight": key_weight, "value_weight": value_weight, "far_blocks": far_blocks, "far_count": far_count}


def attend_block(query_block, grad_block, key_block, value_block, allowed):
    count_rows = query_block.shape[0]
    inv_root = 1.0 / math.sqrt(DH)
    q_heads = query_block.reshape(count_rows, GQ, DH).transpose(1, 0, 2).reshape(GQ * count_rows, DH)
    g_heads = grad_block.reshape(count_rows, GQ, DH).transpose(1, 0, 2).reshape(GQ * count_rows, DH)
    scores = lax.dot_general(q_heads, key_block, (((1,), (1,)), ((), ())), preferred_element_type=jnp.float32) * inv_root
    wide_mask = jnp.tile(allowed, (GQ, 1))
    scores = jnp.where(wide_mask, scores, jnp.float32(-1e+30))
    row_max = lax.optimization_barrier(jnp.max(scores, axis=1, keepdims=True))
    exp_scores = jnp.exp(scores - row_max)
    soft_p = exp_scores / lax.optimization_barrier(jnp.sum(exp_scores, axis=1, keepdims=True))
    soft_b = soft_p.astype(jnp.bfloat16)
    output = jnp.dot(soft_b, value_block, preferred_element_type=jnp.float32)
    deltas = lax.optimization_barrier(jnp.sum(g_heads.astype(jnp.float32) * output, axis=1, keepdims=True))
    grad_p = lax.dot_general(g_heads, value_block, (((1,), (1,)), ((), ())), preferred_element_type=jnp.float32)
    grad_sb = (soft_p * (grad_p - deltas) * inv_root).astype(jnp.bfloat16)
    grad_q = jnp.dot(grad_sb, key_block, preferred_element_type=jnp.float32).astype(jnp.bfloat16)
    grad_q = grad_q.reshape(GQ, count_rows, DH).transpose(1, 0, 2).reshape(count_rows, GQ * DH)
    grad_k = lax.dot_general(grad_sb, q_heads, (((0,), (0,)), ((), ())), preferred_element_type=jnp.float32)
    grad_v = lax.dot_general(soft_b, g_heads, (((0,), (0,)), ((), ())), preferred_element_type=jnp.float32)
    return (grad_q, grad_k, grad_v)

def block_mask(block_index, live_count):
    query_pos = block_index * BLK + jnp.arange(BLK, dtype=jnp.int32)[:, None]
    key_pos = (block_index - WIN + 1) * BLK + jnp.arange(WIN * BLK, dtype=jnp.int32)[None, :]
    window_ok = (key_pos <= query_pos) & (key_pos >= 0)
    far_slots = (jnp.arange(FARS * BLK, dtype=jnp.int32) // BLK)[None, :]
    far_ok = jnp.broadcast_to(far_slots < live_count, (BLK, FARS * BLK))
    return jnp.concatenate([window_ok, far_ok], axis=1)

def add_into(buffer, addend, offset):
    current = lax.dynamic_slice_in_dim(buffer, offset, addend.shape[0], 0)
    return lax.dynamic_update_slice_in_dim(buffer, current + addend, offset, 0)

def reference(queries, key_rows, value_rows, out_grad, inputs, key_weight, value_weight, far_blocks, far_count):
    halo_rows = (WIN - 1) * BLK
    total_rows = queries.shape[0]
    block_total = total_rows // BLK
    grads_query = []
    grads_key = []
    grads_value = []
    for head_index in range(KV):
        query_part = queries[:, head_index * GQ * DH:(head_index + 1) * GQ * DH]
        grad_part = out_grad[:, head_index * GQ * DH:(head_index + 1) * GQ * DH]
        key_part = key_rows[:, head_index * DH:(head_index + 1) * DH]
        value_part = value_rows[:, head_index * DH:(head_index + 1) * DH]
        zero_front = jnp.zeros((halo_rows, DH), jnp.bfloat16)
        keys_padded = jnp.concatenate([zero_front, key_part])
        values_padded = jnp.concatenate([zero_front, value_part])

        def advance(loop_state, block_index):
            key_acc, value_acc = loop_state
            query_block = lax.dynamic_slice_in_dim(query_part, block_index * BLK, BLK, 0)
            grad_block = lax.dynamic_slice_in_dim(grad_part, block_index * BLK, BLK, 0)
            listed = lax.dynamic_index_in_dim(far_blocks, block_index, 0, keepdims=False)
            live_count = lax.dynamic_index_in_dim(far_count, block_index, 0, keepdims=False)
            key_parts = [lax.dynamic_slice_in_dim(keys_padded, block_index * BLK, WIN * BLK, 0)]
            value_parts = [lax.dynamic_slice_in_dim(values_padded, block_index * BLK, WIN * BLK, 0)]
            for slot_index in range(FARS):
                key_parts.append(lax.dynamic_slice_in_dim(key_part, listed[slot_index] * BLK, BLK, 0))
                value_parts.append(lax.dynamic_slice_in_dim(value_part, listed[slot_index] * BLK, BLK, 0))
            allowed = block_mask(block_index, live_count)
            grad_q, grad_k, grad_v = attend_block(query_block, grad_block, jnp.concatenate(key_parts), jnp.concatenate(value_parts), allowed)
            key_acc = add_into(key_acc, grad_k[:WIN * BLK], block_index * BLK)
            value_acc = add_into(value_acc, grad_v[:WIN * BLK], block_index * BLK)
            for slot_index in range(FARS):
                far_start = halo_rows + listed[slot_index] * BLK
                lower = (WIN + slot_index) * BLK
                key_acc = add_into(key_acc, grad_k[lower:lower + BLK], far_start)
                value_acc = add_into(value_acc, grad_v[lower:lower + BLK], far_start)
            return ((key_acc, value_acc), grad_q)
        zero_acc = jnp.zeros((halo_rows + total_rows, DH), jnp.float32)
        final_state, query_blocks = lax.scan(advance, (zero_acc, zero_acc), jnp.arange(block_total, dtype=jnp.int32))
        grads_query.append(query_blocks.reshape(total_rows, GQ * DH))
        grads_key.append(final_state[0][halo_rows:].astype(jnp.bfloat16))
        grads_value.append(final_state[1][halo_rows:].astype(jnp.bfloat16))
    query_grad = jnp.concatenate(grads_query, axis=1)
    key_grad = jnp.concatenate(grads_key, axis=1)
    value_grad = jnp.concatenate(grads_value, axis=1)
    input_grad = jnp.dot(key_grad, key_weight.T, preferred_element_type=jnp.float32) + jnp.dot(value_grad, value_weight.T, preferred_element_type=jnp.float32)
    key_weight_grad = jnp.dot(inputs.T, key_grad, preferred_element_type=jnp.float32)
    value_weight_grad = jnp.dot(inputs.T, value_grad, preferred_element_type=jnp.float32)
    return (query_grad, input_grad.astype(jnp.bfloat16), key_weight_grad, value_weight_grad)
```

```python
import functools
import math

import jax
import jax.numpy as jnp
from jax import lax
from jax.experimental import pallas as pl
from jax.experimental.pallas import tpu as pltpu
from jax.sharding import PartitionSpec as P

DH = 128
GQ = 8
BLK = 128
WIN = 3
FARS = 4
NX = 4
NZ = 8
NB = 2
PLANE = NB * NZ
SLOTS = NB * FARS
X_GROUPS = [[x * NZ + z for x in range(NX)] for z in range(NZ)]
Z_GROUPS = [[x * NZ + z for z in range(NZ)] for x in range(NX)]
SCALE = 1.0 / math.sqrt(DH)
EXP2_SCALE = SCALE * math.log2(math.e)
NEG = -1e30

SMEM = pl.BlockSpec(memory_space=pltpu.SMEM)
VMEM = pl.BlockSpec(memory_space=pltpu.VMEM)
NT = (((1,), (1,)), ((), ()))
F32 = jnp.float32
BF16 = jnp.bfloat16


def params(mib):
    return pltpu.CompilerParams(vmem_limit_bytes=mib << 20)


def shifted(value, axis, steps):
    count = lax.axis_size(axis)
    leading, last = (max(0, -steps), min(count, count - steps))
    return lax.ppermute(value, axis, [(source, source + steps) for source in range(leading, last)])


def pick_kernel(lists_ref, plane_ref, out_ref):
    def body(i, carry):
        row = pl.multiple_of(lax.rem(lists_ref[i], PLANE) * BLK, BLK)
        out_ref[i] = plane_ref[pl.ds(row, BLK), :]
        return carry

    lax.fori_loop(0, NX * SLOTS, body, 0)


def pick(lists, plane):
    return pl.pallas_call(
        pick_kernel,
        out_shape=jax.ShapeDtypeStruct((NX * SLOTS, BLK, 2 * DH), BF16),
        in_specs=[SMEM, VMEM],
        out_specs=VMEM,
        compiler_params=params(16),
        name="pick_far",
    )(lists, plane)


def attend_kernel(
    at_ref, far_ref, count_ref, q_ref, g_ref, prev_ref, own_ref, far_kv_ref,
    qg_ref, win_ref, farg_ref, k_ref, v_ref, kt_ref, acc_ref, tri_ref,
):
    win_ref[...] = jnp.zeros_like(win_ref)
    key_at = lax.broadcasted_iota(jnp.int32, (BLK, 2 * BLK), 0)
    query_at = lax.broadcasted_iota(jnp.int32, (BLK, 2 * BLK), 1) % BLK
    tri_ref[...] = jnp.where(key_at <= query_at, 0.0, NEG)

    def block(b, carry):
        index = at_ref[0] * NB + b
        for w in range(WIN):
            local = b + w
            lower = pl.multiple_of(lax.rem(local, NB) * BLK, BLK)
            before = prev_ref[pl.ds(lower, BLK), :]
            mine = own_ref[pl.ds(lower, BLK), :]
            both = jnp.where(local < NB, before, mine)
            k_ref[w * BLK : (w + 1) * BLK, :] = both[:, :DH]
            v_ref[w * BLK : (w + 1) * BLK, :] = both[:, DH:]
        for j in range(FARS):
            slot = b * FARS + j
            owner = lax.div(far_ref[slot], PLANE)
            both = far_kv_ref[owner * SLOTS + slot]
            k_ref[(WIN + j) * BLK : (WIN + j + 1) * BLK, :] = both[:, :DH]
            v_ref[(WIN + j) * BLK : (WIN + j + 1) * BLK, :] = both[:, DH:]
        kt_ref[...] = k_ref[...].astype(F32).T.astype(BF16)
        acc_ref[...] = jnp.zeros_like(acc_ref)
        biases = [
            jnp.where(index >= 2, 0.0, NEG).astype(F32),
            jnp.where(index >= 1, 0.0, NEG).astype(F32),
            None,
        ] + [jnp.where(j < count_ref[b], 0.0, NEG).astype(F32) for j in range(FARS)]
        rows = pl.ds(pl.multiple_of(b * BLK, BLK), BLK)
        for pair in range(GQ // 2):
            lo = pair * 2 * DH
            q2 = jnp.concatenate([q_ref[rows, lo : lo + DH], q_ref[rows, lo + DH : lo + 2 * DH]])
            g2 = jnp.concatenate([g_ref[rows, lo : lo + DH], g_ref[rows, lo + DH : lo + 2 * DH]])
            scores = lax.dot_general(k_ref[...], q2, NT, preferred_element_type=F32)
            parts = []
            for c in range(WIN + FARS):
                part = scores[c * BLK : (c + 1) * BLK, :]
                bias = tri_ref[...] if biases[c] is None else biases[c]
                parts.append(part + bias)
            scores = jnp.concatenate(parts)
            top = jnp.max(scores, axis=0, keepdims=True)
            expo = jnp.exp2((scores - top) * EXP2_SCALE)
            inv = 1.0 / jnp.sum(expo, axis=0, keepdims=True)
            soft = expo * inv
            grad_p = lax.dot_general(v_ref[...], g2, NT, preferred_element_type=F32)
            delta = jnp.sum(soft * grad_p, axis=0, keepdims=True)
            soft_b = soft.astype(BF16)
            grad_s = (soft * (grad_p - delta)).astype(BF16)
            acc_ref[:, :DH] += jnp.dot(grad_s, q2, preferred_element_type=F32)
            acc_ref[:, DH:] += jnp.dot(soft_b, g2, preferred_element_type=F32)
            grad_q = jnp.dot(kt_ref[...], grad_s, preferred_element_type=F32).T * SCALE
            qg_ref[rows, lo : lo + DH] = grad_q[:BLK].astype(BF16)
            qg_ref[rows, lo + DH : lo + 2 * DH] = grad_q[BLK:].astype(BF16)
        acc_ref[:, :DH] = acc_ref[:, :DH] * SCALE
        window = pl.ds(pl.multiple_of(b * BLK, BLK), WIN * BLK)
        win_ref[window, :] += acc_ref[: WIN * BLK, :]
        for j in range(FARS):
            farg_ref[b * FARS + j] = acc_ref[(WIN + j) * BLK : (WIN + j + 1) * BLK, :].astype(BF16)
        return carry

    lax.fori_loop(0, NB, block, 0)


def attend(at, far, count, queries, out_grad, prev, own, far_kv):
    keys = (WIN + FARS) * BLK
    return pl.pallas_call(
        attend_kernel,
        out_shape=(
            jax.ShapeDtypeStruct((NB * BLK, GQ * DH), BF16),
            jax.ShapeDtypeStruct((2 * NB * BLK, 2 * DH), F32),
            jax.ShapeDtypeStruct((SLOTS, BLK, 2 * DH), BF16),
        ),
        in_specs=[SMEM, SMEM, SMEM] + [VMEM] * 5,
        out_specs=(VMEM, VMEM, VMEM),
        scratch_shapes=[
            pltpu.VMEM((keys, DH), BF16),
            pltpu.VMEM((keys, DH), BF16),
            pltpu.VMEM((DH, keys), BF16),
            pltpu.VMEM((keys, 2 * DH), F32),
            pltpu.VMEM((BLK, 2 * BLK), F32),
        ],
        compiler_params=params(40),
        cost_estimate=pl.CostEstimate(flops=2_400_000_000 * 4, bytes_accessed=6 << 20, transcendentals=2_000_000),
        name="attend",
    )(at, far, count, queries, out_grad, prev, own, far_kv)


def spread_kernel(x_ref, lists_ref, far_ref, out_ref, acc_ref):
    acc_ref[...] = jnp.zeros_like(acc_ref)

    def body(i, carry):
        listed = lists_ref[i]

        @pl.when(lax.div(listed, PLANE) == x_ref[0])
        def _():
            at = lax.rem(listed, PLANE)
            acc_ref[at] += far_ref[i].astype(F32)

        return carry

    lax.fori_loop(0, NX * SLOTS, body, 0)
    out_ref[...] = acc_ref[...].astype(BF16)


def spread(x_at, lists, far_all):
    return pl.pallas_call(
        spread_kernel,
        out_shape=jax.ShapeDtypeStruct((PLANE, BLK, 2 * DH), BF16),
        in_specs=[SMEM, SMEM, VMEM],
        out_specs=VMEM,
        scratch_shapes=[pltpu.VMEM((PLANE, BLK, 2 * DH), F32)],
        compiler_params=params(16),
        name="spread_far",
    )(x_at, lists, far_all)


def local(
    queries, key_rows, value_rows, out_grad, inputs, key_weight, value_weight, far_blocks, far_count
):
    tokens = queries.shape[0]
    seq_index = lax.axis_index("seq").astype(jnp.int32)
    x_index = lax.div(seq_index, NZ)
    at = seq_index.reshape(1)
    own_kv = jnp.concatenate([key_rows, value_rows], axis=1)

    lists = lax.all_gather(far_blocks, "seq", axis=0, axis_index_groups=X_GROUPS, tiled=True)
    lists = lists.reshape(NX * SLOTS)
    prev_kv = shifted(own_kv, "seq", 1)
    plane = lax.all_gather(own_kv, "seq", axis=0, axis_index_groups=Z_GROUPS, tiled=True)
    chosen = pick(lists, plane)
    far_kv = lax.all_to_all(chosen, "seq", 0, 0, axis_index_groups=X_GROUPS, tiled=True)

    key_weight, value_weight, inputs, far_kv = lax.optimization_barrier(
        (key_weight, value_weight, inputs, far_kv)
    )
    key_proj = lax.all_gather(key_weight.T, "seq", axis=0, tiled=True)
    value_proj = lax.all_gather(value_weight.T, "seq", axis=0, tiled=True)
    inputs_x = lax.all_gather(inputs, "seq", axis=0, axis_index_groups=X_GROUPS, tiled=True)

    query_grad, window, far_grad = attend(
        at, far_blocks.reshape(SLOTS), far_count, queries, out_grad, prev_kv, own_kv, far_kv
    )
    back = shifted(window[:tokens].astype(BF16), "seq", -1)
    far_all = lax.all_gather(far_grad, "seq", axis=0, axis_index_groups=X_GROUPS, tiled=True)
    dense = spread(x_index.reshape(1), lists, far_all)
    dense = dense.reshape(NZ, tokens, 2 * DH)
    terms = lax.all_to_all(dense, "seq", 0, 0, axis_index_groups=Z_GROUPS, tiled=True)
    kv_grad = jnp.sum(terms.astype(F32), axis=0) + back.astype(F32) + window[tokens:]
    kv_grad = kv_grad.astype(BF16)

    heads = lax.all_gather(kv_grad, "own", axis=0)
    key_all = heads[:, :, :DH].transpose(1, 0, 2).reshape(tokens, -1)
    value_all = heads[:, :, DH:].transpose(1, 0, 2).reshape(tokens, -1)
    input_grad = jnp.dot(key_all, key_proj, preferred_element_type=F32) + jnp.dot(
        value_all, value_proj, preferred_element_type=F32
    )

    quarter = lax.all_to_all(heads, "seq", 0, 0, axis_index_groups=X_GROUPS, tiled=True)
    quarter = quarter.reshape(NX, 2, tokens, 2, DH).transpose(1, 3, 4, 0, 2)
    quarter = quarter.reshape(4 * DH, NX * tokens)
    weight_t = jnp.dot(quarter, inputs_x, preferred_element_type=F32).astype(BF16)
    width = weight_t.shape[1]
    weight_t = weight_t.reshape(2, 2, 4, 32, width).transpose(0, 2, 1, 3, 4).reshape(NZ, 64, width)
    pieces = lax.all_to_all(weight_t, "seq", 0, 0, axis_index_groups=Z_GROUPS, tiled=True)
    weight_grad = jnp.sum(pieces.astype(F32), axis=0)
    return (
        query_grad,
        input_grad.astype(BF16),
        weight_grad[:32].T,
        weight_grad[32:].T,
    )


def solution(mesh):
    return jax.shard_map(
        local,
        mesh=mesh,
        in_specs=(
            P("seq", "own"),
            P("seq", "own"),
            P("seq", "own"),
            P("seq", "own"),
            P("seq", "own"),
            P("own", "seq"),
            P("own", "seq"),
            P("seq", None),
            P("seq"),
        ),
        out_specs=(P("seq", "own"), P("seq", "own"), P("own", "seq"), P("own", "seq")),
        check_vma=False,
    )
```

```python
import functools
import math

import jax
import jax.numpy as jnp
from jax import lax
from jax.experimental import pallas as pl
from jax.experimental.pallas import tpu as pltpu
from jax.sharding import PartitionSpec as P

DH = 128
GQ = 8
BLK = 128
WIN = 3
FARS = 4
NX = 4
NZ = 8
NB = 2
PLANE = NB * NZ
SLOTS = NB * FARS
X_GROUPS = [[x * NZ + z for x in range(NX)] for z in range(NZ)]
Z_GROUPS = [[x * NZ + z for z in range(NZ)] for x in range(NX)]
Z_UP = [(x * NZ + z, x * NZ + (z + 1) % NZ) for x in range(NX) for z in range(NZ)]
X_UP = [(x * NZ + z, (x + 1) % NX * NZ + z) for x in range(NX) for z in range(NZ)]
NY = 4
Y_UP = [(2 * y + core, 2 * ((y + 1) % NY) + core) for y in range(NY) for core in range(2)]
CORES = [(own, own ^ 1) for own in range(2 * NY)]
SCALE = 1.0 / math.sqrt(DH)
EXP2_SCALE = SCALE * math.log2(math.e)
NEG = -1e30

SMEM = pl.BlockSpec(memory_space=pltpu.SMEM)
VMEM = pl.BlockSpec(memory_space=pltpu.VMEM)
NT = (((1,), (1,)), ((), ()))
F32 = jnp.float32
BF16 = jnp.bfloat16


def params(mib):
    return pltpu.CompilerParams(vmem_limit_bytes=mib << 20)


def shifted(value, axis, steps):
    count = lax.axis_size(axis)
    leading, last = (max(0, -steps), min(count, count - steps))
    return lax.ppermute(value, axis, [(source, source + steps) for source in range(leading, last)])


def both_ways(upward, downward, axis, pairs):
    back = [(target, source) for source, target in pairs]
    return lax.ppermute(upward, axis, pairs), lax.ppermute(downward, axis, back)


def ring_gather(value, axis, pairs, count):
    half = value.shape[0] // 2
    from_below, from_above = value, value
    pieces = []
    for distance in range(1, count // 2 + 1):
        if distance == count // 2:
            from_below, from_above = from_below[:half], from_above[half:]
        from_below, from_above = both_ways(from_below, from_above, axis, pairs)
        pieces += [from_below, from_above]
    return pieces


def place_pieces(out_ref, at, own_ref, pieces, count, size):
    half = size // 2
    out_ref[pl.ds(at * size, size)] = own_ref[...]
    for distance in range(1, count // 2 + 1):
        below = lax.rem(at + (count - distance), count) * size
        above = lax.rem(at + distance, count) * size
        if distance == count // 2:
            out_ref[pl.ds(below, half)] = pieces[2 * distance - 2][...]
            out_ref[pl.ds(below + half, half)] = pieces[2 * distance - 1][...]
        else:
            out_ref[pl.ds(below, size)] = pieces[2 * distance - 2][...]
            out_ref[pl.ds(above, size)] = pieces[2 * distance - 1][...]


def pick_kernel(z_ref, lists_ref, own_ref, *refs):
    *pieces, out_ref, plane_ref = refs
    place_pieces(plane_ref, z_ref[0], own_ref, pieces, NZ, NB)

    def body(i, carry):
        out_ref[i] = plane_ref[lax.rem(lists_ref[i], PLANE)]
        return carry

    lax.fori_loop(0, NX * SLOTS, body, 0)


def pick(z_at, lists, own, pieces):
    return pl.pallas_call(
        pick_kernel,
        out_shape=jax.ShapeDtypeStruct((NX * SLOTS, BLK, 2 * DH), BF16),
        in_specs=[SMEM, SMEM] + [VMEM] * (1 + len(pieces)),
        out_specs=VMEM,
        scratch_shapes=[pltpu.VMEM((PLANE, BLK, 2 * DH), BF16)],
        compiler_params=params(16),
        name="pick_far",
    )(z_at, lists, own, *pieces)


def attend_kernel(
    at_ref, far_ref, count_ref, q_ref, g_ref, prev_ref, own_ref, far_kv_ref,
    qg_ref, win_ref, farg_ref, k_ref, v_ref, kt_ref, acc_ref, tri_ref,
):
    win_ref[...] = jnp.zeros_like(win_ref)
    key_at = lax.broadcasted_iota(jnp.int32, (BLK, 2 * BLK), 0)
    query_at = lax.broadcasted_iota(jnp.int32, (BLK, 2 * BLK), 1) % BLK
    tri_ref[...] = jnp.where(key_at <= query_at, 0.0, NEG)

    def block(b, carry):
        index = at_ref[0] * NB + b
        for w in range(WIN):
            local = b + w
            lower = pl.multiple_of(lax.rem(local, NB) * BLK, BLK)
            before = prev_ref[pl.ds(lower, BLK), :]
            mine = own_ref[pl.ds(lower, BLK), :]
            both = jnp.where(local < NB, before, mine)
            k_ref[w * BLK : (w + 1) * BLK, :] = both[:, :DH]
            v_ref[w * BLK : (w + 1) * BLK, :] = both[:, DH:]
        for j in range(FARS):
            slot = b * FARS + j
            owner = lax.div(far_ref[slot], PLANE)
            both = far_kv_ref[owner * SLOTS + slot]
            k_ref[(WIN + j) * BLK : (WIN + j + 1) * BLK, :] = both[:, :DH]
            v_ref[(WIN + j) * BLK : (WIN + j + 1) * BLK, :] = both[:, DH:]
        kt_ref[...] = k_ref[...].astype(F32).T.astype(BF16)
        acc_ref[...] = jnp.zeros_like(acc_ref)
        biases = [
            jnp.where(index >= 2, 0.0, NEG).astype(F32),
            jnp.where(index >= 1, 0.0, NEG).astype(F32),
            None,
        ] + [jnp.where(j < count_ref[b], 0.0, NEG).astype(F32) for j in range(FARS)]
        rows = pl.ds(pl.multiple_of(b * BLK, BLK), BLK)
        for pair in range(GQ // 2):
            lo = pair * 2 * DH
            q2 = jnp.concatenate([q_ref[rows, lo : lo + DH], q_ref[rows, lo + DH : lo + 2 * DH]])
            g2 = jnp.concatenate([g_ref[rows, lo : lo + DH], g_ref[rows, lo + DH : lo + 2 * DH]])
            scores = lax.dot_general(k_ref[...], q2, NT, preferred_element_type=F32)
            parts = []
            for c in range(WIN + FARS):
                part = scores[c * BLK : (c + 1) * BLK, :]
                bias = tri_ref[...] if biases[c] is None else biases[c]
                parts.append(part + bias)
            scores = jnp.concatenate(parts)
            top = jnp.max(scores, axis=0, keepdims=True)
            expo = jnp.exp2((scores - top) * EXP2_SCALE)
            inv = 1.0 / jnp.sum(expo, axis=0, keepdims=True)
            soft = expo * inv
            grad_p = lax.dot_general(v_ref[...], g2, NT, preferred_element_type=F32)
            delta = jnp.sum(soft * grad_p, axis=0, keepdims=True)
            soft_b = soft.astype(BF16)
            grad_s = (soft * (grad_p - delta)).astype(BF16)
            acc_ref[:, :DH] += jnp.dot(grad_s, q2, preferred_element_type=F32)
            acc_ref[:, DH:] += jnp.dot(soft_b, g2, preferred_element_type=F32)
            grad_q = jnp.dot(kt_ref[...], grad_s, preferred_element_type=F32).T * SCALE
            qg_ref[rows, lo : lo + DH] = grad_q[:BLK].astype(BF16)
            qg_ref[rows, lo + DH : lo + 2 * DH] = grad_q[BLK:].astype(BF16)
        acc_ref[:, :DH] = acc_ref[:, :DH] * SCALE
        window = pl.ds(pl.multiple_of(b * BLK, BLK), WIN * BLK)
        win_ref[window, :] += acc_ref[: WIN * BLK, :]
        for j in range(FARS):
            farg_ref[b * FARS + j] = acc_ref[(WIN + j) * BLK : (WIN + j + 1) * BLK, :].astype(BF16)
        return carry

    lax.fori_loop(0, NB, block, 0)


def attend(at, far, count, queries, out_grad, prev, own, far_kv):
    keys = (WIN + FARS) * BLK
    return pl.pallas_call(
        attend_kernel,
        out_shape=(
            jax.ShapeDtypeStruct((NB * BLK, GQ * DH), BF16),
            jax.ShapeDtypeStruct((2 * NB * BLK, 2 * DH), F32),
            jax.ShapeDtypeStruct((SLOTS, BLK, 2 * DH), BF16),
        ),
        in_specs=[SMEM, SMEM, SMEM] + [VMEM] * 5,
        out_specs=(VMEM, VMEM, VMEM),
        scratch_shapes=[
            pltpu.VMEM((keys, DH), BF16),
            pltpu.VMEM((keys, DH), BF16),
            pltpu.VMEM((DH, keys), BF16),
            pltpu.VMEM((keys, 2 * DH), F32),
            pltpu.VMEM((BLK, 2 * BLK), F32),
        ],
        compiler_params=params(40),
        cost_estimate=pl.CostEstimate(flops=2_400_000_000 * 4, bytes_accessed=6 << 20, transcendentals=2_000_000),
        name="attend",
    )(at, far, count, queries, out_grad, prev, own, far_kv)


def spread_kernel(x_ref, lists_ref, own_ref, *refs):
    *pieces, out_ref, far_ref, acc_ref = refs
    place_pieces(far_ref, x_ref[0], own_ref, pieces, NX, SLOTS)
    acc_ref[...] = jnp.zeros_like(acc_ref)

    def body(i, carry):
        listed = lists_ref[i]

        @pl.when(lax.div(listed, PLANE) == x_ref[0])
        def _():
            at = lax.rem(listed, PLANE)
            acc_ref[at] += far_ref[i].astype(F32)

        return carry

    lax.fori_loop(0, NX * SLOTS, body, 0)
    out_ref[...] = acc_ref[...].astype(BF16)


def spread(x_at, lists, own, pieces):
    return pl.pallas_call(
        spread_kernel,
        out_shape=jax.ShapeDtypeStruct((PLANE, BLK, 2 * DH), BF16),
        in_specs=[SMEM, SMEM] + [VMEM] * (1 + len(pieces)),
        out_specs=VMEM,
        scratch_shapes=[
            pltpu.VMEM((NX * SLOTS, BLK, 2 * DH), BF16),
            pltpu.VMEM((PLANE, BLK, 2 * DH), F32),
        ],
        compiler_params=params(24),
        name="spread_far",
    )(x_at, lists, own, *pieces)


def heads_kernel(at_ref, *refs):
    own_ref, *pieces, other_ref, stack_ref, wide_ref = refs
    at, core = lax.div(at_ref[0], 2), lax.rem(at_ref[0], 2)
    half = BLK * NB // 2

    def put(y, which, rows, value):
        head = 2 * y + which
        stack_ref[head, rows, :] = value
        wide_ref[rows, pl.ds(pl.multiple_of(head * 2 * DH, 2 * DH), 2 * DH)] = value

    everything = slice(0, 2 * half)
    below, above = lax.rem(at + NY - 1, NY), lax.rem(at + 1, NY)
    across = lax.rem(at + 2, NY)
    for which, mine in ((core, True), (1 - core, False)):
        parts = (
            (own_ref, *pieces)
            if mine
            else (
                other_ref.at[: 2 * half],
                other_ref.at[2 * half : 4 * half],
                other_ref.at[4 * half : 6 * half],
                other_ref.at[6 * half : 7 * half],
                other_ref.at[7 * half :],
            )
        )
        put(at, which, everything, parts[0][...])
        put(below, which, everything, parts[1][...])
        put(above, which, everything, parts[2][...])
        put(across, which, slice(0, half), parts[3][...])
        put(across, which, slice(half, 2 * half), parts[4][...])


def place_heads(at, own, pieces, other):
    tokens = own.shape[0]
    return pl.pallas_call(
        heads_kernel,
        out_shape=(
            jax.ShapeDtypeStruct((2 * NY, tokens, 2 * DH), BF16),
            jax.ShapeDtypeStruct((tokens, 2 * NY * 2 * DH), BF16),
        ),
        in_specs=[SMEM] + [VMEM] * (2 + len(pieces)),
        out_specs=(VMEM, VMEM),
        compiler_params=params(16),
        name="place_heads",
    )(at, own, *pieces, other)


def weights_kernel(grad_ref, inputs_ref, out_ref):
    columns = DH // 4
    for head in range(2):
        grad = jnp.concatenate([grad_ref[x * 2 + head] for x in range(NX)])
        term = lax.dot_general(
            grad, inputs_ref[...], (((0,), (0,)), ((), ())), preferred_element_type=F32
        ).astype(BF16)
        for part in range(4):
            for kind in range(2):
                lower = kind * DH + part * columns
                out_ref[head * 4 + part, kind * columns : (kind + 1) * columns, :] = term[
                    lower : lower + columns
                ]


def weight_terms(grad, inputs_x):
    return pl.pallas_call(
        weights_kernel,
        out_shape=jax.ShapeDtypeStruct((NZ, 2 * DH // 4, inputs_x.shape[1]), BF16),
        in_specs=[VMEM, VMEM],
        out_specs=VMEM,
        compiler_params=params(24),
        cost_estimate=pl.CostEstimate(flops=1 << 30, bytes_accessed=4 << 20, transcendentals=0),
        name="weight_terms",
    )(grad, inputs_x)


def local(
    queries, key_rows, value_rows, out_grad, inputs, key_weight, value_weight, far_blocks, far_count
):
    tokens = queries.shape[0]
    seq_index = lax.axis_index("seq").astype(jnp.int32)
    x_index = lax.div(seq_index, NZ)
    at = seq_index.reshape(1)
    own_index = lax.axis_index("own").astype(jnp.int32).reshape(1)
    z_at = lax.rem(seq_index, NZ).reshape(1)
    x_at = x_index.reshape(1)
    own_kv = jnp.concatenate([key_rows, value_rows], axis=1)

    inputs_x = lax.all_gather(inputs, "seq", axis=0, axis_index_groups=X_GROUPS, tiled=True)
    weights = jnp.concatenate([key_weight.T, value_weight.T])
    weights = lax.all_gather(weights, "seq", axis=0, tiled=True)
    columns = DH // 4
    weights = weights.reshape(2 * NY, 4, 2, columns, -1).transpose(0, 2, 1, 3, 4)
    weights = weights.reshape(2 * NY * 2 * DH, -1)

    own_blocks = own_kv.reshape(NB, BLK, 2 * DH)
    plane = ring_gather(own_blocks, "seq", Z_UP, NZ)
    prev_kv = shifted(own_kv, "seq", 1)
    lists = lax.all_gather(far_blocks, "seq", axis=0, axis_index_groups=X_GROUPS, tiled=True)
    lists = lists.reshape(NX * SLOTS)
    chosen = pick(z_at, lists, own_blocks, plane)
    far_kv = lax.all_to_all(chosen, "seq", 0, 0, axis_index_groups=X_GROUPS, tiled=True)

    query_grad, window, far_grad = attend(
        at, far_blocks.reshape(SLOTS), far_count, queries, out_grad, prev_kv, own_kv, far_kv
    )
    far_all = ring_gather(far_grad, "seq", X_UP, NX)
    back = shifted(window[:tokens].astype(BF16), "seq", -1)
    dense = spread(x_at, lists, far_grad, far_all)
    dense = dense.reshape(NZ, tokens, 2 * DH)
    terms = lax.all_to_all(dense, "seq", 0, 0, axis_index_groups=Z_GROUPS, tiled=True)
    kv_grad = jnp.sum(terms.astype(F32), axis=0) + back.astype(F32) + window[tokens:]
    kv_grad = kv_grad.astype(BF16)

    same_core = ring_gather(kv_grad, "own", Y_UP, NY)
    other_core = lax.ppermute(jnp.concatenate([kv_grad, *same_core]), "own", CORES)
    stacked, wide = place_heads(own_index, kv_grad, same_core, other_core)
    quarter = lax.all_to_all(stacked, "seq", 0, 0, axis_index_groups=X_GROUPS, tiled=True)
    pieces = weight_terms(quarter, inputs_x)
    pieces = lax.all_to_all(pieces, "seq", 0, 0, axis_index_groups=Z_GROUPS, tiled=True)
    input_grad = jnp.dot(wide, weights, preferred_element_type=F32)
    weight_grad = jnp.sum(pieces.astype(F32), axis=0)
    return (
        query_grad,
        input_grad.astype(BF16),
        weight_grad[:columns].T,
        weight_grad[columns:].T,
    )


def solution(mesh):
    return jax.shard_map(
        local,
        mesh=mesh,
        in_specs=(
            P("seq", "own"),
            P("seq", "own"),
            P("seq", "own"),
            P("seq", "own"),
            P("seq", "own"),
            P("own", "seq"),
            P("own", "seq"),
            P("seq", None),
            P("seq"),
        ),
        out_specs=(P("seq", "own"), P("seq", "own"), P("own", "seq"), P("own", "seq")),
        check_vma=False,
    )
```

```python
import functools
import math

import jax
import jax.numpy as jnp
from jax import lax
from jax.experimental import pallas as pl
from jax.experimental.pallas import tpu as pltpu
from jax.sharding import PartitionSpec as P

DH = 128
GQ = 8
BLK = 128
WIN = 3
FARS = 4
NX = 4
NZ = 8
NB = 2
PLANE = NB * NZ
SLOTS = NB * FARS
X_GROUPS = [[x * NZ + z for x in range(NX)] for z in range(NZ)]
Z_GROUPS = [[x * NZ + z for z in range(NZ)] for x in range(NX)]
Z_UP = [(x * NZ + z, x * NZ + (z + 1) % NZ) for x in range(NX) for z in range(NZ)]
X_UP = [(x * NZ + z, (x + 1) % NX * NZ + z) for x in range(NX) for z in range(NZ)]
X_ACROSS = [(x * NZ + z, (x + 2) % NX * NZ + z) for x in range(NX) for z in range(NZ)]
NY = 4
Y_UP = [(2 * y + core, 2 * ((y + 1) % NY) + core) for y in range(NY) for core in range(2)]
CORES = [(own, own ^ 1) for own in range(2 * NY)]
SCALE = 1.0 / math.sqrt(DH)
EXP2_SCALE = SCALE * math.log2(math.e)
NEG = -1e30

SMEM = pl.BlockSpec(memory_space=pltpu.SMEM)
VMEM = pl.BlockSpec(memory_space=pltpu.VMEM)
NT = (((1,), (1,)), ((), ()))
F32 = jnp.float32
BF16 = jnp.bfloat16


def params(mib):
    return pltpu.CompilerParams(vmem_limit_bytes=mib << 20)


def shifted(value, axis, steps):
    count = lax.axis_size(axis)
    leading, last = (max(0, -steps), min(count, count - steps))
    return lax.ppermute(value, axis, [(source, source + steps) for source in range(leading, last)])


def both_ways(upward, downward, axis, pairs):
    back = [(target, source) for source, target in pairs]
    return lax.ppermute(upward, axis, pairs), lax.ppermute(downward, axis, back)


def ring_gather(value, axis, pairs, count):
    half = value.shape[0] // 2
    from_below, from_above = value, value
    pieces = []
    for distance in range(1, count // 2 + 1):
        if distance == count // 2:
            from_below, from_above = from_below[:half], from_above[half:]
        from_below, from_above = both_ways(from_below, from_above, axis, pairs)
        pieces += [from_below, from_above]
    return pieces


def place_pieces(out_ref, at, own_ref, pieces, count, size):
    half = size // 2
    out_ref[pl.ds(at * size, size)] = own_ref[...]
    for distance in range(1, count // 2 + 1):
        below = lax.rem(at + (count - distance), count) * size
        above = lax.rem(at + distance, count) * size
        if distance == count // 2:
            out_ref[pl.ds(below, half)] = pieces[2 * distance - 2][...]
            out_ref[pl.ds(below + half, half)] = pieces[2 * distance - 1][...]
        else:
            out_ref[pl.ds(below, size)] = pieces[2 * distance - 2][...]
            out_ref[pl.ds(above, size)] = pieces[2 * distance - 1][...]


def pick_kernel(at_ref, *refs):
    lists, own_ref, pieces = refs[:NX], refs[NX], refs[NX + 1 : -2]
    out_ref, plane_ref = refs[-2:]
    x_at, z_at = lax.div(at_ref[0], NZ), lax.rem(at_ref[0], NZ)
    place_pieces(plane_ref, z_at, own_ref, pieces, NZ, NB)
    for steps, list_ref in enumerate(lists):
        first = lax.rem(x_at + steps, NX) * SLOTS
        for j in range(SLOTS):
            out_ref[first + j] = plane_ref[lax.rem(list_ref[j], PLANE)]


def pick(at, lists, own, pieces):
    return pl.pallas_call(
        pick_kernel,
        out_shape=jax.ShapeDtypeStruct((NX * SLOTS, BLK, 2 * DH), BF16),
        in_specs=[SMEM] * (1 + NX) + [VMEM] * (1 + len(pieces)),
        out_specs=VMEM,
        scratch_shapes=[pltpu.VMEM((PLANE, BLK, 2 * DH), BF16)],
        compiler_params=params(16),
        name="pick_far",
    )(at, *lists, own, *pieces)


def attend_kernel(
    at_ref, far_ref, count_ref, q_ref, g_ref, prev_ref, own_ref, far_kv_ref,
    qg_ref, win_ref, farg_ref, k_ref, v_ref, kt_ref, acc_ref, tri_ref,
):
    win_ref[...] = jnp.zeros_like(win_ref)
    key_at = lax.broadcasted_iota(jnp.int32, (BLK, 2 * BLK), 0)
    query_at = lax.broadcasted_iota(jnp.int32, (BLK, 2 * BLK), 1) % BLK
    tri_ref[...] = jnp.where(key_at <= query_at, 0.0, NEG)

    def block(b, carry):
        index = at_ref[0] * NB + b
        for w in range(WIN):
            local = b + w
            both = jnp.where(local < NB, prev_ref[lax.rem(local, NB)], own_ref[lax.rem(local, NB)])
            k_ref[w * BLK : (w + 1) * BLK, :] = both[:, :DH]
            v_ref[w * BLK : (w + 1) * BLK, :] = both[:, DH:]
        for j in range(FARS):
            slot = b * FARS + j
            owner = lax.div(far_ref[slot], PLANE)
            both = far_kv_ref[owner * SLOTS + slot]
            k_ref[(WIN + j) * BLK : (WIN + j + 1) * BLK, :] = both[:, :DH]
            v_ref[(WIN + j) * BLK : (WIN + j + 1) * BLK, :] = both[:, DH:]
        kt_ref[...] = k_ref[...].astype(F32).T.astype(BF16)
        acc_ref[...] = jnp.zeros_like(acc_ref)
        biases = [
            jnp.where(index >= 2, 0.0, NEG).astype(F32),
            jnp.where(index >= 1, 0.0, NEG).astype(F32),
            None,
        ] + [jnp.where(j < count_ref[b], 0.0, NEG).astype(F32) for j in range(FARS)]
        rows = pl.ds(pl.multiple_of(b * BLK, BLK), BLK)
        for pair in range(GQ // 2):
            lo = pair * 2 * DH
            q2 = jnp.concatenate([q_ref[rows, lo : lo + DH], q_ref[rows, lo + DH : lo + 2 * DH]])
            g2 = jnp.concatenate([g_ref[rows, lo : lo + DH], g_ref[rows, lo + DH : lo + 2 * DH]])
            scores = lax.dot_general(k_ref[...], q2, NT, preferred_element_type=F32)
            parts = []
            for c in range(WIN + FARS):
                part = scores[c * BLK : (c + 1) * BLK, :]
                bias = tri_ref[...] if biases[c] is None else biases[c]
                parts.append(part + bias)
            scores = jnp.concatenate(parts)
            top = jnp.max(scores, axis=0, keepdims=True)
            expo = jnp.exp2((scores - top) * EXP2_SCALE)
            inv = 1.0 / jnp.sum(expo, axis=0, keepdims=True)
            soft = expo * inv
            grad_p = lax.dot_general(v_ref[...], g2, NT, preferred_element_type=F32)
            delta = jnp.sum(soft * grad_p, axis=0, keepdims=True)
            soft_b = soft.astype(BF16)
            grad_s = (soft * (grad_p - delta)).astype(BF16)
            acc_ref[:, :DH] += jnp.dot(grad_s, q2, preferred_element_type=F32)
            acc_ref[:, DH:] += jnp.dot(soft_b, g2, preferred_element_type=F32)
            grad_q = jnp.dot(kt_ref[...], grad_s, preferred_element_type=F32).T * SCALE
            qg_ref[rows, lo : lo + DH] = grad_q[:BLK].astype(BF16)
            qg_ref[rows, lo + DH : lo + 2 * DH] = grad_q[BLK:].astype(BF16)
        acc_ref[:, :DH] = acc_ref[:, :DH] * SCALE
        window = pl.ds(pl.multiple_of(b * BLK, BLK), WIN * BLK)
        win_ref[window, :] += acc_ref[: WIN * BLK, :]
        for j in range(FARS):
            farg_ref[b * FARS + j] = acc_ref[(WIN + j) * BLK : (WIN + j + 1) * BLK, :].astype(BF16)
        return carry

    lax.fori_loop(0, NB, block, 0)


def attend(at, far, count, queries, out_grad, prev, own, far_kv):
    keys = (WIN + FARS) * BLK
    return pl.pallas_call(
        attend_kernel,
        out_shape=(
            jax.ShapeDtypeStruct((NB * BLK, GQ * DH), BF16),
            jax.ShapeDtypeStruct((2 * NB * BLK, 2 * DH), F32),
            jax.ShapeDtypeStruct((SLOTS, BLK, 2 * DH), BF16),
        ),
        in_specs=[SMEM, SMEM, SMEM] + [VMEM] * 5,
        out_specs=(VMEM, VMEM, VMEM),
        scratch_shapes=[
            pltpu.VMEM((keys, DH), BF16),
            pltpu.VMEM((keys, DH), BF16),
            pltpu.VMEM((DH, keys), BF16),
            pltpu.VMEM((keys, 2 * DH), F32),
            pltpu.VMEM((BLK, 2 * BLK), F32),
        ],
        compiler_params=params(24),
        cost_estimate=pl.CostEstimate(flops=2_400_000_000 * 4, bytes_accessed=6 << 20, transcendentals=2_000_000),
        name="attend",
    )(at, far, count, queries, out_grad, prev, own, far_kv)


def spread_kernel(at_ref, *refs):
    lists, pieces = refs[:NX], refs[NX:-2]
    out_ref, acc_ref = refs[-2:]
    mine, below, above, across_low, across_high = pieces
    x_at = lax.div(at_ref[0], NZ)
    acc_ref[...] = jnp.zeros_like(acc_ref)

    def add(listed, term_ref, j):
        @pl.when(lax.div(listed, PLANE) == x_at)
        def _():
            acc_ref[lax.rem(listed, PLANE)] += term_ref[j].astype(F32)

    half = SLOTS // 2
    for j in range(SLOTS):
        add(lists[0][j], mine, j)
        add(lists[1][j], above, j)
        add(lists[2][j], across_low if j < half else across_high, j % half)
        add(lists[3][j], below, j)
    out_ref[...] = acc_ref[...].astype(BF16)


def spread(at, lists, own, pieces):
    return pl.pallas_call(
        spread_kernel,
        out_shape=jax.ShapeDtypeStruct((PLANE, BLK, 2 * DH), BF16),
        in_specs=[SMEM] * (1 + NX) + [VMEM] * (1 + len(pieces)),
        out_specs=VMEM,
        scratch_shapes=[pltpu.VMEM((PLANE, BLK, 2 * DH), F32)],
        compiler_params=params(16),
        name="spread_far",
    )(at, *lists, own, *pieces)


def heads_kernel(at_ref, *refs):
    own_ref, *pieces, other_ref, stack_ref, wide_ref = refs
    at, core = lax.div(at_ref[0], 2), lax.rem(at_ref[0], 2)
    half = BLK * NB // 2

    def put(y, which, rows, value):
        head = 2 * y + which
        stack_ref[head, rows, :] = value
        wide_ref[rows, pl.ds(pl.multiple_of(head * 2 * DH, 2 * DH), 2 * DH)] = value

    everything = slice(0, 2 * half)
    below, above = lax.rem(at + NY - 1, NY), lax.rem(at + 1, NY)
    across = lax.rem(at + 2, NY)
    for which, mine in ((core, True), (1 - core, False)):
        parts = (
            (own_ref, *pieces)
            if mine
            else (
                other_ref.at[: 2 * half],
                other_ref.at[2 * half : 4 * half],
                other_ref.at[4 * half : 6 * half],
                other_ref.at[6 * half : 7 * half],
                other_ref.at[7 * half :],
            )
        )
        put(at, which, everything, parts[0][...])
        put(below, which, everything, parts[1][...])
        put(above, which, everything, parts[2][...])
        put(across, which, slice(0, half), parts[3][...])
        put(across, which, slice(half, 2 * half), parts[4][...])


def place_heads(at, own, pieces, other):
    tokens = own.shape[0]
    return pl.pallas_call(
        heads_kernel,
        out_shape=(
            jax.ShapeDtypeStruct((2 * NY, tokens, 2 * DH), BF16),
            jax.ShapeDtypeStruct((tokens, 2 * NY * 2 * DH), BF16),
        ),
        in_specs=[SMEM] + [VMEM] * (2 + len(pieces)),
        out_specs=(VMEM, VMEM),
        compiler_params=params(16),
        name="place_heads",
    )(at, own, *pieces, other)


def weights_kernel(grad_ref, inputs_ref, out_ref):
    columns = DH // 4
    for head in range(2):
        grad = jnp.concatenate([grad_ref[x * 2 + head] for x in range(NX)])
        term = lax.dot_general(
            grad, inputs_ref[...], (((0,), (0,)), ((), ())), preferred_element_type=F32
        ).astype(BF16)
        for part in range(4):
            for kind in range(2):
                lower = kind * DH + part * columns
                out_ref[head * 4 + part, kind * columns : (kind + 1) * columns, :] = term[
                    lower : lower + columns
                ]


def weight_terms(grad, inputs_x):
    return pl.pallas_call(
        weights_kernel,
        out_shape=jax.ShapeDtypeStruct((NZ, 2 * DH // 4, inputs_x.shape[1]), BF16),
        in_specs=[VMEM, VMEM],
        out_specs=VMEM,
        compiler_params=params(24),
        cost_estimate=pl.CostEstimate(flops=1 << 30, bytes_accessed=4 << 20, transcendentals=0),
        name="weight_terms",
    )(grad, inputs_x)


def local(
    queries, key_rows, value_rows, out_grad, inputs, key_weight, value_weight, far_blocks, far_count
):
    tokens = queries.shape[0]
    seq_index = lax.axis_index("seq").astype(jnp.int32)
    at = seq_index.reshape(1)
    own_index = lax.axis_index("own").astype(jnp.int32).reshape(1)
    own_kv = jnp.concatenate([key_rows, value_rows], axis=1).reshape(NB, BLK, 2 * DH)

    columns = DH // 4
    weights = jnp.concatenate([key_weight.T, value_weight.T])
    weights = lax.all_gather(weights, "seq", axis=0, tiled=True)
    weights, inputs = lax.optimization_barrier((weights, inputs))
    inputs_x = lax.all_gather(inputs, "seq", axis=0, axis_index_groups=X_GROUPS, tiled=True)
    weights = weights.reshape(2 * NY, 4, 2, columns, -1).transpose(0, 2, 1, 3, 4)
    weights = weights.reshape(2 * NY * 2 * DH, -1)

    listed = far_blocks.reshape(SLOTS)
    below, above = both_ways(listed, listed, "seq", X_UP)
    lists = (listed, above, lax.ppermute(listed, "seq", X_ACROSS), below)
    plane = ring_gather(own_kv, "seq", Z_UP, NZ)
    prev_kv = shifted(own_kv, "seq", 1)
    chosen = pick(at, lists, own_kv, plane)
    far_kv = lax.all_to_all(chosen, "seq", 0, 0, axis_index_groups=X_GROUPS, tiled=True)

    query_grad, window, far_grad = attend(
        at, listed, far_count, queries, out_grad, prev_kv, own_kv, far_kv
    )
    far_all = ring_gather(far_grad, "seq", X_UP, NX)
    back = shifted(window[:tokens].astype(BF16), "seq", -1)
    dense = spread(at, lists, far_grad, far_all)
    dense = dense.reshape(NZ, tokens, 2 * DH)
    terms = lax.all_to_all(dense, "seq", 0, 0, axis_index_groups=Z_GROUPS, tiled=True)
    kv_grad = jnp.sum(terms.astype(F32), axis=0) + back.astype(F32) + window[tokens:]
    kv_grad = kv_grad.astype(BF16)

    same_core = ring_gather(kv_grad, "own", Y_UP, NY)
    other_core = lax.ppermute(jnp.concatenate([kv_grad, *same_core]), "own", CORES)
    stacked, wide = place_heads(own_index, kv_grad, same_core, other_core)
    stacked, weights, inputs_x = lax.optimization_barrier((stacked, weights, inputs_x))
    quarter = lax.all_to_all(stacked, "seq", 0, 0, axis_index_groups=X_GROUPS, tiled=True)
    pieces = weight_terms(quarter, inputs_x)
    pieces = lax.all_to_all(pieces, "seq", 0, 0, axis_index_groups=Z_GROUPS, tiled=True)
    input_grad = jnp.dot(wide, weights, preferred_element_type=F32)
    weight_grad = jnp.sum(pieces.astype(F32), axis=0)
    return (
        query_grad,
        input_grad.astype(BF16),
        weight_grad[:columns].T,
        weight_grad[columns:].T,
    )


def solution(mesh):
    return jax.shard_map(
        local,
        mesh=mesh,
        in_specs=(
            P("seq", "own"),
            P("seq", "own"),
            P("seq", "own"),
            P("seq", "own"),
            P("seq", "own"),
            P("own", "seq"),
            P("own", "seq"),
            P("seq", None),
            P("seq"),
        ),
        out_specs=(P("seq", "own"), P("seq", "own"), P("own", "seq"), P("own", "seq")),
        check_vma=False,
    )
```

```python
import functools
import math

import jax
import jax.numpy as jnp
from jax import lax
from jax.experimental import pallas as pl
from jax.experimental.pallas import tpu as pltpu
from jax.sharding import PartitionSpec as P

DH = 128
GQ = 8
BLK = 128
WIN = 3
FARS = 4
NX = 4
NZ = 8
NB = 2
PLANE = NB * NZ
SLOTS = NB * FARS
X_GROUPS = [[x * NZ + z for x in range(NX)] for z in range(NZ)]
Z_GROUPS = [[x * NZ + z for z in range(NZ)] for x in range(NX)]
Z_UP = [(x * NZ + z, x * NZ + (z + 1) % NZ) for x in range(NX) for z in range(NZ)]
X_UP = [(x * NZ + z, (x + 1) % NX * NZ + z) for x in range(NX) for z in range(NZ)]
X_ACROSS = [(x * NZ + z, (x + 2) % NX * NZ + z) for x in range(NX) for z in range(NZ)]
NY = 4
Y_UP = [(2 * y + core, 2 * ((y + 1) % NY) + core) for y in range(NY) for core in range(2)]
CORES = [(own, own ^ 1) for own in range(2 * NY)]
SWAP_XY = [
    (((x * NZ + z) * NY + y) * 2 + core, ((y * NZ + z) * NY + x) * 2 + core)
    for x in range(NX)
    for z in range(NZ)
    for y in range(NY)
    for core in range(2)
]
PART = DH // 4
SCALE = 1.0 / math.sqrt(DH)
EXP2_SCALE = SCALE * math.log2(math.e)
NEG = -1e30

SMEM = pl.BlockSpec(memory_space=pltpu.SMEM)
VMEM = pl.BlockSpec(memory_space=pltpu.VMEM)
NT = (((1,), (1,)), ((), ()))
F32 = jnp.float32
BF16 = jnp.bfloat16


def params(mib):
    return pltpu.CompilerParams(vmem_limit_bytes=mib << 20)


def shifted(value, axis, steps):
    count = lax.axis_size(axis)
    leading, last = (max(0, -steps), min(count, count - steps))
    return lax.ppermute(value, axis, [(source, source + steps) for source in range(leading, last)])


def both_ways(upward, downward, axis, pairs):
    back = [(target, source) for source, target in pairs]
    return lax.ppermute(upward, axis, pairs), lax.ppermute(downward, axis, back)


def ring_gather(value, axis, pairs, count):
    half = value.shape[0] // 2
    from_below, from_above = value, value
    pieces = []
    for distance in range(1, count // 2 + 1):
        if distance == count // 2:
            from_below, from_above = from_below[:half], from_above[half:]
        from_below, from_above = both_ways(from_below, from_above, axis, pairs)
        pieces += [from_below, from_above]
    return pieces


def place_pieces(out_ref, at, own_ref, pieces, count, size):
    half = size // 2
    out_ref[pl.ds(at * size, size)] = own_ref[...]
    for distance in range(1, count // 2 + 1):
        below = lax.rem(at + (count - distance), count) * size
        above = lax.rem(at + distance, count) * size
        if distance == count // 2:
            out_ref[pl.ds(below, half)] = pieces[2 * distance - 2][...]
            out_ref[pl.ds(below + half, half)] = pieces[2 * distance - 1][...]
        else:
            out_ref[pl.ds(below, size)] = pieces[2 * distance - 2][...]
            out_ref[pl.ds(above, size)] = pieces[2 * distance - 1][...]


def pick_kernel(at_ref, *refs):
    lists, own_ref, pieces = refs[:NX], refs[NX], refs[NX + 1 : -2]
    out_ref, plane_ref = refs[-2:]
    x_at, z_at = lax.div(at_ref[0], NZ), lax.rem(at_ref[0], NZ)
    place_pieces(plane_ref, z_at, own_ref, pieces, NZ, NB)
    for steps, list_ref in enumerate(lists):
        first = lax.rem(x_at + steps, NX) * SLOTS
        for j in range(SLOTS):
            out_ref[first + j] = plane_ref[lax.rem(list_ref[j], PLANE)]


def pick(at, lists, own, pieces):
    return pl.pallas_call(
        pick_kernel,
        out_shape=jax.ShapeDtypeStruct((NX * SLOTS, BLK, 2 * DH), BF16),
        in_specs=[SMEM] * (1 + NX) + [VMEM] * (1 + len(pieces)),
        out_specs=VMEM,
        scratch_shapes=[pltpu.VMEM((PLANE, BLK, 2 * DH), BF16)],
        compiler_params=params(16),
        name="pick_far",
    )(at, *lists, own, *pieces)


def attend_kernel(
    at_ref, far_ref, count_ref, q_ref, g_ref, prev_ref, own_ref, far_kv_ref,
    qg_ref, win_ref, farg_ref, k_ref, v_ref, kt_ref, acc_ref, tri_ref,
):
    win_ref[...] = jnp.zeros_like(win_ref)
    key_at = lax.broadcasted_iota(jnp.int32, (BLK, 2 * BLK), 0)
    query_at = lax.broadcasted_iota(jnp.int32, (BLK, 2 * BLK), 1) % BLK
    tri_ref[...] = jnp.where(key_at <= query_at, 0.0, NEG)

    def block(b, carry):
        index = at_ref[0] * NB + b
        for w in range(WIN):
            local = b + w
            both = jnp.where(local < NB, prev_ref[lax.rem(local, NB)], own_ref[lax.rem(local, NB)])
            k_ref[w * BLK : (w + 1) * BLK, :] = both[:, :DH]
            v_ref[w * BLK : (w + 1) * BLK, :] = both[:, DH:]
        for j in range(FARS):
            slot = b * FARS + j
            owner = lax.div(far_ref[slot], PLANE)
            both = far_kv_ref[owner * SLOTS + slot]
            k_ref[(WIN + j) * BLK : (WIN + j + 1) * BLK, :] = both[:, :DH]
            v_ref[(WIN + j) * BLK : (WIN + j + 1) * BLK, :] = both[:, DH:]
        kt_ref[...] = k_ref[...].astype(F32).T.astype(BF16)
        acc_ref[...] = jnp.zeros_like(acc_ref)
        biases = [
            jnp.where(index >= 2, 0.0, NEG).astype(F32),
            jnp.where(index >= 1, 0.0, NEG).astype(F32),
            None,
        ] + [jnp.where(j < count_ref[b], 0.0, NEG).astype(F32) for j in range(FARS)]
        rows = pl.ds(pl.multiple_of(b * BLK, BLK), BLK)
        for pair in range(GQ // 2):
            lo = pair * 2 * DH
            q2 = jnp.concatenate([q_ref[rows, lo : lo + DH], q_ref[rows, lo + DH : lo + 2 * DH]])
            g2 = jnp.concatenate([g_ref[rows, lo : lo + DH], g_ref[rows, lo + DH : lo + 2 * DH]])
            scores = lax.dot_general(k_ref[...], q2, NT, preferred_element_type=F32)
            parts = []
            for c in range(WIN + FARS):
                part = scores[c * BLK : (c + 1) * BLK, :]
                bias = tri_ref[...] if biases[c] is None else biases[c]
                parts.append(part + bias)
            scores = jnp.concatenate(parts)
            top = jnp.max(scores, axis=0, keepdims=True)
            expo = jnp.exp2((scores - top) * EXP2_SCALE)
            inv = 1.0 / jnp.sum(expo, axis=0, keepdims=True)
            soft = expo * inv
            grad_p = lax.dot_general(v_ref[...], g2, NT, preferred_element_type=F32)
            delta = jnp.sum(soft * grad_p, axis=0, keepdims=True)
            soft_b = soft.astype(BF16)
            grad_s = (soft * (grad_p - delta)).astype(BF16)
            acc_ref[:, :DH] += jnp.dot(grad_s, q2, preferred_element_type=F32)
            acc_ref[:, DH:] += jnp.dot(soft_b, g2, preferred_element_type=F32)
            grad_q = jnp.dot(kt_ref[...], grad_s, preferred_element_type=F32).T * SCALE
            qg_ref[rows, lo : lo + DH] = grad_q[:BLK].astype(BF16)
            qg_ref[rows, lo + DH : lo + 2 * DH] = grad_q[BLK:].astype(BF16)
        acc_ref[:, :DH] = acc_ref[:, :DH] * SCALE
        window = pl.ds(pl.multiple_of(b * BLK, BLK), WIN * BLK)
        win_ref[window, :] += acc_ref[: WIN * BLK, :]
        for j in range(FARS):
            farg_ref[b * FARS + j] = acc_ref[(WIN + j) * BLK : (WIN + j + 1) * BLK, :].astype(BF16)
        return carry

    lax.fori_loop(0, NB, block, 0)


def attend(at, far, count, queries, out_grad, prev, own, far_kv):
    keys = (WIN + FARS) * BLK
    return pl.pallas_call(
        attend_kernel,
        out_shape=(
            jax.ShapeDtypeStruct((NB * BLK, GQ * DH), BF16),
            jax.ShapeDtypeStruct((2 * NB * BLK, 2 * DH), F32),
            jax.ShapeDtypeStruct((SLOTS, BLK, 2 * DH), BF16),
        ),
        in_specs=[SMEM, SMEM, SMEM] + [VMEM] * 5,
        out_specs=(VMEM, VMEM, VMEM),
        scratch_shapes=[
            pltpu.VMEM((keys, DH), BF16),
            pltpu.VMEM((keys, DH), BF16),
            pltpu.VMEM((DH, keys), BF16),
            pltpu.VMEM((keys, 2 * DH), F32),
            pltpu.VMEM((BLK, 2 * BLK), F32),
        ],
        compiler_params=params(24),
        cost_estimate=pl.CostEstimate(flops=2_400_000_000 * 4, bytes_accessed=6 << 20, transcendentals=2_000_000),
        name="attend",
    )(at, far, count, queries, out_grad, prev, own, far_kv)


def spread_kernel(at_ref, *refs):
    lists, pieces = refs[:NX], refs[NX:-2]
    out_ref, acc_ref = refs[-2:]
    mine, below, above, across_low, across_high = pieces
    x_at = lax.div(at_ref[0], NZ)
    acc_ref[...] = jnp.zeros_like(acc_ref)

    def add(listed, term_ref, j):
        @pl.when(lax.div(listed, PLANE) == x_at)
        def _():
            acc_ref[lax.rem(listed, PLANE)] += term_ref[j].astype(F32)

    half = SLOTS // 2
    for j in range(SLOTS):
        add(lists[0][j], mine, j)
        add(lists[1][j], above, j)
        add(lists[2][j], across_low if j < half else across_high, j % half)
        add(lists[3][j], below, j)
    out_ref[...] = acc_ref[...].astype(BF16)


def spread(at, lists, own, pieces):
    return pl.pallas_call(
        spread_kernel,
        out_shape=jax.ShapeDtypeStruct((PLANE, BLK, 2 * DH), BF16),
        in_specs=[SMEM] * (1 + NX) + [VMEM] * (1 + len(pieces)),
        out_specs=VMEM,
        scratch_shapes=[pltpu.VMEM((PLANE, BLK, 2 * DH), F32)],
        compiler_params=params(16),
        name="spread_far",
    )(at, *lists, own, *pieces)


def finish_kernel(terms_ref, back_ref, window_ref, out_ref):
    total = window_ref[NB * BLK :, :] + back_ref[...].astype(F32)
    for z in range(NZ):
        total += terms_ref[z].astype(F32)
    source = lax.broadcasted_iota(jnp.int32, (2 * DH, 2 * DH), 0)
    target = lax.broadcasted_iota(jnp.int32, (2 * DH, 2 * DH), 1)
    part, rest = target // (2 * PART), target % (2 * PART)
    wanted = (rest // PART) * DH + part * PART + rest % PART
    order = jnp.where(source == wanted, 1.0, 0.0).astype(BF16)
    out_ref[...] = jnp.dot(
        total.astype(BF16), order, preferred_element_type=F32
    ).astype(BF16)


def finish(terms, back, window):
    return pl.pallas_call(
        finish_kernel,
        out_shape=jax.ShapeDtypeStruct((NB * BLK, 2 * DH), BF16),
        in_specs=[VMEM] * 3,
        out_specs=VMEM,
        compiler_params=params(12),
        name="finish_kv",
    )(terms, back, window)


def heads_kernel(at_ref, own_ref, *refs):
    *pieces, other_ref, out_ref = refs
    at, core = lax.div(at_ref[0], 2), lax.rem(at_ref[0], 2)
    rows = NB * BLK
    half = rows // 2
    below, above = lax.rem(at + NY - 1, NY), lax.rem(at + 1, NY)
    across = lax.rem(at + 2, NY)
    starts = (0, rows, 2 * rows, 3 * rows, 3 * rows + half)
    for k, (y, low, high) in enumerate(
        ((at, 0, rows), (below, 0, rows), (above, 0, rows), (across, 0, half), (across, half, rows))
    ):
        mine = own_ref if k == 0 else pieces[k - 1]
        out_ref[2 * y + core, low:high, :] = mine[...]
        out_ref[2 * y + 1 - core, low:high, :] = other_ref[starts[k] : starts[k] + high - low, :]


def place_heads(at, own, pieces, other):
    return pl.pallas_call(
        heads_kernel,
        out_shape=jax.ShapeDtypeStruct((2 * NY, *own.shape), BF16),
        in_specs=[SMEM] + [VMEM] * (2 + len(pieces)),
        out_specs=VMEM,
        compiler_params=params(8),
        name="place_heads",
    )(at, own, *pieces, other)


def weights_kernel(grad_ref, inputs_ref, out_ref):
    quarters, wide = 4, inputs_ref.shape[1] // 4
    for head in range(2):
        grad = jnp.concatenate([grad_ref[x * 2 + head] for x in range(NX)])
        term = lax.dot_general(
            grad, inputs_ref[...], (((0,), (0,)), ((), ())), preferred_element_type=F32
        ).astype(BF16)
        for part in range(4):
            for quarter in range(quarters):
                out_ref[
                    head * 4 + part, quarter * 2 * PART : (quarter + 1) * 2 * PART, :
                ] = term[
                    part * 2 * PART : (part + 1) * 2 * PART, quarter * wide : (quarter + 1) * wide
                ]


def weight_terms(grad, inputs_x):
    return pl.pallas_call(
        weights_kernel,
        out_shape=jax.ShapeDtypeStruct((NZ, 4 * 2 * PART, inputs_x.shape[1] // 4), BF16),
        in_specs=[VMEM, VMEM],
        out_specs=VMEM,
        compiler_params=params(16),
        cost_estimate=pl.CostEstimate(flops=1 << 30, bytes_accessed=4 << 20, transcendentals=0),
        name="weight_terms",
    )(grad, inputs_x)


def weight_sum_kernel(terms_ref, key_ref, value_ref):
    total = terms_ref[0].astype(F32)
    for z in range(1, NZ):
        total += terms_ref[z].astype(F32)
    wide = total.shape[1]
    for quarter in range(4):
        low = quarter * 2 * PART
        key_ref[:, quarter * wide : (quarter + 1) * wide] = total[low : low + PART]
        value_ref[:, quarter * wide : (quarter + 1) * wide] = total[low + PART : low + 2 * PART]


def weight_sum(terms):
    out = jax.ShapeDtypeStruct((PART, 4 * terms.shape[2]), F32)
    return pl.pallas_call(
        weight_sum_kernel,
        out_shape=(out, out),
        in_specs=[VMEM],
        out_specs=(VMEM, VMEM),
        compiler_params=params(8),
        name="weight_sum",
    )(terms)


def input_kernel(at_ref, grad_ref, weights_ref, mine_ref, above_ref, across_ref, below_ref):
    x_at = lax.div(at_ref[0], NZ)
    for steps, out_ref in enumerate((mine_ref, above_ref, across_ref, below_ref)):
        x = lax.rem(x_at + steps, NX)
        grad = jnp.concatenate([grad_ref[2 * x], grad_ref[2 * x + 1]], axis=1)
        out_ref[...] = jnp.dot(grad, weights_ref[...], preferred_element_type=F32).astype(
            out_ref.dtype
        )


def input_terms(at, grad, weights):
    shape = (grad.shape[1], weights.shape[1])
    send = jax.ShapeDtypeStruct(shape, BF16)
    return pl.pallas_call(
        input_kernel,
        out_shape=(jax.ShapeDtypeStruct(shape, F32), send, send, send),
        in_specs=[SMEM, VMEM, VMEM],
        out_specs=(VMEM,) * 4,
        compiler_params=params(16),
        cost_estimate=pl.CostEstimate(flops=1 << 30, bytes_accessed=4 << 20, transcendentals=0),
        name="input_terms",
    )(at, grad, weights)


def added(term, arrived, low):
    high = low + arrived.shape[0]
    rows = (term[low:high].astype(F32) + arrived.astype(F32)).astype(BF16)
    return jnp.concatenate([term[:low], rows, term[high:]])


def local(
    queries, key_rows, value_rows, out_grad, inputs, key_weight, value_weight, far_blocks, far_count
):
    tokens = queries.shape[0]
    seq_index = lax.axis_index("seq").astype(jnp.int32)
    at = seq_index.reshape(1)
    own_index = lax.axis_index("own").astype(jnp.int32).reshape(1)
    own_kv = jnp.concatenate([key_rows, value_rows], axis=1).reshape(NB, BLK, 2 * DH)

    inputs_x = lax.all_gather(inputs, "seq", axis=0, axis_index_groups=X_GROUPS, tiled=True)

    listed = far_blocks.reshape(SLOTS)
    list_below, list_above = both_ways(listed, listed, "seq", X_UP)
    list_across = lax.ppermute(listed, "seq", X_ACROSS)
    from_below, from_above = both_ways(own_kv, own_kv, "seq", Z_UP)
    list_below, list_above, list_across, from_below, from_above, key_weight, value_weight = (
        lax.optimization_barrier(
            (list_below, list_above, list_across, from_below, from_above, key_weight, value_weight)
        )
    )
    lists = (listed, list_above, list_across, list_below)
    weights = jnp.concatenate([key_weight.T, value_weight.T])
    weights = lax.all_gather(weights, "seq", axis=0, axis_index_groups=Z_GROUPS, tiled=True)
    plane = [from_below, from_above]
    for distance in range(2, NZ // 2 + 1):
        if distance == NZ // 2:
            from_below, from_above = from_below[: NB // 2], from_above[NB // 2 :]
        from_below, from_above = both_ways(from_below, from_above, "seq", Z_UP)
        plane += [from_below, from_above]
    prev_kv = shifted(own_kv, "seq", 1)
    chosen = pick(at, lists, own_kv, plane)
    far_kv = lax.all_to_all(chosen, "seq", 0, 0, axis_index_groups=X_GROUPS, tiled=True)

    far_kv, inputs_x = lax.optimization_barrier((far_kv, inputs_x))
    query_grad, window, far_grad = attend(
        at, listed, far_count, queries, out_grad, prev_kv, own_kv, far_kv
    )
    far_all = ring_gather(far_grad, "seq", X_UP, NX)
    back = shifted(window[:tokens].astype(BF16), "seq", -1)
    dense = spread(at, lists, far_grad, far_all)
    dense, weights = lax.optimization_barrier((dense, weights))
    dense = dense.reshape(NZ, tokens, 2 * DH)
    terms = lax.all_to_all(dense, "seq", 0, 0, axis_index_groups=Z_GROUPS, tiled=True)
    kv_grad = finish(terms, back, window)

    moved = lax.ppermute(kv_grad, ("seq", "own"), SWAP_XY)
    same_core = ring_gather(moved, "own", Y_UP, NY)
    other_core = lax.ppermute(jnp.concatenate([moved, *same_core]), "own", CORES)
    heads = place_heads(own_index, moved, same_core, other_core)

    pieces = weight_terms(heads, inputs_x)
    pieces = lax.all_to_all(pieces, "seq", 0, 0, axis_index_groups=Z_GROUPS, tiled=True)
    mine, above, across, below = input_terms(at, heads, weights)
    half = tokens // 2
    from_below, from_above = both_ways(across[:half], across[half:], "seq", X_UP)
    above, below = added(above, from_below, 0), added(below, from_above, half)
    from_below, from_above = both_ways(above, below, "seq", X_UP)
    input_grad = mine + from_below.astype(F32) + from_above.astype(F32)
    key_weight_grad, value_weight_grad = weight_sum(pieces)
    return (query_grad, input_grad.astype(BF16), key_weight_grad.T, value_weight_grad.T)


def solution(mesh):
    return jax.shard_map(
        local,
        mesh=mesh,
        in_specs=(
            P("seq", "own"),
            P("seq", "own"),
            P("seq", "own"),
            P("seq", "own"),
            P("seq", "own"),
            P("own", "seq"),
            P("own", "seq"),
            P("seq", None),
            P("seq"),
        ),
        out_specs=(P("seq", "own"), P("seq", "own"), P("own", "seq"), P("own", "seq")),
        check_vma=False,
    )
```

```python
import functools
import math

import jax
import jax.numpy as jnp
from jax import lax
from jax.experimental import pallas as pl
from jax.experimental.pallas import tpu as pltpu
from jax.sharding import PartitionSpec as P

DH = 128
GQ = 8
BLK = 128
WIN = 3
FARS = 4
NX = 4
NZ = 8
NB = 2
PLANE = NB * NZ
SLOTS = NB * FARS
X_GROUPS = [[x * NZ + z for x in range(NX)] for z in range(NZ)]
Z_GROUPS = [[x * NZ + z for z in range(NZ)] for x in range(NX)]
Z_UP = [(x * NZ + z, x * NZ + (z + 1) % NZ) for x in range(NX) for z in range(NZ)]
X_UP = [(x * NZ + z, (x + 1) % NX * NZ + z) for x in range(NX) for z in range(NZ)]
X_ACROSS = [(x * NZ + z, (x + 2) % NX * NZ + z) for x in range(NX) for z in range(NZ)]
NY = 4
CORES = [(own, own ^ 1) for own in range(2 * NY)]
SWAP_XY = [
    [
        (((x * NZ + z) * NY + y) * 2 + core, ((y * NZ + z) * NY + (x + step) % NY) * 2 + core)
        for x in range(NX)
        for z in range(NZ)
        for y in range(NY)
        for core in range(2)
    ]
    for step in range(NY)
]
PART = DH // 4
SCALE = 1.0 / math.sqrt(DH)
EXP2_SCALE = SCALE * math.log2(math.e)
NEG = -1e30

SMEM = pl.BlockSpec(memory_space=pltpu.SMEM)
VMEM = pl.BlockSpec(memory_space=pltpu.VMEM)
NT = (((1,), (1,)), ((), ()))
F32 = jnp.float32
BF16 = jnp.bfloat16


def params(mib):
    return pltpu.CompilerParams(vmem_limit_bytes=mib << 20)


def shifted(value, axis, steps):
    count = lax.axis_size(axis)
    leading, last = (max(0, -steps), min(count, count - steps))
    return lax.ppermute(value, axis, [(source, source + steps) for source in range(leading, last)])


def both_ways(upward, downward, axis, pairs):
    back = [(target, source) for source, target in pairs]
    return lax.ppermute(upward, axis, pairs), lax.ppermute(downward, axis, back)


def ring_gather(value, axis, pairs, count):
    half = value.shape[0] // 2
    from_below, from_above = value, value
    pieces = []
    for distance in range(1, count // 2 + 1):
        if distance == count // 2:
            from_below, from_above = from_below[:half], from_above[half:]
        from_below, from_above = both_ways(from_below, from_above, axis, pairs)
        pieces += [from_below, from_above]
    return pieces


def pick_kernel(at_ref, *refs):
    *lists, plane_ref, out_ref = refs
    x_at = lax.div(at_ref[0], NZ)
    for steps, list_ref in enumerate(lists):
        first = lax.rem(x_at + steps, NX) * SLOTS
        for j in range(SLOTS):
            listed = list_ref[j // FARS, j % FARS]
            out_ref[first + j] = plane_ref[lax.rem(listed, PLANE)]


def pick(at, lists, plane):
    return pl.pallas_call(
        pick_kernel,
        out_shape=jax.ShapeDtypeStruct((NX * SLOTS, BLK, 2 * DH), BF16),
        in_specs=[SMEM] * (1 + NX) + [VMEM],
        out_specs=VMEM,
        compiler_params=params(8),
        name="pick_far",
    )(at, *lists, plane)


def attend_kernel(
    at_ref, far_ref, count_ref, q_ref, g_ref, prev_ref, own_ref, far_kv_ref,
    qg_ref, win_ref, farg_ref, k_ref, v_ref, kt_ref, acc_ref, tri_ref,
):
    win_ref[...] = jnp.zeros_like(win_ref)
    key_at = lax.broadcasted_iota(jnp.int32, (BLK, 2 * BLK), 0)
    query_at = lax.broadcasted_iota(jnp.int32, (BLK, 2 * BLK), 1) % BLK
    tri_ref[...] = jnp.where(key_at <= query_at, 0.0, NEG)

    def block(b, carry):
        index = at_ref[0] * NB + b
        for w in range(WIN):
            local = b + w
            both = jnp.where(local < NB, prev_ref[lax.rem(local, NB)], own_ref[lax.rem(local, NB)])
            k_ref[w * BLK : (w + 1) * BLK, :] = both[:, :DH]
            v_ref[w * BLK : (w + 1) * BLK, :] = both[:, DH:]
        for j in range(FARS):
            slot = b * FARS + j
            owner = lax.div(far_ref[b, j], PLANE)
            both = far_kv_ref[owner * SLOTS + slot]
            k_ref[(WIN + j) * BLK : (WIN + j + 1) * BLK, :] = both[:, :DH]
            v_ref[(WIN + j) * BLK : (WIN + j + 1) * BLK, :] = both[:, DH:]
        kt_ref[...] = k_ref[...].astype(F32).T.astype(BF16)
        acc_ref[...] = jnp.zeros_like(acc_ref)
        biases = [
            jnp.where(index >= 2, 0.0, NEG).astype(F32),
            jnp.where(index >= 1, 0.0, NEG).astype(F32),
            None,
        ] + [jnp.where(j < count_ref[b], 0.0, NEG).astype(F32) for j in range(FARS)]
        rows = pl.ds(pl.multiple_of(b * BLK, BLK), BLK)
        for pair in range(GQ // 2):
            lo = pair * 2 * DH
            q2 = jnp.concatenate([q_ref[rows, lo : lo + DH], q_ref[rows, lo + DH : lo + 2 * DH]])
            g2 = jnp.concatenate([g_ref[rows, lo : lo + DH], g_ref[rows, lo + DH : lo + 2 * DH]])
            scores = lax.dot_general(k_ref[...], q2, NT, preferred_element_type=F32)
            parts = []
            for c in range(WIN + FARS):
                part = scores[c * BLK : (c + 1) * BLK, :]
                bias = tri_ref[...] if biases[c] is None else biases[c]
                parts.append(part + bias)
            scores = jnp.concatenate(parts)
            top = jnp.max(scores, axis=0, keepdims=True)
            expo = jnp.exp2((scores - top) * EXP2_SCALE)
            inv = 1.0 / jnp.sum(expo, axis=0, keepdims=True)
            soft = expo * inv
            grad_p = lax.dot_general(v_ref[...], g2, NT, preferred_element_type=F32)
            delta = jnp.sum(soft * grad_p, axis=0, keepdims=True)
            soft_b = soft.astype(BF16)
            grad_s = (soft * (grad_p - delta)).astype(BF16)
            acc_ref[:, :DH] += jnp.dot(grad_s, q2, preferred_element_type=F32)
            acc_ref[:, DH:] += jnp.dot(soft_b, g2, preferred_element_type=F32)
            grad_q = jnp.dot(kt_ref[...], grad_s, preferred_element_type=F32).T * SCALE
            qg_ref[rows, lo : lo + DH] = grad_q[:BLK].astype(BF16)
            qg_ref[rows, lo + DH : lo + 2 * DH] = grad_q[BLK:].astype(BF16)
        acc_ref[:, :DH] = acc_ref[:, :DH] * SCALE
        window = pl.ds(pl.multiple_of(b * BLK, BLK), WIN * BLK)
        win_ref[window, :] += acc_ref[: WIN * BLK, :]
        for j in range(FARS):
            farg_ref[b * FARS + j] = acc_ref[(WIN + j) * BLK : (WIN + j + 1) * BLK, :].astype(BF16)
        return carry

    lax.fori_loop(0, NB, block, 0)


def attend(at, far, count, queries, out_grad, prev, own, far_kv):
    keys = (WIN + FARS) * BLK
    return pl.pallas_call(
        attend_kernel,
        out_shape=(
            jax.ShapeDtypeStruct((NB * BLK, GQ * DH), BF16),
            jax.ShapeDtypeStruct((2 * NB * BLK, 2 * DH), F32),
            jax.ShapeDtypeStruct((SLOTS, BLK, 2 * DH), BF16),
        ),
        in_specs=[SMEM, SMEM, SMEM] + [VMEM] * 5,
        out_specs=(VMEM, VMEM, VMEM),
        scratch_shapes=[
            pltpu.VMEM((keys, DH), BF16),
            pltpu.VMEM((keys, DH), BF16),
            pltpu.VMEM((DH, keys), BF16),
            pltpu.VMEM((keys, 2 * DH), F32),
            pltpu.VMEM((BLK, 2 * BLK), F32),
        ],
        compiler_params=params(24),
        cost_estimate=pl.CostEstimate(flops=2_400_000_000 * 4, bytes_accessed=6 << 20, transcendentals=2_000_000),
        name="attend",
    )(at, far, count, queries, out_grad, prev, own, far_kv)


def spread_kernel(at_ref, *refs):
    lists, pieces = refs[:NX], refs[NX:-2]
    out_ref, acc_ref = refs[-2:]
    mine, below, above, across_low, across_high = pieces
    x_at = lax.div(at_ref[0], NZ)
    acc_ref[...] = jnp.zeros_like(acc_ref)

    def add(listed, term_ref, j):
        @pl.when(lax.div(listed, PLANE) == x_at)
        def _():
            acc_ref[lax.rem(listed, PLANE)] += term_ref[j].astype(F32)

    half = SLOTS // 2
    for j in range(SLOTS):
        add(lists[0][j // FARS, j % FARS], mine, j)
        add(lists[1][j // FARS, j % FARS], above, j)
        add(lists[2][j // FARS, j % FARS], across_low if j < half else across_high, j % half)
        add(lists[3][j // FARS, j % FARS], below, j)
    out_ref[...] = acc_ref[...].astype(BF16)


def spread(at, lists, own, pieces):
    return pl.pallas_call(
        spread_kernel,
        out_shape=jax.ShapeDtypeStruct((PLANE, BLK, 2 * DH), BF16),
        in_specs=[SMEM] * (1 + NX) + [VMEM] * (1 + len(pieces)),
        out_specs=VMEM,
        scratch_shapes=[pltpu.VMEM((PLANE, BLK, 2 * DH), F32)],
        compiler_params=params(16),
        name="spread_far",
    )(at, *lists, own, *pieces)


def finish_kernel(terms_ref, back_ref, window_ref, out_ref):
    total = window_ref[NB * BLK :, :] + back_ref[...].astype(F32)
    for z in range(NZ):
        total += terms_ref[z].astype(F32)
    source = lax.broadcasted_iota(jnp.int32, (2 * DH, 2 * DH), 0)
    target = lax.broadcasted_iota(jnp.int32, (2 * DH, 2 * DH), 1)
    part, rest = target // (2 * PART), target % (2 * PART)
    wanted = (rest // PART) * DH + part * PART + rest % PART
    order = jnp.where(source == wanted, 1.0, 0.0).astype(BF16)
    out_ref[...] = jnp.dot(
        total.astype(BF16), order, preferred_element_type=F32
    ).astype(BF16)


def finish(terms, back, window):
    return pl.pallas_call(
        finish_kernel,
        out_shape=jax.ShapeDtypeStruct((NB * BLK, 2 * DH), BF16),
        in_specs=[VMEM] * 3,
        out_specs=VMEM,
        compiler_params=params(12),
        name="finish_kv",
    )(terms, back, window)


def heads_kernel(at_ref, *refs):
    pieces, out_ref = refs[:-1], refs[-1]
    y_at, core = lax.div(at_ref[0], 2), lax.rem(at_ref[0], 2)
    for step in range(NY):
        x = lax.rem(y_at + (NY - step), NY)
        out_ref[2 * x + core] = pieces[step][...]
        out_ref[2 * x + 1 - core] = pieces[NY + step][...]


def place_heads(at, pieces):
    return pl.pallas_call(
        heads_kernel,
        out_shape=jax.ShapeDtypeStruct((2 * NY, *pieces[0].shape), BF16),
        in_specs=[SMEM] + [VMEM] * len(pieces),
        out_specs=VMEM,
        compiler_params=params(8),
        name="place_heads",
    )(at, *pieces)


def weights_kernel(grad_ref, inputs_ref, out_ref):
    quarters, wide = 4, inputs_ref.shape[1] // 4
    for head in range(2):
        grad = jnp.concatenate([grad_ref[x * 2 + head] for x in range(NX)])
        term = lax.dot_general(
            grad, inputs_ref[...], (((0,), (0,)), ((), ())), preferred_element_type=F32
        ).astype(BF16)
        for part in range(4):
            for quarter in range(quarters):
                out_ref[
                    head * 4 + part, quarter * 2 * PART : (quarter + 1) * 2 * PART, :
                ] = term[
                    part * 2 * PART : (part + 1) * 2 * PART, quarter * wide : (quarter + 1) * wide
                ]


def weight_terms(grad, inputs_x):
    return pl.pallas_call(
        weights_kernel,
        out_shape=jax.ShapeDtypeStruct((NZ, 4 * 2 * PART, inputs_x.shape[1] // 4), BF16),
        in_specs=[VMEM, VMEM],
        out_specs=VMEM,
        compiler_params=params(16),
        cost_estimate=pl.CostEstimate(flops=1 << 30, bytes_accessed=4 << 20, transcendentals=0),
        name="weight_terms",
    )(grad, inputs_x)


def weight_sum_kernel(terms_ref, key_ref, value_ref):
    total = terms_ref[0].astype(F32)
    for z in range(1, NZ):
        total += terms_ref[z].astype(F32)
    wide = total.shape[1]
    for quarter in range(4):
        low = quarter * 2 * PART
        key_ref[:, quarter * wide : (quarter + 1) * wide] = total[low : low + PART]
        value_ref[:, quarter * wide : (quarter + 1) * wide] = total[low + PART : low + 2 * PART]


def weight_sum(terms):
    out = jax.ShapeDtypeStruct((PART, 4 * terms.shape[2]), F32)
    return pl.pallas_call(
        weight_sum_kernel,
        out_shape=(out, out),
        in_specs=[VMEM],
        out_specs=(VMEM, VMEM),
        compiler_params=params(8),
        name="weight_sum",
    )(terms)


def input_kernel(at_ref, grad_ref, weights_ref, mine_ref, above_ref, across_ref, below_ref):
    x_at = lax.div(at_ref[0], NZ)
    for steps, out_ref in enumerate((mine_ref, above_ref, across_ref, below_ref)):
        x = lax.rem(x_at + steps, NX)
        grad = jnp.concatenate([grad_ref[2 * x], grad_ref[2 * x + 1]], axis=1)
        out_ref[...] = jnp.dot(grad, weights_ref[...], preferred_element_type=F32).astype(
            out_ref.dtype
        )


def input_terms(at, grad, weights):
    shape = (grad.shape[1], weights.shape[1])
    send = jax.ShapeDtypeStruct(shape, BF16)
    return pl.pallas_call(
        input_kernel,
        out_shape=(jax.ShapeDtypeStruct(shape, F32), send, send, send),
        in_specs=[SMEM, VMEM, VMEM],
        out_specs=(VMEM,) * 4,
        compiler_params=params(16),
        cost_estimate=pl.CostEstimate(flops=1 << 30, bytes_accessed=4 << 20, transcendentals=0),
        name="input_terms",
    )(at, grad, weights)


def added(term, arrived, low):
    high = low + arrived.shape[0]
    rows = (term[low:high].astype(F32) + arrived.astype(F32)).astype(BF16)
    return jnp.concatenate([term[:low], rows, term[high:]])


def local(
    queries, key_rows, value_rows, out_grad, inputs, key_weight, value_weight, far_blocks, far_count
):
    tokens = queries.shape[0]
    seq_index = lax.axis_index("seq").astype(jnp.int32)
    at = seq_index.reshape(1)
    own_index = lax.axis_index("own").astype(jnp.int32).reshape(1)
    own_kv = jnp.concatenate([key_rows, value_rows], axis=1).reshape(NB, BLK, 2 * DH)

    inputs_x = lax.all_gather(inputs, "seq", axis=0, axis_index_groups=X_GROUPS, tiled=True)

    own_copies = jnp.broadcast_to(own_kv[None], (NZ, NB, BLK, 2 * DH)).reshape(-1, BLK, 2 * DH)
    plane = lax.all_to_all(own_copies, "seq", 0, 0, axis_index_groups=Z_GROUPS, tiled=True)
    list_below, list_above = both_ways(far_blocks, far_blocks, "seq", X_UP)
    list_across = lax.ppermute(far_blocks, "seq", X_ACROSS)
    prev_kv = shifted(own_kv, "seq", 1)
    lists = (far_blocks, list_above, list_across, list_below)
    plane, key_weight, value_weight = lax.optimization_barrier((plane, key_weight, value_weight))
    weights = jnp.concatenate([key_weight.T, value_weight.T])
    weights = lax.all_gather(weights, "seq", axis=0, axis_index_groups=Z_GROUPS, tiled=True)
    chosen = pick(at, lists, plane)
    far_kv = lax.all_to_all(chosen, "seq", 0, 0, axis_index_groups=X_GROUPS, tiled=True)

    far_kv, inputs_x = lax.optimization_barrier((far_kv, inputs_x))
    query_grad, window, far_grad = attend(
        at, far_blocks, far_count, queries, out_grad, prev_kv, own_kv, far_kv
    )
    far_all = ring_gather(far_grad, "seq", X_UP, NX)
    back = shifted(window[:tokens].astype(BF16), "seq", -1)
    dense = spread(at, lists, far_grad, far_all)
    dense, weights = lax.optimization_barrier((dense, weights))
    dense = dense.reshape(NZ, tokens, 2 * DH)
    terms = lax.all_to_all(dense, "seq", 0, 0, axis_index_groups=Z_GROUPS, tiled=True)
    kv_grad = finish(terms, back, window)

    moved = [lax.ppermute(kv_grad, ("seq", "own"), pairs) for pairs in SWAP_XY]
    heads = place_heads(own_index, moved + [lax.ppermute(piece, "own", CORES) for piece in moved])

    pieces = weight_terms(heads, inputs_x)
    heads, pieces = lax.optimization_barrier((heads, pieces))
    pieces = lax.all_to_all(pieces, "seq", 0, 0, axis_index_groups=Z_GROUPS, tiled=True)
    mine, above, across, below = input_terms(at, heads, weights)
    half = tokens // 2
    from_below, from_above = both_ways(across[:half], across[half:], "seq", X_UP)
    above, below = added(above, from_below, 0), added(below, from_above, half)
    from_below, from_above = both_ways(above, below, "seq", X_UP)
    input_grad = mine + from_below.astype(F32) + from_above.astype(F32)
    key_weight_grad, value_weight_grad = weight_sum(pieces)
    return (query_grad, input_grad.astype(BF16), key_weight_grad.T, value_weight_grad.T)


def solution(mesh):
    return jax.shard_map(
        local,
        mesh=mesh,
        in_specs=(
            P("seq", "own"),
            P("seq", "own"),
            P("seq", "own"),
            P("seq", "own"),
            P("seq", "own"),
            P("own", "seq"),
            P("own", "seq"),
            P("seq", None),
            P("seq"),
        ),
        out_specs=(P("seq", "own"), P("seq", "own"), P("own", "seq"), P("own", "seq")),
        check_vma=False,
    )
```

```python
import functools
import math

import jax
import jax.numpy as jnp
from jax import lax
from jax.experimental import pallas as pl
from jax.experimental.pallas import tpu as pltpu
from jax.sharding import PartitionSpec as P

DH = 128
GQ = 8
BLK = 128
WIN = 3
FARS = 4
NX = 4
NZ = 8
NB = 2
PLANE = NB * NZ
SLOTS = NB * FARS
X_GROUPS = [[x * NZ + z for x in range(NX)] for z in range(NZ)]
Z_GROUPS = [[x * NZ + z for z in range(NZ)] for x in range(NX)]
Z_UP = [(x * NZ + z, x * NZ + (z + 1) % NZ) for x in range(NX) for z in range(NZ)]
X_UP = [(x * NZ + z, (x + 1) % NX * NZ + z) for x in range(NX) for z in range(NZ)]
NY = 4
Y_UP = [(2 * y + core, 2 * ((y + 1) % NY) + core) for y in range(NY) for core in range(2)]
CORES = [(own, own ^ 1) for own in range(2 * NY)]
SWAP_XY = [
    (((x * NZ + z) * NY + y) * 2 + core, ((y * NZ + z) * NY + x) * 2 + core)
    for x in range(NX)
    for z in range(NZ)
    for y in range(NY)
    for core in range(2)
]
PART = DH // 4
SCALE = 1.0 / math.sqrt(DH)
EXP2_SCALE = SCALE * math.log2(math.e)
NEG = -1e30

SMEM = pl.BlockSpec(memory_space=pltpu.SMEM)
VMEM = pl.BlockSpec(memory_space=pltpu.VMEM)
NT = (((1,), (1,)), ((), ()))
F32 = jnp.float32
BF16 = jnp.bfloat16


def params(mib):
    return pltpu.CompilerParams(vmem_limit_bytes=mib << 20)


def shifted(value, axis, steps):
    count = lax.axis_size(axis)
    leading, last = (max(0, -steps), min(count, count - steps))
    return lax.ppermute(value, axis, [(source, source + steps) for source in range(leading, last)])


def both_ways(upward, downward, axis, pairs):
    back = [(target, source) for source, target in pairs]
    return lax.ppermute(upward, axis, pairs), lax.ppermute(downward, axis, back)


def ring_gather(value, axis, pairs, count):
    half = value.shape[0] // 2
    from_below, from_above = value, value
    pieces = []
    for distance in range(1, count // 2 + 1):
        if distance == count // 2:
            from_below, from_above = from_below[:half], from_above[half:]
        from_below, from_above = both_ways(from_below, from_above, axis, pairs)
        pieces += [from_below, from_above]
    return pieces


def place_pieces(out_ref, at, own_ref, pieces, count, size):
    half = size // 2
    out_ref[pl.ds(at * size, size)] = own_ref[...]
    for distance in range(1, count // 2 + 1):
        below = lax.rem(at + (count - distance), count) * size
        above = lax.rem(at + distance, count) * size
        if distance == count // 2:
            out_ref[pl.ds(below, half)] = pieces[2 * distance - 2][...]
            out_ref[pl.ds(below + half, half)] = pieces[2 * distance - 1][...]
        else:
            out_ref[pl.ds(below, size)] = pieces[2 * distance - 2][...]
            out_ref[pl.ds(above, size)] = pieces[2 * distance - 1][...]


def pick_kernel(at_ref, *refs):
    lists, own_ref, pieces = refs[:NX], refs[NX], refs[NX + 1 : -2]
    out_ref, plane_ref = refs[-2:]
    x_at, z_at = lax.div(at_ref[0], NZ), lax.rem(at_ref[0], NZ)
    place_pieces(plane_ref, z_at, own_ref, pieces, NZ, NB)
    for steps, list_ref in enumerate(lists):
        first = lax.rem(x_at + steps, NX) * SLOTS
        for j in range(SLOTS):
            out_ref[first + j] = plane_ref[lax.rem(list_ref[j // FARS, j % FARS], PLANE)]


def pick(at, lists, own, pieces):
    return pl.pallas_call(
        pick_kernel,
        out_shape=jax.ShapeDtypeStruct((NX * SLOTS, BLK, 2 * DH), BF16),
        in_specs=[SMEM] * (1 + NX) + [VMEM] * (1 + len(pieces)),
        out_specs=VMEM,
        scratch_shapes=[pltpu.VMEM((PLANE, BLK, 2 * DH), BF16)],
        compiler_params=params(16),
        name="pick_far",
    )(at, *lists, own, *pieces)


def attend_kernel(
    at_ref, far_ref, count_ref, q_ref, g_ref, prev_ref, own_ref, far_kv_ref,
    qg_ref, win_ref, farg_ref, k_ref, v_ref, kt_ref, acc_ref, tri_ref,
):
    win_ref[...] = jnp.zeros_like(win_ref)
    key_at = lax.broadcasted_iota(jnp.int32, (BLK, 2 * BLK), 0)
    query_at = lax.broadcasted_iota(jnp.int32, (BLK, 2 * BLK), 1) % BLK
    tri_ref[...] = jnp.where(key_at <= query_at, 0.0, NEG)

    def block(b, carry):
        index = at_ref[0] * NB + b
        for w in range(WIN):
            local = b + w
            both = jnp.where(local < NB, prev_ref[lax.rem(local, NB)], own_ref[lax.rem(local, NB)])
            k_ref[w * BLK : (w + 1) * BLK, :] = both[:, :DH]
            v_ref[w * BLK : (w + 1) * BLK, :] = both[:, DH:]
        for j in range(FARS):
            slot = b * FARS + j
            owner = lax.div(far_ref[b, j], PLANE)
            both = far_kv_ref[owner * SLOTS + slot]
            k_ref[(WIN + j) * BLK : (WIN + j + 1) * BLK, :] = both[:, :DH]
            v_ref[(WIN + j) * BLK : (WIN + j + 1) * BLK, :] = both[:, DH:]
        kt_ref[...] = k_ref[...].astype(F32).T.astype(BF16)
        acc_ref[...] = jnp.zeros_like(acc_ref)
        biases = [
            jnp.where(index >= 2, 0.0, NEG).astype(F32),
            jnp.where(index >= 1, 0.0, NEG).astype(F32),
            None,
        ] + [jnp.where(j < count_ref[b], 0.0, NEG).astype(F32) for j in range(FARS)]
        rows = pl.ds(pl.multiple_of(b * BLK, BLK), BLK)
        for pair in range(GQ // 2):
            lo = pair * 2 * DH
            q2 = jnp.concatenate([q_ref[rows, lo : lo + DH], q_ref[rows, lo + DH : lo + 2 * DH]])
            g2 = jnp.concatenate([g_ref[rows, lo : lo + DH], g_ref[rows, lo + DH : lo + 2 * DH]])
            scores = lax.dot_general(k_ref[...], q2, NT, preferred_element_type=F32)
            parts = []
            for c in range(WIN + FARS):
                part = scores[c * BLK : (c + 1) * BLK, :]
                bias = tri_ref[...] if biases[c] is None else biases[c]
                parts.append(part + bias)
            scores = jnp.concatenate(parts)
            top = jnp.max(scores, axis=0, keepdims=True)
            expo = jnp.exp2((scores - top) * EXP2_SCALE)
            inv = 1.0 / jnp.sum(expo, axis=0, keepdims=True)
            soft = expo * inv
            grad_p = lax.dot_general(v_ref[...], g2, NT, preferred_element_type=F32)
            delta = jnp.sum(soft * grad_p, axis=0, keepdims=True)
            soft_b = soft.astype(BF16)
            grad_s = (soft * (grad_p - delta)).astype(BF16)
            acc_ref[:, :DH] += jnp.dot(grad_s, q2, preferred_element_type=F32)
            acc_ref[:, DH:] += jnp.dot(soft_b, g2, preferred_element_type=F32)
            grad_q = jnp.dot(kt_ref[...], grad_s, preferred_element_type=F32).T * SCALE
            qg_ref[rows, lo : lo + DH] = grad_q[:BLK].astype(BF16)
            qg_ref[rows, lo + DH : lo + 2 * DH] = grad_q[BLK:].astype(BF16)
        acc_ref[:, :DH] = acc_ref[:, :DH] * SCALE
        window = pl.ds(pl.multiple_of(b * BLK, BLK), WIN * BLK)
        win_ref[window, :] += acc_ref[: WIN * BLK, :]
        for j in range(FARS):
            farg_ref[b * FARS + j] = acc_ref[(WIN + j) * BLK : (WIN + j + 1) * BLK, :].astype(BF16)
        return carry

    lax.fori_loop(0, NB, block, 0)


def attend(at, far, count, queries, out_grad, prev, own, far_kv):
    keys = (WIN + FARS) * BLK
    return pl.pallas_call(
        attend_kernel,
        out_shape=(
            jax.ShapeDtypeStruct((NB * BLK, GQ * DH), BF16),
            jax.ShapeDtypeStruct((2 * NB * BLK, 2 * DH), F32),
            jax.ShapeDtypeStruct((SLOTS, BLK, 2 * DH), BF16),
        ),
        in_specs=[SMEM, SMEM, SMEM] + [VMEM] * 5,
        out_specs=(VMEM, VMEM, VMEM),
        scratch_shapes=[
            pltpu.VMEM((keys, DH), BF16),
            pltpu.VMEM((keys, DH), BF16),
            pltpu.VMEM((DH, keys), BF16),
            pltpu.VMEM((keys, 2 * DH), F32),
            pltpu.VMEM((BLK, 2 * BLK), F32),
        ],
        compiler_params=params(24),
        cost_estimate=pl.CostEstimate(flops=2_400_000_000 * 4, bytes_accessed=6 << 20, transcendentals=2_000_000),
        name="attend",
    )(at, far, count, queries, out_grad, prev, own, far_kv)


def spread_kernel(at_ref, *refs):
    lists, pieces = refs[:NX], refs[NX:-2]
    out_ref, acc_ref = refs[-2:]
    mine, below, above, across_low, across_high = pieces
    x_at = lax.div(at_ref[0], NZ)
    acc_ref[...] = jnp.zeros_like(acc_ref)

    def add(listed, term_ref, j):
        @pl.when(lax.div(listed, PLANE) == x_at)
        def _():
            acc_ref[lax.rem(listed, PLANE)] += term_ref[j].astype(F32)

    half = SLOTS // 2
    for j in range(SLOTS):
        add(lists[0][j // FARS, j % FARS], mine, j)
        add(lists[1][j // FARS, j % FARS], above, j)
        add(lists[2][j // FARS, j % FARS], across_low if j < half else across_high, j % half)
        add(lists[3][j // FARS, j % FARS], below, j)
    out_ref[...] = acc_ref[...].astype(BF16)


def spread(at, lists, own, pieces):
    return pl.pallas_call(
        spread_kernel,
        out_shape=jax.ShapeDtypeStruct((PLANE, BLK, 2 * DH), BF16),
        in_specs=[SMEM] * (1 + NX) + [VMEM] * (1 + len(pieces)),
        out_specs=VMEM,
        scratch_shapes=[pltpu.VMEM((PLANE, BLK, 2 * DH), F32)],
        compiler_params=params(16),
        name="spread_far",
    )(at, *lists, own, *pieces)


def finish_kernel(terms_ref, back_ref, window_ref, out_ref):
    total = window_ref[NB * BLK :, :] + back_ref[...].astype(F32)
    for z in range(NZ):
        total += terms_ref[z].astype(F32)
    source = lax.broadcasted_iota(jnp.int32, (2 * DH, 2 * DH), 0)
    target = lax.broadcasted_iota(jnp.int32, (2 * DH, 2 * DH), 1)
    part, rest = target // (2 * PART), target % (2 * PART)
    wanted = (rest // PART) * DH + part * PART + rest % PART
    order = jnp.where(source == wanted, 1.0, 0.0).astype(BF16)
    out_ref[...] = jnp.dot(
        total.astype(BF16), order, preferred_element_type=F32
    ).astype(BF16)


def finish(terms, back, window):
    return pl.pallas_call(
        finish_kernel,
        out_shape=jax.ShapeDtypeStruct((NB * BLK, 2 * DH), BF16),
        in_specs=[VMEM] * 3,
        out_specs=VMEM,
        compiler_params=params(12),
        name="finish_kv",
    )(terms, back, window)


def heads_kernel(at_ref, own_ref, *refs):
    *pieces, other_ref, out_ref = refs
    at, core = lax.div(at_ref[0], 2), lax.rem(at_ref[0], 2)
    rows = NB * BLK
    half = rows // 2
    below, above = lax.rem(at + NY - 1, NY), lax.rem(at + 1, NY)
    across = lax.rem(at + 2, NY)
    starts = (0, rows, 2 * rows, 3 * rows, 3 * rows + half)
    for k, (y, low, high) in enumerate(
        ((at, 0, rows), (below, 0, rows), (above, 0, rows), (across, 0, half), (across, half, rows))
    ):
        mine = own_ref if k == 0 else pieces[k - 1]
        out_ref[2 * y + core, low:high, :] = mine[...]
        out_ref[2 * y + 1 - core, low:high, :] = other_ref[starts[k] : starts[k] + high - low, :]


def place_heads(at, own, pieces, other):
    return pl.pallas_call(
        heads_kernel,
        out_shape=jax.ShapeDtypeStruct((2 * NY, *own.shape), BF16),
        in_specs=[SMEM] + [VMEM] * (2 + len(pieces)),
        out_specs=VMEM,
        compiler_params=params(8),
        name="place_heads",
    )(at, own, *pieces, other)


def weights_kernel(grad_ref, inputs_ref, out_ref):
    quarters, wide = 4, inputs_ref.shape[1] // 4
    for head in range(2):
        grad = jnp.concatenate([grad_ref[x * 2 + head] for x in range(NX)])
        term = lax.dot_general(
            grad, inputs_ref[...], (((0,), (0,)), ((), ())), preferred_element_type=F32
        ).astype(BF16)
        for part in range(4):
            for quarter in range(quarters):
                out_ref[
                    head * 4 + part, quarter * 2 * PART : (quarter + 1) * 2 * PART, :
                ] = term[
                    part * 2 * PART : (part + 1) * 2 * PART, quarter * wide : (quarter + 1) * wide
                ]


def weight_terms(grad, inputs_x):
    return pl.pallas_call(
        weights_kernel,
        out_shape=jax.ShapeDtypeStruct((NZ, 4 * 2 * PART, inputs_x.shape[1] // 4), BF16),
        in_specs=[VMEM, VMEM],
        out_specs=VMEM,
        compiler_params=params(16),
        cost_estimate=pl.CostEstimate(flops=1 << 30, bytes_accessed=4 << 20, transcendentals=0),
        name="weight_terms",
    )(grad, inputs_x)


def weight_sum_kernel(terms_ref, key_ref, value_ref):
    total = terms_ref[0].astype(F32)
    for z in range(1, NZ):
        total += terms_ref[z].astype(F32)
    wide = total.shape[1]
    for quarter in range(4):
        low = quarter * 2 * PART
        key_ref[:, quarter * wide : (quarter + 1) * wide] = total[low : low + PART]
        value_ref[:, quarter * wide : (quarter + 1) * wide] = total[low + PART : low + 2 * PART]


def weight_sum(terms):
    out = jax.ShapeDtypeStruct((PART, 4 * terms.shape[2]), F32)
    return pl.pallas_call(
        weight_sum_kernel,
        out_shape=(out, out),
        in_specs=[VMEM],
        out_specs=(VMEM, VMEM),
        compiler_params=params(8),
        name="weight_sum",
    )(terms)


def input_kernel(at_ref, grad_ref, weights_ref, mine_ref, above_ref, low_ref, high_ref, below_ref):
    x_at = lax.div(at_ref[0], NZ)
    half = low_ref.shape[0]
    for steps in range(NX):
        x = lax.rem(x_at + steps, NX)
        grad = jnp.concatenate([grad_ref[2 * x], grad_ref[2 * x + 1]], axis=1)
        term = jnp.dot(grad, weights_ref[...], preferred_element_type=F32)
        if steps == 2:
            low_ref[...] = term[:half].astype(BF16)
            high_ref[...] = term[half:].astype(BF16)
        else:
            out_ref = (mine_ref, above_ref, None, below_ref)[steps]
            out_ref[...] = term.astype(out_ref.dtype)


def input_terms(at, grad, weights):
    rows, wide = grad.shape[1], weights.shape[1]
    send, half = (jax.ShapeDtypeStruct((size, wide), BF16) for size in (rows, rows // 2))
    return pl.pallas_call(
        input_kernel,
        out_shape=(jax.ShapeDtypeStruct((rows, wide), F32), send, half, half, send),
        in_specs=[SMEM, VMEM, VMEM],
        out_specs=(VMEM,) * 5,
        compiler_params=params(16),
        cost_estimate=pl.CostEstimate(flops=1 << 30, bytes_accessed=4 << 20, transcendentals=0),
        name="input_terms",
    )(at, grad, weights)


def added(term, arrived, low):
    high = low + arrived.shape[0]
    rows = (term[low:high].astype(F32) + arrived.astype(F32)).astype(BF16)
    return jnp.concatenate([term[:low], rows, term[high:]])


def local(
    queries, key_rows, value_rows, out_grad, inputs, key_weight, value_weight, far_blocks, far_count
):
    tokens = queries.shape[0]
    seq_index = lax.axis_index("seq").astype(jnp.int32)
    at = seq_index.reshape(1)
    own_index = lax.axis_index("own").astype(jnp.int32).reshape(1)
    own_kv = jnp.concatenate([key_rows, value_rows], axis=1).reshape(NB, BLK, 2 * DH)

    inputs_x = lax.all_gather(inputs, "seq", axis=0, axis_index_groups=X_GROUPS, tiled=True)

    from_below, from_above, listed = own_kv, own_kv, far_blocks
    plane, lists = [], []
    for distance in range(1, NZ // 2 + 1):
        if distance == NZ // 2:
            from_below, from_above = from_below[: NB // 2], from_above[NB // 2 :]
        from_below, from_above = both_ways(from_below, from_above, "seq", Z_UP)
        if distance < NX:
            pairs = [(x * NZ + z, (x - distance) % NX * NZ + z) for x in range(NX) for z in range(NZ)]
            arrived = lax.ppermute(listed, "seq", pairs)
            arrived, listed, from_below, from_above = lax.optimization_barrier(
                (arrived, listed, from_below, from_above)
            )
            lists.append(arrived)
        plane += [from_below, from_above]
    lists = [far_blocks, *lists]
    from_below, key_weight, value_weight = lax.optimization_barrier(
        (plane[0], key_weight, value_weight)
    )
    plane[0] = from_below
    weights = jnp.concatenate([key_weight.T, value_weight.T])
    weights = lax.all_gather(weights, "seq", axis=0, axis_index_groups=Z_GROUPS, tiled=True)
    prev_kv = shifted(own_kv, "seq", 1)
    chosen = pick(at, lists, own_kv, plane)
    far_kv = lax.all_to_all(chosen, "seq", 0, 0, axis_index_groups=X_GROUPS, tiled=True)

    far_kv, inputs_x = lax.optimization_barrier((far_kv, inputs_x))
    query_grad, window, far_grad = attend(
        at, far_blocks, far_count, queries, out_grad, prev_kv, own_kv, far_kv
    )
    far_all = ring_gather(far_grad, "seq", X_UP, NX)
    back = shifted(window[:tokens].astype(BF16), "seq", -1)
    dense = spread(at, lists, far_grad, far_all)
    dense, weights = lax.optimization_barrier((dense, weights))
    dense = dense.reshape(NZ, tokens, 2 * DH)
    terms = lax.all_to_all(dense, "seq", 0, 0, axis_index_groups=Z_GROUPS, tiled=True)
    kv_grad = finish(terms, back, window)

    moved = lax.ppermute(kv_grad, ("seq", "own"), SWAP_XY)
    same_core = ring_gather(moved, "own", Y_UP, NY)
    other_core = lax.ppermute(jnp.concatenate([moved, *same_core]), "own", CORES)
    heads = place_heads(own_index, moved, same_core, other_core)

    mine, above, low, high, below = input_terms(at, heads, weights)
    heads, low, high = lax.optimization_barrier((heads, low, high))
    from_below, from_above = both_ways(low, high, "seq", X_UP)
    pieces = weight_terms(heads, inputs_x)
    pieces = lax.all_to_all(pieces, "seq", 0, 0, axis_index_groups=Z_GROUPS, tiled=True)
    above, below = added(above, from_below, 0), added(below, from_above, tokens // 2)
    from_below, from_above = both_ways(above, below, "seq", X_UP)
    input_grad = mine + from_below.astype(F32) + from_above.astype(F32)
    key_weight_grad, value_weight_grad = weight_sum(pieces)
    return (query_grad, input_grad.astype(BF16), key_weight_grad.T, value_weight_grad.T)


def solution(mesh):
    return jax.shard_map(
        local,
        mesh=mesh,
        in_specs=(
            P("seq", "own"),
            P("seq", "own"),
            P("seq", "own"),
            P("seq", "own"),
            P("seq", "own"),
            P("own", "seq"),
            P("own", "seq"),
            P("seq", None),
            P("seq"),
        ),
        out_specs=(P("seq", "own"), P("seq", "own"), P("own", "seq"), P("own", "seq")),
        check_vma=False,
    )
```

```python
import functools
import math

import jax
import jax.numpy as jnp
from jax import lax
from jax.experimental import pallas as pl
from jax.experimental.pallas import tpu as pltpu
from jax.sharding import PartitionSpec as P

DH = 128
GQ = 8
BLK = 128
WIN = 3
FARS = 4
NX = 4
NZ = 8
NB = 2
PLANE = NB * NZ
SLOTS = NB * FARS
X_GROUPS = [[x * NZ + z for x in range(NX)] for z in range(NZ)]
Z_GROUPS = [[x * NZ + z for z in range(NZ)] for x in range(NX)]
Z_UP = [(x * NZ + z, x * NZ + (z + 1) % NZ) for x in range(NX) for z in range(NZ)]
X_UP = [(x * NZ + z, (x + 1) % NX * NZ + z) for x in range(NX) for z in range(NZ)]
NY = 4
Y_UP = [(2 * y + core, 2 * ((y + 1) % NY) + core) for y in range(NY) for core in range(2)]
CORES = [(own, own ^ 1) for own in range(2 * NY)]
SWAP_XY = [
    (((x * NZ + z) * NY + y) * 2 + core, ((y * NZ + z) * NY + x) * 2 + core)
    for x in range(NX)
    for z in range(NZ)
    for y in range(NY)
    for core in range(2)
]
PART = DH // 4
SCALE = 1.0 / math.sqrt(DH)
EXP2_SCALE = SCALE * math.log2(math.e)
NEG = -1e30

SMEM = pl.BlockSpec(memory_space=pltpu.SMEM)
VMEM = pl.BlockSpec(memory_space=pltpu.VMEM)
NT = (((1,), (1,)), ((), ()))
F32 = jnp.float32
BF16 = jnp.bfloat16


def params(mib):
    return pltpu.CompilerParams(vmem_limit_bytes=mib << 20)


def shifted(value, axis, steps):
    count = lax.axis_size(axis)
    leading, last = (max(0, -steps), min(count, count - steps))
    return lax.ppermute(value, axis, [(source, source + steps) for source in range(leading, last)])


def both_ways(upward, downward, axis, pairs):
    back = [(target, source) for source, target in pairs]
    return lax.ppermute(upward, axis, pairs), lax.ppermute(downward, axis, back)


def ring_gather(value, axis, pairs, count):
    half = value.shape[0] // 2
    from_below, from_above = value, value
    pieces = []
    for distance in range(1, count // 2 + 1):
        if distance == count // 2:
            from_below, from_above = from_below[:half], from_above[half:]
        from_below, from_above = both_ways(from_below, from_above, axis, pairs)
        pieces += [from_below, from_above]
    return pieces


def place_pieces(out_ref, at, own_ref, pieces, count, size):
    half = size // 2
    out_ref[pl.ds(at * size, size)] = own_ref[...]
    for distance in range(1, count // 2 + 1):
        below = lax.rem(at + (count - distance), count) * size
        above = lax.rem(at + distance, count) * size
        if distance == count // 2:
            out_ref[pl.ds(below, half)] = pieces[2 * distance - 2][...]
            out_ref[pl.ds(below + half, half)] = pieces[2 * distance - 1][...]
        else:
            out_ref[pl.ds(below, size)] = pieces[2 * distance - 2][...]
            out_ref[pl.ds(above, size)] = pieces[2 * distance - 1][...]


def across_kernel(at_ref, across_ref, own_ref, *refs):
    *pieces, plane_ref, low_ref, high_ref = refs
    place_pieces(plane_ref, lax.rem(at_ref[0], NZ), own_ref, pieces, NZ, NB)
    for b, out_ref in enumerate((low_ref, high_ref)):
        for j in range(FARS):
            out_ref[j] = plane_ref[lax.rem(across_ref[b, j], PLANE)]


def pick_across(at, across, own, pieces):
    half = jax.ShapeDtypeStruct((FARS, BLK, 2 * DH), BF16)
    return pl.pallas_call(
        across_kernel,
        out_shape=(jax.ShapeDtypeStruct((PLANE, BLK, 2 * DH), BF16), half, half),
        in_specs=[SMEM] * 2 + [VMEM] * (1 + len(pieces)),
        out_specs=(VMEM,) * 3,
        compiler_params=params(8),
        name="pick_across",
    )(at, across, own, *pieces)


def pick_kernel(at_ref, above_ref, below_ref, plane_ref, low_ref, high_ref, up_ref, down_ref):
    x_at = lax.div(at_ref[0], NZ)
    for list_ref, arrived_ref, behind, passed, out_ref in (
        (above_ref, low_ref, lax.rem(x_at + NX - 1, NX), 0, up_ref),
        (below_ref, high_ref, lax.rem(x_at + 1, NX), 1, down_ref),
    ):
        for b in range(NB):
            for j in range(FARS):
                listed = list_ref[b, j]
                slot = b * FARS + j
                if b == passed:
                    passes = lax.div(listed, PLANE) == behind

                    @pl.when(passes)
                    def _():
                        out_ref[slot] = arrived_ref[j]

                    @pl.when(jnp.logical_not(passes))
                    def _():
                        out_ref[slot] = plane_ref[lax.rem(listed, PLANE)]
                else:
                    out_ref[slot] = plane_ref[lax.rem(listed, PLANE)]


def pick(at, above, below, plane, low, high):
    out = jax.ShapeDtypeStruct((SLOTS, BLK, 2 * DH), BF16)
    return pl.pallas_call(
        pick_kernel,
        out_shape=(out, out),
        in_specs=[SMEM] * 3 + [VMEM] * 3,
        out_specs=(VMEM, VMEM),
        compiler_params=params(8),
        name="pick_far",
    )(at, above, below, plane, low, high)


def attend_kernel(
    at_ref, far_ref, count_ref, q_ref, g_ref, prev_ref, own_ref, plane_ref, below_ref, above_ref,
    qg_ref, win_ref, farg_ref, k_ref, v_ref, kt_ref, acc_ref, tri_ref,
):
    win_ref[...] = jnp.zeros_like(win_ref)
    key_at = lax.broadcasted_iota(jnp.int32, (BLK, 2 * BLK), 0)
    query_at = lax.broadcasted_iota(jnp.int32, (BLK, 2 * BLK), 1) % BLK
    tri_ref[...] = jnp.where(key_at <= query_at, 0.0, NEG)

    def block(b, carry):
        index = at_ref[0] * NB + b
        for w in range(WIN):
            local = b + w
            both = jnp.where(local < NB, prev_ref[lax.rem(local, NB)], own_ref[lax.rem(local, NB)])
            k_ref[w * BLK : (w + 1) * BLK, :] = both[:, :DH]
            v_ref[w * BLK : (w + 1) * BLK, :] = both[:, DH:]
        for j in range(FARS):
            slot = b * FARS + j
            steps = lax.rem(lax.div(far_ref[b, j], PLANE) + (NX - lax.div(at_ref[0], NZ)), NX)
            mine = plane_ref[lax.rem(far_ref[b, j], PLANE)]
            from_below = (steps == NX - 1) | ((steps == 2) & (b == 0))
            both = jnp.where(from_below, below_ref[slot], above_ref[slot])
            both = jnp.where(steps == 0, mine, both)
            k_ref[(WIN + j) * BLK : (WIN + j + 1) * BLK, :] = both[:, :DH]
            v_ref[(WIN + j) * BLK : (WIN + j + 1) * BLK, :] = both[:, DH:]
        kt_ref[...] = k_ref[...].astype(F32).T.astype(BF16)
        acc_ref[...] = jnp.zeros_like(acc_ref)
        biases = [
            jnp.where(index >= 2, 0.0, NEG).astype(F32),
            jnp.where(index >= 1, 0.0, NEG).astype(F32),
            None,
        ] + [jnp.where(j < count_ref[b], 0.0, NEG).astype(F32) for j in range(FARS)]
        rows = pl.ds(pl.multiple_of(b * BLK, BLK), BLK)
        for pair in range(GQ // 2):
            lo = pair * 2 * DH
            q2 = jnp.concatenate([q_ref[rows, lo : lo + DH], q_ref[rows, lo + DH : lo + 2 * DH]])
            g2 = jnp.concatenate([g_ref[rows, lo : lo + DH], g_ref[rows, lo + DH : lo + 2 * DH]])
            scores = lax.dot_general(k_ref[...], q2, NT, preferred_element_type=F32)
            parts = [scores[c * BLK : (c + 1) * BLK, :] for c in range(WIN + FARS)]
            parts[WIN - 1] = parts[WIN - 1] + tri_ref[...]
            tops = [
                jnp.max(part, axis=0, keepdims=True) + (0.0 if bias is None else bias)
                for part, bias in zip(parts, biases)
            ]
            top = functools.reduce(jnp.maximum, tops)
            expo = jnp.concatenate(
                [
                    jnp.exp2((part - (top if bias is None else top - bias)) * EXP2_SCALE)
                    for part, bias in zip(parts, biases)
                ]
            )
            inv = 1.0 / jnp.sum(expo, axis=0, keepdims=True)
            soft = expo * inv
            grad_p = lax.dot_general(v_ref[...], g2, NT, preferred_element_type=F32)
            delta = jnp.sum(soft * grad_p, axis=0, keepdims=True)
            soft_b = soft.astype(BF16)
            grad_s = (soft * (grad_p - delta)).astype(BF16)
            acc_ref[:, :DH] += jnp.dot(grad_s, q2, preferred_element_type=F32)
            acc_ref[:, DH:] += jnp.dot(soft_b, g2, preferred_element_type=F32)
            grad_q = jnp.dot(kt_ref[...], grad_s, preferred_element_type=F32).T * SCALE
            qg_ref[rows, lo : lo + DH] = grad_q[:BLK].astype(BF16)
            qg_ref[rows, lo + DH : lo + 2 * DH] = grad_q[BLK:].astype(BF16)
        acc_ref[:, :DH] = acc_ref[:, :DH] * SCALE
        window = pl.ds(pl.multiple_of(b * BLK, BLK), WIN * BLK)
        win_ref[window, :] += acc_ref[: WIN * BLK, :]
        for j in range(FARS):
            farg_ref[b * FARS + j] = acc_ref[(WIN + j) * BLK : (WIN + j + 1) * BLK, :].astype(BF16)
        return carry

    for b in range(NB):
        block(b, 0)


def attend(at, far, count, queries, out_grad, prev, own, plane, below, above):
    keys = (WIN + FARS) * BLK
    return pl.pallas_call(
        attend_kernel,
        out_shape=(
            jax.ShapeDtypeStruct((NB * BLK, GQ * DH), BF16),
            jax.ShapeDtypeStruct((2 * NB * BLK, 2 * DH), F32),
            jax.ShapeDtypeStruct((SLOTS, BLK, 2 * DH), BF16),
        ),
        in_specs=[SMEM, SMEM, SMEM] + [VMEM] * 7,
        out_specs=(VMEM, VMEM, VMEM),
        scratch_shapes=[
            pltpu.VMEM((keys, DH), BF16),
            pltpu.VMEM((keys, DH), BF16),
            pltpu.VMEM((DH, keys), BF16),
            pltpu.VMEM((keys, 2 * DH), F32),
            pltpu.VMEM((BLK, 2 * BLK), F32),
        ],
        compiler_params=params(24),
        cost_estimate=pl.CostEstimate(flops=2_400_000_000 * 4, bytes_accessed=6 << 20, transcendentals=2_000_000),
        name="attend",
    )(at, far, count, queries, out_grad, prev, own, plane, below, above)


def spread_kernel(at_ref, *refs):
    lists, pieces = refs[:NX], refs[NX:-2]
    out_ref, acc_ref = refs[-2:]
    mine, below, above, across_low, across_high = pieces
    x_at = lax.div(at_ref[0], NZ)
    acc_ref[...] = jnp.zeros_like(acc_ref)

    def add(listed, term_ref, j):
        @pl.when(lax.div(listed, PLANE) == x_at)
        def _():
            acc_ref[lax.rem(listed, PLANE)] += term_ref[j].astype(F32)

    half = SLOTS // 2
    for j in range(SLOTS):
        add(lists[0][j // FARS, j % FARS], mine, j)
        add(lists[1][j // FARS, j % FARS], above, j)
        add(lists[2][j // FARS, j % FARS], across_low if j < half else across_high, j % half)
        add(lists[3][j // FARS, j % FARS], below, j)
    out_ref[...] = acc_ref[...].astype(BF16)


def spread(at, lists, own, pieces):
    return pl.pallas_call(
        spread_kernel,
        out_shape=jax.ShapeDtypeStruct((PLANE, BLK, 2 * DH), BF16),
        in_specs=[SMEM] * (1 + NX) + [VMEM] * (1 + len(pieces)),
        out_specs=VMEM,
        scratch_shapes=[pltpu.VMEM((PLANE, BLK, 2 * DH), F32)],
        compiler_params=params(16),
        name="spread_far",
    )(at, *lists, own, *pieces)


def finish_kernel(terms_ref, back_ref, window_ref, out_ref):
    total = window_ref[NB * BLK :, :] + back_ref[...].astype(F32)
    for z in range(NZ):
        total += terms_ref[z].astype(F32)
    source = lax.broadcasted_iota(jnp.int32, (2 * DH, 2 * DH), 0)
    target = lax.broadcasted_iota(jnp.int32, (2 * DH, 2 * DH), 1)
    part, rest = target // (2 * PART), target % (2 * PART)
    wanted = (rest // PART) * DH + part * PART + rest % PART
    order = jnp.where(source == wanted, 1.0, 0.0).astype(BF16)
    out_ref[...] = jnp.dot(
        total.astype(BF16), order, preferred_element_type=F32
    ).astype(BF16)


def finish(terms, back, window):
    return pl.pallas_call(
        finish_kernel,
        out_shape=jax.ShapeDtypeStruct((NB * BLK, 2 * DH), BF16),
        in_specs=[VMEM] * 3,
        out_specs=VMEM,
        compiler_params=params(12),
        name="finish_kv",
    )(terms, back, window)


def heads_kernel(at_ref, own_ref, *refs):
    *pieces, other_ref, out_ref = refs
    at, core = lax.div(at_ref[0], 2), lax.rem(at_ref[0], 2)
    rows = NB * BLK
    half = rows // 2
    below, above = lax.rem(at + NY - 1, NY), lax.rem(at + 1, NY)
    across = lax.rem(at + 2, NY)
    starts = (0, rows, 2 * rows, 3 * rows, 3 * rows + half)
    for k, (y, low, high) in enumerate(
        ((at, 0, rows), (below, 0, rows), (above, 0, rows), (across, 0, half), (across, half, rows))
    ):
        mine = own_ref if k == 0 else pieces[k - 1]
        out_ref[2 * y + core, low:high, :] = mine[...]
        out_ref[2 * y + 1 - core, low:high, :] = other_ref[starts[k] : starts[k] + high - low, :]


def place_heads(at, own, pieces, other):
    return pl.pallas_call(
        heads_kernel,
        out_shape=jax.ShapeDtypeStruct((2 * NY, *own.shape), BF16),
        in_specs=[SMEM] + [VMEM] * (2 + len(pieces)),
        out_specs=VMEM,
        compiler_params=params(8),
        name="place_heads",
    )(at, own, *pieces, other)


def weights_kernel(grad_ref, inputs_ref, out_ref):
    quarters, wide = 4, inputs_ref.shape[1] // 4
    for head in range(2):
        grad = jnp.concatenate([grad_ref[x * 2 + head] for x in range(NX)])
        term = lax.dot_general(
            grad, inputs_ref[...], (((0,), (0,)), ((), ())), preferred_element_type=F32
        ).astype(BF16)
        for part in range(4):
            for quarter in range(quarters):
                out_ref[
                    head * 4 + part, quarter * 2 * PART : (quarter + 1) * 2 * PART, :
                ] = term[
                    part * 2 * PART : (part + 1) * 2 * PART, quarter * wide : (quarter + 1) * wide
                ]


def weight_terms(grad, inputs_x):
    return pl.pallas_call(
        weights_kernel,
        out_shape=jax.ShapeDtypeStruct((NZ, 4 * 2 * PART, inputs_x.shape[1] // 4), BF16),
        in_specs=[VMEM, VMEM],
        out_specs=VMEM,
        compiler_params=params(16),
        cost_estimate=pl.CostEstimate(flops=1 << 30, bytes_accessed=4 << 20, transcendentals=0),
        name="weight_terms",
    )(grad, inputs_x)


def weight_sum_kernel(terms_ref, key_ref, value_ref):
    total = terms_ref[0].astype(F32)
    for z in range(1, NZ):
        total += terms_ref[z].astype(F32)
    wide = total.shape[1]
    for quarter in range(4):
        low = quarter * 2 * PART
        key_ref[:, quarter * wide : (quarter + 1) * wide] = total[low : low + PART]
        value_ref[:, quarter * wide : (quarter + 1) * wide] = total[low + PART : low + 2 * PART]


def weight_sum(terms):
    out = jax.ShapeDtypeStruct((PART, 4 * terms.shape[2]), F32)
    return pl.pallas_call(
        weight_sum_kernel,
        out_shape=(out, out),
        in_specs=[VMEM],
        out_specs=(VMEM, VMEM),
        compiler_params=params(8),
        name="weight_sum",
    )(terms)


def input_kernel(at_ref, grad_ref, weights_ref, mine_ref, above_ref, low_ref, high_ref, below_ref):
    x_at = lax.div(at_ref[0], NZ)
    half = low_ref.shape[0]
    for steps in range(NX):
        x = lax.rem(x_at + steps, NX)
        grad = jnp.concatenate([grad_ref[2 * x], grad_ref[2 * x + 1]], axis=1)
        term = jnp.dot(grad, weights_ref[...], preferred_element_type=F32)
        if steps == 2:
            low_ref[...] = term[:half].astype(BF16)
            high_ref[...] = term[half:].astype(BF16)
        else:
            out_ref = (mine_ref, above_ref, None, below_ref)[steps]
            out_ref[...] = term.astype(out_ref.dtype)


def input_terms(at, grad, weights):
    rows, wide = grad.shape[1], weights.shape[1]
    send, half = (jax.ShapeDtypeStruct((size, wide), BF16) for size in (rows, rows // 2))
    return pl.pallas_call(
        input_kernel,
        out_shape=(jax.ShapeDtypeStruct((rows, wide), F32), send, half, half, send),
        in_specs=[SMEM, VMEM, VMEM],
        out_specs=(VMEM,) * 5,
        compiler_params=params(16),
        cost_estimate=pl.CostEstimate(flops=1 << 30, bytes_accessed=4 << 20, transcendentals=0),
        name="input_terms",
    )(at, grad, weights)


def added(term, arrived, low):
    high = low + arrived.shape[0]
    rows = (term[low:high].astype(F32) + arrived.astype(F32)).astype(BF16)
    return jnp.concatenate([term[:low], rows, term[high:]])


def local(
    queries, key_rows, value_rows, out_grad, inputs, key_weight, value_weight, far_blocks, far_count
):
    tokens = queries.shape[0]
    seq_index = lax.axis_index("seq").astype(jnp.int32)
    at = seq_index.reshape(1)
    own_index = lax.axis_index("own").astype(jnp.int32).reshape(1)
    own_kv = jnp.concatenate([key_rows, value_rows], axis=1).reshape(NB, BLK, 2 * DH)

    inputs_x = lax.all_gather(inputs, "seq", axis=0, axis_index_groups=X_GROUPS, tiled=True)

    from_below, from_above, listed = own_kv, own_kv, far_blocks
    plane, lists = [], []
    for distance in range(1, NZ // 2 + 1):
        if distance == NZ // 2:
            from_below, from_above = from_below[: NB // 2], from_above[NB // 2 :]
        from_below, from_above = both_ways(from_below, from_above, "seq", Z_UP)
        if distance < NX:
            pairs = [(x * NZ + z, (x - distance) % NX * NZ + z) for x in range(NX) for z in range(NZ)]
            arrived = lax.ppermute(listed, "seq", pairs)
            arrived, listed, from_below, from_above = lax.optimization_barrier(
                (arrived, listed, from_below, from_above)
            )
            lists.append(arrived)
        plane += [from_below, from_above]
    lists = [far_blocks, *lists]
    from_below, key_weight, value_weight = lax.optimization_barrier(
        (plane[0], key_weight, value_weight)
    )
    plane[0] = from_below
    weights = jnp.concatenate([key_weight.T, value_weight.T])
    weights = lax.all_gather(weights, "seq", axis=0, axis_index_groups=Z_GROUPS, tiled=True)
    prev_kv = shifted(own_kv, "seq", 1)
    plane, low, high = pick_across(at, lists[2], own_kv, plane)
    low, high = both_ways(low, high, "seq", X_UP)
    up, down = pick(at, lists[1], lists[3], plane, low, high)
    from_below, from_above = both_ways(up, down, "seq", X_UP)

    far_count, inputs_x = lax.optimization_barrier((far_count, inputs_x))
    query_grad, window, far_grad = attend(
        at, far_blocks, far_count, queries, out_grad, prev_kv, own_kv, plane, from_below, from_above
    )
    far_all = ring_gather(far_grad, "seq", X_UP, NX)
    back = shifted(window[:tokens].astype(BF16), "seq", -1)
    above, weights = lax.optimization_barrier((lists[1], weights))
    dense = spread(at, [lists[0], above, *lists[2:]], far_grad, far_all)
    dense = dense.reshape(NZ, tokens, 2 * DH)
    terms = lax.all_to_all(dense, "seq", 0, 0, axis_index_groups=Z_GROUPS, tiled=True)
    kv_grad = finish(terms, back, window)

    moved = lax.ppermute(kv_grad, ("seq", "own"), SWAP_XY)
    same_core = ring_gather(moved, "own", Y_UP, NY)
    other_core = lax.ppermute(jnp.concatenate([moved, *same_core]), "own", CORES)
    heads = place_heads(own_index, moved, same_core, other_core)

    mine, above, low, high, below = input_terms(at, heads, weights)
    from_below, from_above = both_ways(low, high, "seq", X_UP)
    pieces = weight_terms(heads, inputs_x)
    pieces = lax.all_to_all(pieces, "seq", 0, 0, axis_index_groups=Z_GROUPS, tiled=True)
    above, below = added(above, from_below, 0), added(below, from_above, tokens // 2)
    from_below, from_above = both_ways(above, below, "seq", X_UP)
    input_grad = mine + from_below.astype(F32) + from_above.astype(F32)
    key_weight_grad, value_weight_grad = weight_sum(pieces)
    return (query_grad, input_grad.astype(BF16), key_weight_grad.T, value_weight_grad.T)


def solution(mesh):
    return jax.shard_map(
        local,
        mesh=mesh,
        in_specs=(
            P("seq", "own"),
            P("seq", "own"),
            P("seq", "own"),
            P("seq", "own"),
            P("seq", "own"),
            P("own", "seq"),
            P("own", "seq"),
            P("seq", None),
            P("seq"),
        ),
        out_specs=(P("seq", "own"), P("seq", "own"), P("own", "seq"), P("own", "seq")),
        check_vma=False,
    )
```

```python
import functools
import math

import jax
import jax.numpy as jnp
from jax import lax
from jax.experimental import pallas as pl
from jax.experimental.pallas import tpu as pltpu
from jax.sharding import PartitionSpec as P

DH = 128
GQ = 8
BLK = 128
WIN = 3
FARS = 4
NX = 4
NZ = 8
NB = 2
PLANE = NB * NZ
SLOTS = NB * FARS
X_GROUPS = [[x * NZ + z for x in range(NX)] for z in range(NZ)]
Z_GROUPS = [[x * NZ + z for z in range(NZ)] for x in range(NX)]
Z_UP = [(x * NZ + z, x * NZ + (z + 1) % NZ) for x in range(NX) for z in range(NZ)]
X_UP = [(x * NZ + z, (x + 1) % NX * NZ + z) for x in range(NX) for z in range(NZ)]
NY = 4
Y_UP = [(2 * y + core, 2 * ((y + 1) % NY) + core) for y in range(NY) for core in range(2)]
CORES = [(own, own ^ 1) for own in range(2 * NY)]
SWAP_XY = [
    (((x * NZ + z) * NY + y) * 2 + core, ((y * NZ + z) * NY + x) * 2 + core)
    for x in range(NX)
    for z in range(NZ)
    for y in range(NY)
    for core in range(2)
]
PART = DH // 4
SCALE = 1.0 / math.sqrt(DH)
EXP2_SCALE = SCALE * math.log2(math.e)
NEG = -1e30

SMEM = pl.BlockSpec(memory_space=pltpu.SMEM)
VMEM = pl.BlockSpec(memory_space=pltpu.VMEM)
HBM = pl.BlockSpec(memory_space=pltpu.HBM)
NT = (((1,), (1,)), ((), ()))
F32 = jnp.float32
BF16 = jnp.bfloat16


def params(mib):
    return pltpu.CompilerParams(vmem_limit_bytes=mib << 20)


def shifted(value, axis, steps):
    count = lax.axis_size(axis)
    leading, last = (max(0, -steps), min(count, count - steps))
    return lax.ppermute(value, axis, [(source, source + steps) for source in range(leading, last)])


def both_ways(upward, downward, axis, pairs):
    back = [(target, source) for source, target in pairs]
    return lax.ppermute(upward, axis, pairs), lax.ppermute(downward, axis, back)


def ring_gather(value, axis, pairs, count):
    half = value.shape[0] // 2
    from_below, from_above = value, value
    pieces = []
    for distance in range(1, count // 2 + 1):
        if distance == count // 2:
            from_below, from_above = from_below[:half], from_above[half:]
        from_below, from_above = both_ways(from_below, from_above, axis, pairs)
        pieces += [from_below, from_above]
    return pieces


def place_pieces(out_ref, at, own_ref, pieces, count, size):
    half = size // 2
    out_ref[pl.ds(at * size, size)] = own_ref[...]
    for distance in range(1, count // 2 + 1):
        below = lax.rem(at + (count - distance), count) * size
        above = lax.rem(at + distance, count) * size
        if distance == count // 2:
            out_ref[pl.ds(below, half)] = pieces[2 * distance - 2][...]
            out_ref[pl.ds(below + half, half)] = pieces[2 * distance - 1][...]
        else:
            out_ref[pl.ds(below, size)] = pieces[2 * distance - 2][...]
            out_ref[pl.ds(above, size)] = pieces[2 * distance - 1][...]


def across_kernel(at_ref, across_ref, own_ref, *refs):
    *pieces, plane_ref, low_ref, high_ref = refs
    place_pieces(plane_ref, lax.rem(at_ref[0], NZ), own_ref, pieces, NZ, NB)
    for b, out_ref in enumerate((low_ref, high_ref)):
        for j in range(FARS):
            out_ref[j] = plane_ref[lax.rem(across_ref[b, j], PLANE)]


def pick_across(at, across, own, pieces):
    half = jax.ShapeDtypeStruct((FARS, BLK, 2 * DH), BF16)
    return pl.pallas_call(
        across_kernel,
        out_shape=(jax.ShapeDtypeStruct((PLANE, BLK, 2 * DH), BF16), half, half),
        in_specs=[SMEM] * 2 + [VMEM] * (1 + len(pieces)),
        out_specs=(VMEM,) * 3,
        compiler_params=params(8),
        name="pick_across",
    )(at, across, own, *pieces)


def pick_kernel(at_ref, above_ref, below_ref, plane_ref, low_ref, high_ref, up_ref, down_ref):
    x_at = lax.div(at_ref[0], NZ)
    for list_ref, arrived_ref, behind, passed, out_ref in (
        (above_ref, low_ref, lax.rem(x_at + NX - 1, NX), 0, up_ref),
        (below_ref, high_ref, lax.rem(x_at + 1, NX), 1, down_ref),
    ):
        for b in range(NB):
            for j in range(FARS):
                listed = list_ref[b, j]
                slot = b * FARS + j
                if b == passed:
                    passes = lax.div(listed, PLANE) == behind

                    @pl.when(passes)
                    def _():
                        out_ref[slot] = arrived_ref[j]

                    @pl.when(jnp.logical_not(passes))
                    def _():
                        out_ref[slot] = plane_ref[lax.rem(listed, PLANE)]
                else:
                    out_ref[slot] = plane_ref[lax.rem(listed, PLANE)]


def pick(at, above, below, plane, low, high):
    out = jax.ShapeDtypeStruct((SLOTS, BLK, 2 * DH), BF16)
    return pl.pallas_call(
        pick_kernel,
        out_shape=(out, out),
        in_specs=[SMEM] * 3 + [VMEM] * 3,
        out_specs=(VMEM, VMEM),
        compiler_params=params(8),
        name="pick_far",
    )(at, above, below, plane, low, high)


def attend_kernel(
    at_ref, far_ref, count_ref, q_ref, g_ref, prev_ref, own_ref, plane_ref, below_ref, above_ref,
    qg_ref, win_ref, farg_ref, k_ref, v_ref, kt_ref, acc_ref, tri_ref, got_ref, sems,
):
    places = []
    for slot in range(SLOTS):
        listed = far_ref[slot // FARS, slot % FARS]
        steps = lax.rem(lax.div(listed, PLANE) + (NX - lax.div(at_ref[0], NZ)), NX)
        upward = (steps == NX - 1) | (steps == 2) if slot < FARS else steps == NX - 1
        places.append((steps == 0, lax.rem(listed, PLANE)))
        for here, source in (
            (upward, below_ref),
            (jnp.logical_not(upward | (steps == 0)), above_ref),
        ):

            @pl.when(here)
            def _():
                pltpu.make_async_copy(source.at[slot], got_ref.at[slot], sems.at[slot]).start()

    win_ref[...] = jnp.zeros_like(win_ref)
    key_at = lax.broadcasted_iota(jnp.int32, (BLK, 2 * BLK), 0)
    query_at = lax.broadcasted_iota(jnp.int32, (BLK, 2 * BLK), 1) % BLK
    tri_ref[...] = jnp.where(key_at <= query_at, 0.0, NEG)

    def block(b, carry):
        index = at_ref[0] * NB + b
        for w in range(WIN):
            local = b + w
            both = jnp.where(local < NB, prev_ref[lax.rem(local, NB)], own_ref[lax.rem(local, NB)])
            k_ref[w * BLK : (w + 1) * BLK, :] = both[:, :DH]
            v_ref[w * BLK : (w + 1) * BLK, :] = both[:, DH:]
        for j in range(FARS):
            slot = b * FARS + j
            mine, row = places[slot]

            @pl.when(mine)
            def _():
                got_ref[slot] = plane_ref[row]

            @pl.when(jnp.logical_not(mine))
            def _():
                pltpu.make_async_copy(below_ref.at[slot], got_ref.at[slot], sems.at[slot]).wait()

            both = got_ref[slot]
            k_ref[(WIN + j) * BLK : (WIN + j + 1) * BLK, :] = both[:, :DH]
            v_ref[(WIN + j) * BLK : (WIN + j + 1) * BLK, :] = both[:, DH:]
        kt_ref[...] = k_ref[...].astype(F32).T.astype(BF16)
        acc_ref[...] = jnp.zeros_like(acc_ref)
        biases = [
            jnp.where(index >= 2, 0.0, NEG).astype(F32),
            jnp.where(index >= 1, 0.0, NEG).astype(F32),
            None,
        ] + [jnp.where(j < count_ref[b], 0.0, NEG).astype(F32) for j in range(FARS)]
        rows = pl.ds(pl.multiple_of(b * BLK, BLK), BLK)
        for pair in range(GQ // 2):
            lo = pair * 2 * DH
            q2 = jnp.concatenate([q_ref[rows, lo : lo + DH], q_ref[rows, lo + DH : lo + 2 * DH]])
            g2 = jnp.concatenate([g_ref[rows, lo : lo + DH], g_ref[rows, lo + DH : lo + 2 * DH]])
            scores = lax.dot_general(k_ref[...], q2, NT, preferred_element_type=F32)
            parts = [scores[c * BLK : (c + 1) * BLK, :] for c in range(WIN + FARS)]
            parts[WIN - 1] = parts[WIN - 1] + tri_ref[...]
            tops = [
                jnp.max(part, axis=0, keepdims=True) + (0.0 if bias is None else bias)
                for part, bias in zip(parts, biases)
            ]
            top = functools.reduce(jnp.maximum, tops)
            expo = jnp.concatenate(
                [
                    jnp.exp2((part - (top if bias is None else top - bias)) * EXP2_SCALE)
                    for part, bias in zip(parts, biases)
                ]
            )
            inv = 1.0 / jnp.sum(expo, axis=0, keepdims=True)
            soft = expo * inv
            grad_p = lax.dot_general(v_ref[...], g2, NT, preferred_element_type=F32)
            delta = jnp.sum(soft * grad_p, axis=0, keepdims=True)
            soft_b = soft.astype(BF16)
            grad_s = (soft * (grad_p - delta)).astype(BF16)
            acc_ref[:, :DH] += jnp.dot(grad_s, q2, preferred_element_type=F32)
            acc_ref[:, DH:] += jnp.dot(soft_b, g2, preferred_element_type=F32)
            grad_q = jnp.dot(kt_ref[...], grad_s, preferred_element_type=F32).T * SCALE
            qg_ref[rows, lo : lo + DH] = grad_q[:BLK].astype(BF16)
            qg_ref[rows, lo + DH : lo + 2 * DH] = grad_q[BLK:].astype(BF16)
        acc_ref[:, :DH] = acc_ref[:, :DH] * SCALE
        window = pl.ds(pl.multiple_of(b * BLK, BLK), WIN * BLK)
        win_ref[window, :] += acc_ref[: WIN * BLK, :]
        for j in range(FARS):
            farg_ref[b * FARS + j] = acc_ref[(WIN + j) * BLK : (WIN + j + 1) * BLK, :].astype(BF16)
        return carry

    for b in range(NB):
        block(b, 0)


def attend(at, far, count, queries, out_grad, prev, own, plane, below, above):
    keys = (WIN + FARS) * BLK
    return pl.pallas_call(
        attend_kernel,
        out_shape=(
            jax.ShapeDtypeStruct((NB * BLK, GQ * DH), BF16),
            jax.ShapeDtypeStruct((2 * NB * BLK, 2 * DH), F32),
            jax.ShapeDtypeStruct((SLOTS, BLK, 2 * DH), BF16),
        ),
        in_specs=[SMEM, SMEM, SMEM] + [VMEM] * 5 + [HBM] * 2,
        out_specs=(VMEM, VMEM, VMEM),
        scratch_shapes=[
            pltpu.VMEM((keys, DH), BF16),
            pltpu.VMEM((keys, DH), BF16),
            pltpu.VMEM((DH, keys), BF16),
            pltpu.VMEM((keys, 2 * DH), F32),
            pltpu.VMEM((BLK, 2 * BLK), F32),
            pltpu.VMEM((SLOTS, BLK, 2 * DH), BF16),
            pltpu.SemaphoreType.DMA((SLOTS,)),
        ],
        compiler_params=params(24),
        cost_estimate=pl.CostEstimate(flops=2_400_000_000 * 4, bytes_accessed=6 << 20, transcendentals=2_000_000),
        name="attend",
    )(at, far, count, queries, out_grad, prev, own, plane, below, above)


def spread_kernel(at_ref, *refs):
    lists, pieces = refs[:NX], refs[NX:-2]
    out_ref, acc_ref = refs[-2:]
    mine, below, above, across_low, across_high = pieces
    x_at = lax.div(at_ref[0], NZ)
    acc_ref[...] = jnp.zeros_like(acc_ref)

    def add(listed, term_ref, j):
        @pl.when(lax.div(listed, PLANE) == x_at)
        def _():
            acc_ref[lax.rem(listed, PLANE)] += term_ref[j].astype(F32)

    half = SLOTS // 2
    for j in range(SLOTS):
        add(lists[0][j // FARS, j % FARS], mine, j)
        add(lists[1][j // FARS, j % FARS], above, j)
        add(lists[2][j // FARS, j % FARS], across_low if j < half else across_high, j % half)
        add(lists[3][j // FARS, j % FARS], below, j)
    out_ref[...] = acc_ref[...].astype(BF16)


def spread(at, lists, own, pieces):
    return pl.pallas_call(
        spread_kernel,
        out_shape=jax.ShapeDtypeStruct((PLANE, BLK, 2 * DH), BF16),
        in_specs=[SMEM] * (1 + NX) + [VMEM] * (1 + len(pieces)),
        out_specs=VMEM,
        scratch_shapes=[pltpu.VMEM((PLANE, BLK, 2 * DH), F32)],
        compiler_params=params(16),
        name="spread_far",
    )(at, *lists, own, *pieces)


def finish_kernel(terms_ref, back_ref, window_ref, out_ref):
    total = window_ref[NB * BLK :, :] + back_ref[...].astype(F32)
    for z in range(NZ):
        total += terms_ref[z].astype(F32)
    source = lax.broadcasted_iota(jnp.int32, (2 * DH, 2 * DH), 0)
    target = lax.broadcasted_iota(jnp.int32, (2 * DH, 2 * DH), 1)
    part, rest = target // (2 * PART), target % (2 * PART)
    wanted = (rest // PART) * DH + part * PART + rest % PART
    order = jnp.where(source == wanted, 1.0, 0.0).astype(BF16)
    out_ref[...] = jnp.dot(
        total.astype(BF16), order, preferred_element_type=F32
    ).astype(BF16)


def finish(terms, back, window):
    return pl.pallas_call(
        finish_kernel,
        out_shape=jax.ShapeDtypeStruct((NB * BLK, 2 * DH), BF16),
        in_specs=[VMEM] * 3,
        out_specs=VMEM,
        compiler_params=params(12),
        name="finish_kv",
    )(terms, back, window)


def heads_kernel(at_ref, own_ref, *refs):
    *pieces, other_ref, out_ref = refs
    at, core = lax.div(at_ref[0], 2), lax.rem(at_ref[0], 2)
    rows = NB * BLK
    half = rows // 2
    below, above = lax.rem(at + NY - 1, NY), lax.rem(at + 1, NY)
    across = lax.rem(at + 2, NY)
    starts = (0, rows, 2 * rows, 3 * rows, 3 * rows + half)
    for k, (y, low, high) in enumerate(
        ((at, 0, rows), (below, 0, rows), (above, 0, rows), (across, 0, half), (across, half, rows))
    ):
        mine = own_ref if k == 0 else pieces[k - 1]
        out_ref[2 * y + core, low:high, :] = mine[...]
        out_ref[2 * y + 1 - core, low:high, :] = other_ref[starts[k] : starts[k] + high - low, :]


def place_heads(at, own, pieces, other):
    return pl.pallas_call(
        heads_kernel,
        out_shape=jax.ShapeDtypeStruct((2 * NY, *own.shape), BF16),
        in_specs=[SMEM] + [VMEM] * (2 + len(pieces)),
        out_specs=VMEM,
        compiler_params=params(8),
        name="place_heads",
    )(at, own, *pieces, other)


def weights_kernel(grad_ref, inputs_ref, out_ref, quarters_ref, sems):
    wide = quarters_ref.shape[2]
    copies = [
        pltpu.make_async_copy(
            inputs_ref.at[:, pl.ds(quarter * wide, wide)], quarters_ref.at[quarter], sems.at[quarter]
        )
        for quarter in range(4)
    ]
    for copy in copies:
        copy.start()
    grads = [jnp.concatenate([grad_ref[x * 2 + head] for x in range(NX)]) for head in range(2)]
    for quarter in range(4):
        copies[quarter].wait()
        rows = slice(quarter * 2 * PART, (quarter + 1) * 2 * PART)
        for head in range(2):
            term = lax.dot_general(
                grads[head],
                quarters_ref[quarter],
                (((0,), (0,)), ((), ())),
                preferred_element_type=F32,
            ).astype(BF16)
            for part in range(4):
                out_ref[head * 4 + part, rows, :] = term[part * 2 * PART : (part + 1) * 2 * PART]


def weight_terms(grad, inputs_x):
    tokens, rows = inputs_x.shape
    return pl.pallas_call(
        weights_kernel,
        out_shape=jax.ShapeDtypeStruct((NZ, 4 * 2 * PART, rows // 4), BF16),
        in_specs=[VMEM, HBM],
        out_specs=VMEM,
        scratch_shapes=[
            pltpu.VMEM((4, tokens, rows // 4), BF16),
            pltpu.SemaphoreType.DMA((4,)),
        ],
        compiler_params=params(16),
        cost_estimate=pl.CostEstimate(flops=1 << 30, bytes_accessed=4 << 20, transcendentals=0),
        name="weight_terms",
    )(grad, inputs_x)


def weight_sum_kernel(terms_ref, key_ref, value_ref):
    total = terms_ref[0].astype(F32)
    for z in range(1, NZ):
        total += terms_ref[z].astype(F32)
    wide = total.shape[1]
    for quarter in range(4):
        low = quarter * 2 * PART
        key_ref[:, quarter * wide : (quarter + 1) * wide] = total[low : low + PART]
        value_ref[:, quarter * wide : (quarter + 1) * wide] = total[low + PART : low + 2 * PART]


def weight_sum(terms):
    out = jax.ShapeDtypeStruct((PART, 4 * terms.shape[2]), F32)
    return pl.pallas_call(
        weight_sum_kernel,
        out_shape=(out, out),
        in_specs=[VMEM],
        out_specs=(VMEM, VMEM),
        compiler_params=params(8),
        name="weight_sum",
    )(terms)


def input_kernel(at_ref, grad_ref, weights_ref, mine_ref, above_ref, low_ref, high_ref, below_ref):
    x_at = lax.div(at_ref[0], NZ)
    half = low_ref.shape[0]
    for steps in range(NX):
        x = lax.rem(x_at + steps, NX)
        grad = jnp.concatenate([grad_ref[2 * x], grad_ref[2 * x + 1]], axis=1)
        term = jnp.dot(grad, weights_ref[...], preferred_element_type=F32)
        if steps == 2:
            low_ref[...] = term[:half].astype(BF16)
            high_ref[...] = term[half:].astype(BF16)
        else:
            out_ref = (mine_ref, above_ref, None, below_ref)[steps]
            out_ref[...] = term.astype(out_ref.dtype)


def input_terms(at, grad, weights):
    rows, wide = grad.shape[1], weights.shape[1]
    send, half = (jax.ShapeDtypeStruct((size, wide), BF16) for size in (rows, rows // 2))
    return pl.pallas_call(
        input_kernel,
        out_shape=(jax.ShapeDtypeStruct((rows, wide), F32), send, half, half, send),
        in_specs=[SMEM, VMEM, VMEM],
        out_specs=(VMEM,) * 5,
        compiler_params=params(16),
        cost_estimate=pl.CostEstimate(flops=1 << 30, bytes_accessed=4 << 20, transcendentals=0),
        name="input_terms",
    )(at, grad, weights)


def added(term, arrived, low):
    high = low + arrived.shape[0]
    rows = (term[low:high].astype(F32) + arrived.astype(F32)).astype(BF16)
    return jnp.concatenate([term[:low], rows, term[high:]])


def local(
    queries, key_rows, value_rows, out_grad, inputs, key_weight, value_weight, far_blocks, far_count
):
    tokens = queries.shape[0]
    seq_index = lax.axis_index("seq").astype(jnp.int32)
    at = seq_index.reshape(1)
    own_index = lax.axis_index("own").astype(jnp.int32).reshape(1)
    own_kv = jnp.concatenate([key_rows, value_rows], axis=1).reshape(NB, BLK, 2 * DH)

    inputs_x = lax.all_gather(inputs, "seq", axis=0, axis_index_groups=X_GROUPS, tiled=True)

    from_below, from_above = both_ways(own_kv, own_kv, "seq", Z_UP)
    across = [(x * NZ + z, (x + 2) % NX * NZ + z) for x in range(NX) for z in range(NZ)]
    list_across = lax.ppermute(far_blocks, "seq", across)
    from_below, from_above, list_across, listed = lax.optimization_barrier(
        (from_below, from_above, list_across, far_blocks)
    )
    plane = [from_below, from_above]
    for distance in range(2, NZ // 2 + 1):
        if distance == NZ // 2:
            from_below, from_above = from_below[: NB // 2], from_above[NB // 2 :]
        from_below, from_above = both_ways(from_below, from_above, "seq", Z_UP)
        plane += [from_below, from_above]
    from_below, key_weight, value_weight = lax.optimization_barrier(
        (plane[0], key_weight, value_weight)
    )
    plane[0] = from_below
    weights = jnp.concatenate([key_weight.T, value_weight.T])
    weights = lax.all_gather(weights, "seq", axis=0, axis_index_groups=Z_GROUPS, tiled=True)
    prev_kv = shifted(own_kv, "seq", 1)
    plane, low, high = pick_across(at, list_across, own_kv, plane)
    low, high, listed = lax.optimization_barrier((low, high, listed))
    low, high = both_ways(low, high, "seq", X_UP)
    list_below, list_above = both_ways(listed, listed, "seq", X_UP)
    up, down = pick(at, list_above, list_below, plane, low, high)
    from_below, from_above = both_ways(up, down, "seq", X_UP)

    far_count, inputs_x = lax.optimization_barrier((far_count, inputs_x))
    query_grad, window, far_grad = attend(
        at, far_blocks, far_count, queries, out_grad, prev_kv, own_kv, plane, from_below, from_above
    )
    far_all = ring_gather(far_grad, "seq", X_UP, NX)
    back = shifted(window[:tokens].astype(BF16), "seq", -1)
    list_above, weights = lax.optimization_barrier((list_above, weights))
    lists = (far_blocks, list_above, list_across, list_below)
    dense = spread(at, lists, far_grad, far_all)
    dense = dense.reshape(NZ, tokens, 2 * DH)
    terms = lax.all_to_all(dense, "seq", 0, 0, axis_index_groups=Z_GROUPS, tiled=True)
    kv_grad = finish(terms, back, window)

    moved = lax.ppermute(kv_grad, ("seq", "own"), SWAP_XY)
    same_core = ring_gather(moved, "own", Y_UP, NY)
    other_core = lax.ppermute(jnp.concatenate([moved, *same_core]), "own", CORES)
    heads = place_heads(own_index, moved, same_core, other_core)

    mine, above, low, high, below = input_terms(at, heads, weights)
    from_below, from_above = both_ways(low, high, "seq", X_UP)
    pieces = weight_terms(heads, inputs_x)
    pieces = lax.all_to_all(pieces, "seq", 0, 0, axis_index_groups=Z_GROUPS, tiled=True)
    above, below = added(above, from_below, 0), added(below, from_above, tokens // 2)
    from_below, from_above = both_ways(above, below, "seq", X_UP)
    input_grad = mine + from_below.astype(F32) + from_above.astype(F32)
    key_weight_grad, value_weight_grad = weight_sum(pieces)
    return (query_grad, input_grad.astype(BF16), key_weight_grad.T, value_weight_grad.T)


def solution(mesh):
    return jax.shard_map(
        local,
        mesh=mesh,
        in_specs=(
            P("seq", "own"),
            P("seq", "own"),
            P("seq", "own"),
            P("seq", "own"),
            P("seq", "own"),
            P("own", "seq"),
            P("own", "seq"),
            P("seq", None),
            P("seq"),
        ),
        out_specs=(P("seq", "own"), P("seq", "own"), P("own", "seq"), P("own", "seq")),
        check_vma=False,
    )
```

```python
import functools
import math

import jax
import jax.numpy as jnp
from jax import lax
from jax.experimental import pallas as pl
from jax.experimental.pallas import tpu as pltpu
from jax.sharding import PartitionSpec as P

DH = 128
GQ = 8
BLK = 128
WIN = 3
FARS = 4
NX = 4
NZ = 8
NB = 2
PLANE = NB * NZ
SLOTS = NB * FARS
X_GROUPS = [[x * NZ + z for x in range(NX)] for z in range(NZ)]
Z_GROUPS = [[x * NZ + z for z in range(NZ)] for x in range(NX)]
Z_UP = [(x * NZ + z, x * NZ + (z + 1) % NZ) for x in range(NX) for z in range(NZ)]
X_UP = [(x * NZ + z, (x + 1) % NX * NZ + z) for x in range(NX) for z in range(NZ)]
NY = 4
Y_UP = [(2 * y + core, 2 * ((y + 1) % NY) + core) for y in range(NY) for core in range(2)]
CORES = [(own, own ^ 1) for own in range(2 * NY)]
SWAP_XY = [
    (((x * NZ + z) * NY + y) * 2 + core, ((y * NZ + z) * NY + x) * 2 + core)
    for x in range(NX)
    for z in range(NZ)
    for y in range(NY)
    for core in range(2)
]
PART = DH // 4
SCALE = 1.0 / math.sqrt(DH)
EXP2_SCALE = SCALE * math.log2(math.e)
NEG = -1e30

SMEM = pl.BlockSpec(memory_space=pltpu.SMEM)
VMEM = pl.BlockSpec(memory_space=pltpu.VMEM)
HBM = pl.BlockSpec(memory_space=pltpu.HBM)
NT = (((1,), (1,)), ((), ()))
F32 = jnp.float32
BF16 = jnp.bfloat16


def params(mib):
    return pltpu.CompilerParams(vmem_limit_bytes=mib << 20)


def shifted(value, axis, steps):
    count = lax.axis_size(axis)
    leading, last = (max(0, -steps), min(count, count - steps))
    return lax.ppermute(value, axis, [(source, source + steps) for source in range(leading, last)])


def both_ways(upward, downward, axis, pairs):
    back = [(target, source) for source, target in pairs]
    return lax.ppermute(upward, axis, pairs), lax.ppermute(downward, axis, back)


def ring_gather(value, axis, pairs, count):
    half = value.shape[0] // 2
    from_below, from_above = value, value
    pieces = []
    for distance in range(1, count // 2 + 1):
        if distance == count // 2:
            from_below, from_above = from_below[:half], from_above[half:]
        from_below, from_above = both_ways(from_below, from_above, axis, pairs)
        pieces += [from_below, from_above]
    return pieces


def place_pieces(out_ref, at, own_ref, pieces, count, size):
    half = size // 2
    out_ref[pl.ds(at * size, size)] = own_ref[...]
    for distance in range(1, count // 2 + 1):
        below = lax.rem(at + (count - distance), count) * size
        above = lax.rem(at + distance, count) * size
        if distance == count // 2:
            out_ref[pl.ds(below, half)] = pieces[2 * distance - 2][...]
            out_ref[pl.ds(below + half, half)] = pieces[2 * distance - 1][...]
        else:
            out_ref[pl.ds(below, size)] = pieces[2 * distance - 2][...]
            out_ref[pl.ds(above, size)] = pieces[2 * distance - 1][...]


def across_kernel(at_ref, across_ref, own_ref, *refs):
    *pieces, plane_ref, low_ref, high_ref = refs
    place_pieces(plane_ref, lax.rem(at_ref[0], NZ), own_ref, pieces, NZ, NB)
    for b, out_ref in enumerate((low_ref, high_ref)):
        for j in range(FARS):
            out_ref[j] = plane_ref[lax.rem(across_ref[b, j], PLANE)]


def pick_across(at, across, own, pieces):
    half = jax.ShapeDtypeStruct((FARS, BLK, 2 * DH), BF16)
    return pl.pallas_call(
        across_kernel,
        out_shape=(jax.ShapeDtypeStruct((PLANE, BLK, 2 * DH), BF16), half, half),
        in_specs=[SMEM] * 2 + [VMEM] * (1 + len(pieces)),
        out_specs=(VMEM,) * 3,
        compiler_params=params(8),
        name="pick_across",
    )(at, across, own, *pieces)


def pick_kernel(at_ref, above_ref, below_ref, plane_ref, low_ref, high_ref, up_ref, down_ref):
    x_at = lax.div(at_ref[0], NZ)
    for list_ref, arrived_ref, behind, passed, out_ref in (
        (above_ref, low_ref, lax.rem(x_at + NX - 1, NX), 0, up_ref),
        (below_ref, high_ref, lax.rem(x_at + 1, NX), 1, down_ref),
    ):
        for b in range(NB):
            for j in range(FARS):
                listed = list_ref[b, j]
                slot = b * FARS + j
                if b == passed:
                    passes = lax.div(listed, PLANE) == behind

                    @pl.when(passes)
                    def _():
                        out_ref[slot] = arrived_ref[j]

                    @pl.when(jnp.logical_not(passes))
                    def _():
                        out_ref[slot] = plane_ref[lax.rem(listed, PLANE)]
                else:
                    out_ref[slot] = plane_ref[lax.rem(listed, PLANE)]


def pick(at, above, below, plane, low, high):
    out = jax.ShapeDtypeStruct((SLOTS, BLK, 2 * DH), BF16)
    return pl.pallas_call(
        pick_kernel,
        out_shape=(out, out),
        in_specs=[SMEM] * 3 + [VMEM] * 3,
        out_specs=(VMEM, VMEM),
        compiler_params=params(8),
        name="pick_far",
    )(at, above, below, plane, low, high)


def attend_kernel(
    at_ref, far_ref, count_ref, q_ref, g_ref, prev_ref, own_ref, plane_ref, below_ref, above_ref,
    qg_ref, win_ref, farg_ref, k_ref, v_ref, kt_ref, acc_ref, tri_ref,
):
    win_ref[...] = jnp.zeros_like(win_ref)
    key_at = lax.broadcasted_iota(jnp.int32, (BLK, 2 * BLK), 0)
    query_at = lax.broadcasted_iota(jnp.int32, (BLK, 2 * BLK), 1) % BLK
    tri_ref[...] = jnp.where(key_at <= query_at, 0.0, NEG)

    def block(b, carry):
        index = at_ref[0] * NB + b
        for w in range(WIN):
            local = b + w
            both = jnp.where(local < NB, prev_ref[lax.rem(local, NB)], own_ref[lax.rem(local, NB)])
            k_ref[w * BLK : (w + 1) * BLK, :] = both[:, :DH]
            v_ref[w * BLK : (w + 1) * BLK, :] = both[:, DH:]
        for j in range(FARS):
            slot = b * FARS + j
            steps = lax.rem(lax.div(far_ref[b, j], PLANE) + (NX - lax.div(at_ref[0], NZ)), NX)
            mine = plane_ref[lax.rem(far_ref[b, j], PLANE)]
            from_below = (steps == NX - 1) | ((steps == 2) & (b == 0))
            both = jnp.where(from_below, below_ref[slot], above_ref[slot])
            both = jnp.where(steps == 0, mine, both)
            k_ref[(WIN + j) * BLK : (WIN + j + 1) * BLK, :] = both[:, :DH]
            v_ref[(WIN + j) * BLK : (WIN + j + 1) * BLK, :] = both[:, DH:]
        kt_ref[...] = k_ref[...].astype(F32).T.astype(BF16)
        acc_ref[...] = jnp.zeros_like(acc_ref)
        biases = [
            jnp.where(index >= 2, 0.0, NEG).astype(F32),
            jnp.where(index >= 1, 0.0, NEG).astype(F32),
            None,
        ] + [jnp.where(j < count_ref[b], 0.0, NEG).astype(F32) for j in range(FARS)]
        rows = pl.ds(pl.multiple_of(b * BLK, BLK), BLK)
        for pair in range(GQ // 2):
            lo = pair * 2 * DH
            q2 = jnp.concatenate([q_ref[rows, lo : lo + DH], q_ref[rows, lo + DH : lo + 2 * DH]])
            g2 = jnp.concatenate([g_ref[rows, lo : lo + DH], g_ref[rows, lo + DH : lo + 2 * DH]])
            scores = lax.dot_general(k_ref[...], q2, NT, preferred_element_type=F32)
            parts = [scores[c * BLK : (c + 1) * BLK, :] for c in range(WIN + FARS)]
            parts[WIN - 1] = parts[WIN - 1] + tri_ref[...]
            tops = [
                jnp.max(part, axis=0, keepdims=True) + (0.0 if bias is None else bias)
                for part, bias in zip(parts, biases)
            ]
            top = functools.reduce(jnp.maximum, tops)
            expo = jnp.concatenate(
                [
                    jnp.exp2((part - (top if bias is None else top - bias)) * EXP2_SCALE)
                    for part, bias in zip(parts, biases)
                ]
            )
            inv = 1.0 / jnp.sum(expo, axis=0, keepdims=True)
            soft = expo * inv
            grad_p = lax.dot_general(v_ref[...], g2, NT, preferred_element_type=F32)
            delta = jnp.sum(soft * grad_p, axis=0, keepdims=True)
            soft_b = soft.astype(BF16)
            grad_s = (soft * (grad_p - delta)).astype(BF16)
            acc_ref[:, :DH] += jnp.dot(grad_s, q2, preferred_element_type=F32)
            acc_ref[:, DH:] += jnp.dot(soft_b, g2, preferred_element_type=F32)
            grad_q = jnp.dot(kt_ref[...], grad_s, preferred_element_type=F32).T * SCALE
            qg_ref[rows, lo : lo + DH] = grad_q[:BLK].astype(BF16)
            qg_ref[rows, lo + DH : lo + 2 * DH] = grad_q[BLK:].astype(BF16)
        acc_ref[:, :DH] = acc_ref[:, :DH] * SCALE
        window = pl.ds(pl.multiple_of(b * BLK, BLK), WIN * BLK)
        win_ref[window, :] += acc_ref[: WIN * BLK, :]
        for j in range(FARS):
            farg_ref[b * FARS + j] = acc_ref[(WIN + j) * BLK : (WIN + j + 1) * BLK, :].astype(BF16)
        return carry

    for b in range(NB):
        block(b, 0)


def attend(at, far, count, queries, out_grad, prev, own, plane, below, above):
    keys = (WIN + FARS) * BLK
    return pl.pallas_call(
        attend_kernel,
        out_shape=(
            jax.ShapeDtypeStruct((NB * BLK, GQ * DH), BF16),
            jax.ShapeDtypeStruct((2 * NB * BLK, 2 * DH), F32),
            jax.ShapeDtypeStruct((SLOTS, BLK, 2 * DH), BF16),
        ),
        in_specs=[SMEM, SMEM, SMEM] + [VMEM] * 7,
        out_specs=(VMEM, VMEM, VMEM),
        scratch_shapes=[
            pltpu.VMEM((keys, DH), BF16),
            pltpu.VMEM((keys, DH), BF16),
            pltpu.VMEM((DH, keys), BF16),
            pltpu.VMEM((keys, 2 * DH), F32),
            pltpu.VMEM((BLK, 2 * BLK), F32),
        ],
        compiler_params=params(24),
        cost_estimate=pl.CostEstimate(flops=2_400_000_000 * 4, bytes_accessed=6 << 20, transcendentals=2_000_000),
        name="attend",
    )(at, far, count, queries, out_grad, prev, own, plane, below, above)


def spread_kernel(at_ref, *refs):
    lists, pieces = refs[:NX], refs[NX:-2]
    out_ref, acc_ref = refs[-2:]
    mine, below, above, across_low, across_high = pieces
    x_at = lax.div(at_ref[0], NZ)
    acc_ref[...] = jnp.zeros_like(acc_ref)

    def add(listed, term_ref, j):
        @pl.when(lax.div(listed, PLANE) == x_at)
        def _():
            acc_ref[lax.rem(listed, PLANE)] += term_ref[j].astype(F32)

    half = SLOTS // 2
    for j in range(SLOTS):
        add(lists[0][j // FARS, j % FARS], mine, j)
        add(lists[1][j // FARS, j % FARS], above, j)
        add(lists[2][j // FARS, j % FARS], across_low if j < half else across_high, j % half)
        add(lists[3][j // FARS, j % FARS], below, j)
    out_ref[...] = acc_ref[...].astype(BF16)


def spread(at, lists, own, pieces):
    return pl.pallas_call(
        spread_kernel,
        out_shape=jax.ShapeDtypeStruct((PLANE, BLK, 2 * DH), BF16),
        in_specs=[SMEM] * (1 + NX) + [VMEM] * (1 + len(pieces)),
        out_specs=VMEM,
        scratch_shapes=[pltpu.VMEM((PLANE, BLK, 2 * DH), F32)],
        compiler_params=params(16),
        name="spread_far",
    )(at, *lists, own, *pieces)


def finish_kernel(terms_ref, back_ref, window_ref, out_ref):
    total = window_ref[NB * BLK :, :] + back_ref[...].astype(F32)
    for z in range(NZ):
        total += terms_ref[z].astype(F32)
    source = lax.broadcasted_iota(jnp.int32, (2 * DH, 2 * DH), 0)
    target = lax.broadcasted_iota(jnp.int32, (2 * DH, 2 * DH), 1)
    part, rest = target // (2 * PART), target % (2 * PART)
    wanted = (rest // PART) * DH + part * PART + rest % PART
    order = jnp.where(source == wanted, 1.0, 0.0).astype(BF16)
    out_ref[...] = jnp.dot(
        total.astype(BF16), order, preferred_element_type=F32
    ).astype(BF16)


def finish(terms, back, window):
    return pl.pallas_call(
        finish_kernel,
        out_shape=jax.ShapeDtypeStruct((NB * BLK, 2 * DH), BF16),
        in_specs=[VMEM] * 3,
        out_specs=VMEM,
        compiler_params=params(12),
        name="finish_kv",
    )(terms, back, window)


def heads_kernel(at_ref, own_ref, *refs):
    *pieces, other_ref, out_ref = refs
    at, core = lax.div(at_ref[0], 2), lax.rem(at_ref[0], 2)
    rows = NB * BLK
    half = rows // 2
    below, above = lax.rem(at + NY - 1, NY), lax.rem(at + 1, NY)
    across = lax.rem(at + 2, NY)
    starts = (0, rows, 2 * rows, 3 * rows, 3 * rows + half)
    for k, (y, low, high) in enumerate(
        ((at, 0, rows), (below, 0, rows), (above, 0, rows), (across, 0, half), (across, half, rows))
    ):
        mine = own_ref if k == 0 else pieces[k - 1]
        out_ref[2 * y + core, low:high, :] = mine[...]
        out_ref[2 * y + 1 - core, low:high, :] = other_ref[starts[k] : starts[k] + high - low, :]


def place_heads(at, own, pieces, other):
    return pl.pallas_call(
        heads_kernel,
        out_shape=jax.ShapeDtypeStruct((2 * NY, *own.shape), BF16),
        in_specs=[SMEM] + [VMEM] * (2 + len(pieces)),
        out_specs=VMEM,
        compiler_params=params(8),
        name="place_heads",
    )(at, own, *pieces, other)


def weights_kernel(grad_ref, inputs_ref, out_ref, quarters_ref, sems):
    wide = quarters_ref.shape[2]
    copies = [
        pltpu.make_async_copy(
            inputs_ref.at[:, pl.ds(quarter * wide, wide)], quarters_ref.at[quarter], sems.at[quarter]
        )
        for quarter in range(4)
    ]
    for copy in copies:
        copy.start()
    grads = [jnp.concatenate([grad_ref[x * 2 + head] for x in range(NX)]) for head in range(2)]
    for quarter in range(4):
        copies[quarter].wait()
        rows = slice(quarter * 2 * PART, (quarter + 1) * 2 * PART)
        for head in range(2):
            term = lax.dot_general(
                grads[head],
                quarters_ref[quarter],
                (((0,), (0,)), ((), ())),
                preferred_element_type=F32,
            ).astype(BF16)
            for part in range(4):
                out_ref[head * 4 + part, rows, :] = term[part * 2 * PART : (part + 1) * 2 * PART]


def weight_terms(grad, inputs_x):
    tokens, rows = inputs_x.shape
    return pl.pallas_call(
        weights_kernel,
        out_shape=jax.ShapeDtypeStruct((NZ, 4 * 2 * PART, rows // 4), BF16),
        in_specs=[VMEM, HBM],
        out_specs=VMEM,
        scratch_shapes=[
            pltpu.VMEM((4, tokens, rows // 4), BF16),
            pltpu.SemaphoreType.DMA((4,)),
        ],
        compiler_params=params(16),
        cost_estimate=pl.CostEstimate(flops=1 << 30, bytes_accessed=4 << 20, transcendentals=0),
        name="weight_terms",
    )(grad, inputs_x)


def weight_sum_kernel(terms_ref, key_ref, value_ref):
    total = terms_ref[0].astype(F32)
    for z in range(1, NZ):
        total += terms_ref[z].astype(F32)
    wide = total.shape[1]
    for quarter in range(4):
        low = quarter * 2 * PART
        key_ref[:, quarter * wide : (quarter + 1) * wide] = total[low : low + PART]
        value_ref[:, quarter * wide : (quarter + 1) * wide] = total[low + PART : low + 2 * PART]


def weight_sum(terms):
    out = jax.ShapeDtypeStruct((PART, 4 * terms.shape[2]), F32)
    return pl.pallas_call(
        weight_sum_kernel,
        out_shape=(out, out),
        in_specs=[VMEM],
        out_specs=(VMEM, VMEM),
        compiler_params=params(8),
        name="weight_sum",
    )(terms)


def input_kernel(at_ref, grad_ref, weights_ref, mine_ref, above_ref, low_ref, high_ref, below_ref):
    x_at = lax.div(at_ref[0], NZ)
    half = low_ref.shape[0]
    for steps in range(NX):
        x = lax.rem(x_at + steps, NX)
        grad = jnp.concatenate([grad_ref[2 * x], grad_ref[2 * x + 1]], axis=1)
        term = jnp.dot(grad, weights_ref[...], preferred_element_type=F32)
        if steps == 2:
            low_ref[...] = term[:half].astype(BF16)
            high_ref[...] = term[half:].astype(BF16)
        else:
            out_ref = (mine_ref, above_ref, None, below_ref)[steps]
            out_ref[...] = term.astype(out_ref.dtype)


def input_terms(at, grad, weights):
    rows, wide = grad.shape[1], weights.shape[1]
    send, half = (jax.ShapeDtypeStruct((size, wide), BF16) for size in (rows, rows // 2))
    return pl.pallas_call(
        input_kernel,
        out_shape=(jax.ShapeDtypeStruct((rows, wide), F32), send, half, half, send),
        in_specs=[SMEM, VMEM, VMEM],
        out_specs=(VMEM,) * 5,
        compiler_params=params(16),
        cost_estimate=pl.CostEstimate(flops=1 << 30, bytes_accessed=4 << 20, transcendentals=0),
        name="input_terms",
    )(at, grad, weights)


def added(term, arrived, low):
    high = low + arrived.shape[0]
    rows = (term[low:high].astype(F32) + arrived.astype(F32)).astype(BF16)
    return jnp.concatenate([term[:low], rows, term[high:]])


def local(
    queries, key_rows, value_rows, out_grad, inputs, key_weight, value_weight, far_blocks, far_count
):
    tokens = queries.shape[0]
    seq_index = lax.axis_index("seq").astype(jnp.int32)
    at = seq_index.reshape(1)
    own_index = lax.axis_index("own").astype(jnp.int32).reshape(1)
    own_kv = jnp.concatenate([key_rows, value_rows], axis=1).reshape(NB, BLK, 2 * DH)

    from_below, from_above = both_ways(own_kv, own_kv, "seq", Z_UP)
    across = [(x * NZ + z, (x + 2) % NX * NZ + z) for x in range(NX) for z in range(NZ)]
    list_across = lax.ppermute(far_blocks, "seq", across)
    from_below, from_above, list_across, listed = lax.optimization_barrier(
        (from_below, from_above, list_across, far_blocks)
    )
    plane = [from_below, from_above]
    for distance in range(2, NZ // 2 + 1):
        if distance == NZ // 2:
            from_below, from_above = from_below[: NB // 2], from_above[NB // 2 :]
        from_below, from_above = both_ways(from_below, from_above, "seq", Z_UP)
        plane += [from_below, from_above]
    prev_kv = shifted(own_kv, "seq", 1)
    plane, low, high = pick_across(at, list_across, own_kv, plane)
    low, high, listed, key_weight, value_weight = lax.optimization_barrier(
        (low, high, listed, key_weight, value_weight)
    )
    weights = jnp.concatenate([key_weight.T, value_weight.T])
    weights = lax.all_gather(weights, "seq", axis=0, axis_index_groups=Z_GROUPS, tiled=True)
    low, high = both_ways(low, high, "seq", X_UP)
    list_below, list_above = both_ways(listed, listed, "seq", X_UP)
    up, down = pick(at, list_above, list_below, plane, low, high)
    from_below, from_above = both_ways(up, down, "seq", X_UP)

    query_grad, window, far_grad = attend(
        at, far_blocks, far_count, queries, out_grad, prev_kv, own_kv, plane, from_below, from_above
    )
    far_all = ring_gather(far_grad, "seq", X_UP, NX)
    back = shifted(window[:tokens].astype(BF16), "seq", -1)
    list_above, weights, back, inputs = lax.optimization_barrier((list_above, weights, back, inputs))
    inputs_x = lax.all_gather(inputs, "seq", axis=0, axis_index_groups=X_GROUPS, tiled=True)
    lists = (far_blocks, list_above, list_across, list_below)
    dense = spread(at, lists, far_grad, far_all)
    dense = dense.reshape(NZ, tokens, 2 * DH)
    terms = lax.all_to_all(dense, "seq", 0, 0, axis_index_groups=Z_GROUPS, tiled=True)
    kv_grad = finish(terms, back, window)

    moved = lax.ppermute(kv_grad, ("seq", "own"), SWAP_XY)
    same_core = ring_gather(moved, "own", Y_UP, NY)
    other_core = lax.ppermute(jnp.concatenate([moved, *same_core]), "own", CORES)
    heads = place_heads(own_index, moved, same_core, other_core)

    mine, above, low, high, below = input_terms(at, heads, weights)
    from_below, from_above = both_ways(low, high, "seq", X_UP)
    pieces = weight_terms(heads, inputs_x)
    pieces = lax.all_to_all(pieces, "seq", 0, 0, axis_index_groups=Z_GROUPS, tiled=True)
    above, below = added(above, from_below, 0), added(below, from_above, tokens // 2)
    from_below, from_above = both_ways(above, below, "seq", X_UP)
    input_grad = mine + from_below.astype(F32) + from_above.astype(F32)
    key_weight_grad, value_weight_grad = weight_sum(pieces)
    return (query_grad, input_grad.astype(BF16), key_weight_grad.T, value_weight_grad.T)


def solution(mesh):
    return jax.shard_map(
        local,
        mesh=mesh,
        in_specs=(
            P("seq", "own"),
            P("seq", "own"),
            P("seq", "own"),
            P("seq", "own"),
            P("seq", "own"),
            P("own", "seq"),
            P("own", "seq"),
            P("seq", None),
            P("seq"),
        ),
        out_specs=(P("seq", "own"), P("seq", "own"), P("own", "seq"), P("own", "seq")),
        check_vma=False,
    )
```

```python
import functools
import math

import jax
import jax.numpy as jnp
from jax import lax
from jax.experimental import pallas as pl
from jax.experimental.pallas import tpu as pltpu
from jax.sharding import PartitionSpec as P

DH = 128
GQ = 8
BLK = 128
WIN = 3
FARS = 4
NX = 4
NZ = 8
NB = 2
PLANE = NB * NZ
SLOTS = NB * FARS
X_GROUPS = [[x * NZ + z for x in range(NX)] for z in range(NZ)]
Z_GROUPS = [[x * NZ + z for z in range(NZ)] for x in range(NX)]
Z_UP = [(x * NZ + z, x * NZ + (z + 1) % NZ) for x in range(NX) for z in range(NZ)]
X_UP = [(x * NZ + z, (x + 1) % NX * NZ + z) for x in range(NX) for z in range(NZ)]
NY = 4
Y_UP = [(2 * y + core, 2 * ((y + 1) % NY) + core) for y in range(NY) for core in range(2)]
CORES = [(own, own ^ 1) for own in range(2 * NY)]
SWAP_XY = [
    (((x * NZ + z) * NY + y) * 2 + core, ((y * NZ + z) * NY + x) * 2 + core)
    for x in range(NX)
    for z in range(NZ)
    for y in range(NY)
    for core in range(2)
]
PART = DH // 4
SCALE = 1.0 / math.sqrt(DH)
EXP2_SCALE = SCALE * math.log2(math.e)
NEG = -1e30

SMEM = pl.BlockSpec(memory_space=pltpu.SMEM)
VMEM = pl.BlockSpec(memory_space=pltpu.VMEM)
NT = (((1,), (1,)), ((), ()))
F32 = jnp.float32
BF16 = jnp.bfloat16


def params(mib):
    return pltpu.CompilerParams(vmem_limit_bytes=mib << 20)


def shifted(value, axis, steps):
    count = lax.axis_size(axis)
    leading, last = (max(0, -steps), min(count, count - steps))
    return lax.ppermute(value, axis, [(source, source + steps) for source in range(leading, last)])


def both_ways(upward, downward, axis, pairs):
    back = [(target, source) for source, target in pairs]
    return lax.ppermute(upward, axis, pairs), lax.ppermute(downward, axis, back)


def ring_gather(value, axis, pairs, count):
    half = value.shape[0] // 2
    from_below, from_above = value, value
    pieces = []
    for distance in range(1, count // 2 + 1):
        if distance == count // 2:
            from_below, from_above = from_below[:half], from_above[half:]
        from_below, from_above = both_ways(from_below, from_above, axis, pairs)
        pieces += [from_below, from_above]
    return pieces


def place_pieces(out_ref, at, own_ref, pieces, count, size):
    half = size // 2
    out_ref[pl.ds(at * size, size)] = own_ref[...]
    for distance in range(1, count // 2 + 1):
        below = lax.rem(at + (count - distance), count) * size
        above = lax.rem(at + distance, count) * size
        if distance == count // 2:
            out_ref[pl.ds(below, half)] = pieces[2 * distance - 2][...]
            out_ref[pl.ds(below + half, half)] = pieces[2 * distance - 1][...]
        else:
            out_ref[pl.ds(below, size)] = pieces[2 * distance - 2][...]
            out_ref[pl.ds(above, size)] = pieces[2 * distance - 1][...]


def across_kernel(at_ref, across_ref, own_ref, *refs):
    *pieces, plane_ref, low_ref, high_ref = refs
    place_pieces(plane_ref, lax.rem(at_ref[0], NZ), own_ref, pieces, NZ, NB)
    for b, out_ref in enumerate((low_ref, high_ref)):
        for j in range(FARS):
            out_ref[j] = plane_ref[lax.rem(across_ref[b, j], PLANE)]


def pick_across(at, across, own, pieces):
    half = jax.ShapeDtypeStruct((FARS, BLK, 2 * DH), BF16)
    return pl.pallas_call(
        across_kernel,
        out_shape=(jax.ShapeDtypeStruct((PLANE, BLK, 2 * DH), BF16), half, half),
        in_specs=[SMEM] * 2 + [VMEM] * (1 + len(pieces)),
        out_specs=(VMEM,) * 3,
        compiler_params=params(8),
        name="pick_across",
    )(at, across, own, *pieces)


def pick_kernel(at_ref, above_ref, below_ref, plane_ref, low_ref, high_ref, up_ref, down_ref):
    x_at = lax.div(at_ref[0], NZ)
    for list_ref, arrived_ref, behind, passed, out_ref in (
        (above_ref, low_ref, lax.rem(x_at + NX - 1, NX), 0, up_ref),
        (below_ref, high_ref, lax.rem(x_at + 1, NX), 1, down_ref),
    ):
        for b in range(NB):
            for j in range(FARS):
                listed = list_ref[b, j]
                slot = b * FARS + j
                if b == passed:
                    passes = lax.div(listed, PLANE) == behind

                    @pl.when(passes)
                    def _():
                        out_ref[slot] = arrived_ref[j]

                    @pl.when(jnp.logical_not(passes))
                    def _():
                        out_ref[slot] = plane_ref[lax.rem(listed, PLANE)]
                else:
                    out_ref[slot] = plane_ref[lax.rem(listed, PLANE)]


def pick(at, above, below, plane, low, high):
    out = jax.ShapeDtypeStruct((SLOTS, BLK, 2 * DH), BF16)
    return pl.pallas_call(
        pick_kernel,
        out_shape=(out, out),
        in_specs=[SMEM] * 3 + [VMEM] * 3,
        out_specs=(VMEM, VMEM),
        compiler_params=params(8),
        name="pick_far",
    )(at, above, below, plane, low, high)


def attend_kernel(
    at_ref, far_ref, count_ref, q_ref, g_ref, prev_ref, own_ref, plane_ref, below_ref, above_ref,
    qg_ref, win_ref, farg_ref, k_ref, v_ref, kt_ref, acc_ref, tri_ref,
):
    win_ref[...] = jnp.zeros_like(win_ref)
    key_at = lax.broadcasted_iota(jnp.int32, (BLK, 2 * BLK), 0)
    query_at = lax.broadcasted_iota(jnp.int32, (BLK, 2 * BLK), 1) % BLK
    tri_ref[...] = jnp.where(key_at <= query_at, 0.0, NEG)

    def block(b, carry):
        index = at_ref[0] * NB + b
        for w in range(WIN):
            local = b + w
            both = jnp.where(local < NB, prev_ref[lax.rem(local, NB)], own_ref[lax.rem(local, NB)])
            k_ref[w * BLK : (w + 1) * BLK, :] = both[:, :DH]
            v_ref[w * BLK : (w + 1) * BLK, :] = both[:, DH:]
        for j in range(FARS):
            slot = b * FARS + j
            steps = lax.rem(lax.div(far_ref[b, j], PLANE) + (NX - lax.div(at_ref[0], NZ)), NX)
            mine = plane_ref[lax.rem(far_ref[b, j], PLANE)]
            from_below = (steps == NX - 1) | ((steps == 2) & (b == 0))
            both = jnp.where(from_below, below_ref[slot], above_ref[slot])
            both = jnp.where(steps == 0, mine, both)
            k_ref[(WIN + j) * BLK : (WIN + j + 1) * BLK, :] = both[:, :DH]
            v_ref[(WIN + j) * BLK : (WIN + j + 1) * BLK, :] = both[:, DH:]
        kt_ref[...] = k_ref[...].astype(F32).T.astype(BF16)
        acc_ref[...] = jnp.zeros_like(acc_ref)
        biases = [
            jnp.where(index >= 2, 0.0, NEG).astype(F32),
            jnp.where(index >= 1, 0.0, NEG).astype(F32),
            None,
        ] + [jnp.where(j < count_ref[b], 0.0, NEG).astype(F32) for j in range(FARS)]
        rows = pl.ds(pl.multiple_of(b * BLK, BLK), BLK)
        for pair in range(GQ // 2):
            lo = pair * 2 * DH
            q2 = jnp.concatenate([q_ref[rows, lo : lo + DH], q_ref[rows, lo + DH : lo + 2 * DH]])
            g2 = jnp.concatenate([g_ref[rows, lo : lo + DH], g_ref[rows, lo + DH : lo + 2 * DH]])
            scores = lax.dot_general(k_ref[...], q2, NT, preferred_element_type=F32)
            parts = [scores[c * BLK : (c + 1) * BLK, :] for c in range(WIN + FARS)]
            parts[WIN - 1] = parts[WIN - 1] + tri_ref[...]
            tops = [
                jnp.max(part, axis=0, keepdims=True) + (0.0 if bias is None else bias)
                for part, bias in zip(parts, biases)
            ]
            top = functools.reduce(jnp.maximum, tops)
            expo = jnp.concatenate(
                [
                    jnp.exp2((part - (top if bias is None else top - bias)) * EXP2_SCALE)
                    for part, bias in zip(parts, biases)
                ]
            )
            inv = 1.0 / jnp.sum(expo, axis=0, keepdims=True)
            soft = expo * inv
            grad_p = lax.dot_general(v_ref[...], g2, NT, preferred_element_type=F32)
            delta = jnp.sum(soft * grad_p, axis=0, keepdims=True)
            soft_b = soft.astype(BF16)
            grad_s = (soft * (grad_p - delta)).astype(BF16)
            acc_ref[:, :DH] += jnp.dot(grad_s, q2, preferred_element_type=F32)
            acc_ref[:, DH:] += jnp.dot(soft_b, g2, preferred_element_type=F32)
            grad_q = jnp.dot(kt_ref[...], grad_s, preferred_element_type=F32).T * SCALE
            qg_ref[rows, lo : lo + DH] = grad_q[:BLK].astype(BF16)
            qg_ref[rows, lo + DH : lo + 2 * DH] = grad_q[BLK:].astype(BF16)
        acc_ref[:, :DH] = acc_ref[:, :DH] * SCALE
        window = pl.ds(pl.multiple_of(b * BLK, BLK), WIN * BLK)
        win_ref[window, :] += acc_ref[: WIN * BLK, :]
        for j in range(FARS):
            farg_ref[b * FARS + j] = acc_ref[(WIN + j) * BLK : (WIN + j + 1) * BLK, :].astype(BF16)
        return carry

    for b in range(NB):
        block(b, 0)


def attend(at, far, count, queries, out_grad, prev, own, plane, below, above):
    keys = (WIN + FARS) * BLK
    return pl.pallas_call(
        attend_kernel,
        out_shape=(
            jax.ShapeDtypeStruct((NB * BLK, GQ * DH), BF16),
            jax.ShapeDtypeStruct((2 * NB * BLK, 2 * DH), F32),
            jax.ShapeDtypeStruct((SLOTS, BLK, 2 * DH), BF16),
        ),
        in_specs=[SMEM, SMEM, SMEM] + [VMEM] * 7,
        out_specs=(VMEM, VMEM, VMEM),
        scratch_shapes=[
            pltpu.VMEM((keys, DH), BF16),
            pltpu.VMEM((keys, DH), BF16),
            pltpu.VMEM((DH, keys), BF16),
            pltpu.VMEM((keys, 2 * DH), F32),
            pltpu.VMEM((BLK, 2 * BLK), F32),
        ],
        compiler_params=params(24),
        cost_estimate=pl.CostEstimate(flops=2_400_000_000 * 4, bytes_accessed=6 << 20, transcendentals=2_000_000),
        name="attend",
    )(at, far, count, queries, out_grad, prev, own, plane, below, above)


def spread_kernel(at_ref, *refs):
    lists, pieces = refs[:NX], refs[NX:-2]
    out_ref, acc_ref = refs[-2:]
    mine, below, above, across_low, across_high = pieces
    x_at = lax.div(at_ref[0], NZ)
    acc_ref[...] = jnp.zeros_like(acc_ref)

    def add(listed, term_ref, j):
        @pl.when(lax.div(listed, PLANE) == x_at)
        def _():
            acc_ref[lax.rem(listed, PLANE)] += term_ref[j].astype(F32)

    half = SLOTS // 2
    for j in range(SLOTS):
        add(lists[0][j // FARS, j % FARS], mine, j)
        add(lists[1][j // FARS, j % FARS], above, j)
        add(lists[2][j // FARS, j % FARS], across_low if j < half else across_high, j % half)
        add(lists[3][j // FARS, j % FARS], below, j)
    out_ref[...] = acc_ref[...].astype(BF16)


def spread(at, lists, own, pieces):
    return pl.pallas_call(
        spread_kernel,
        out_shape=jax.ShapeDtypeStruct((PLANE, BLK, 2 * DH), BF16),
        in_specs=[SMEM] * (1 + NX) + [VMEM] * (1 + len(pieces)),
        out_specs=VMEM,
        scratch_shapes=[pltpu.VMEM((PLANE, BLK, 2 * DH), F32)],
        compiler_params=params(16),
        name="spread_far",
    )(at, *lists, own, *pieces)


def finish_kernel(terms_ref, back_ref, window_ref, out_ref):
    total = window_ref[NB * BLK :, :] + back_ref[...].astype(F32)
    for z in range(NZ):
        total += terms_ref[z].astype(F32)
    source = lax.broadcasted_iota(jnp.int32, (2 * DH, 2 * DH), 0)
    target = lax.broadcasted_iota(jnp.int32, (2 * DH, 2 * DH), 1)
    part, rest = target // (2 * PART), target % (2 * PART)
    wanted = (rest // PART) * DH + part * PART + rest % PART
    order = jnp.where(source == wanted, 1.0, 0.0).astype(BF16)
    out_ref[...] = jnp.dot(
        total.astype(BF16), order, preferred_element_type=F32
    ).astype(BF16)


def finish(terms, back, window):
    return pl.pallas_call(
        finish_kernel,
        out_shape=jax.ShapeDtypeStruct((NB * BLK, 2 * DH), BF16),
        in_specs=[VMEM] * 3,
        out_specs=VMEM,
        compiler_params=params(12),
        name="finish_kv",
    )(terms, back, window)


def heads_kernel(at_ref, own_ref, *refs):
    *pieces, other_ref, out_ref = refs
    at, core = lax.div(at_ref[0], 2), lax.rem(at_ref[0], 2)
    rows = NB * BLK
    half = rows // 2
    below, above = lax.rem(at + NY - 1, NY), lax.rem(at + 1, NY)
    across = lax.rem(at + 2, NY)
    starts = (0, rows, 2 * rows, 3 * rows, 3 * rows + half)
    for k, (y, low, high) in enumerate(
        ((at, 0, rows), (below, 0, rows), (above, 0, rows), (across, 0, half), (across, half, rows))
    ):
        mine = own_ref if k == 0 else pieces[k - 1]
        out_ref[2 * y + core, low:high, :] = mine[...]
        out_ref[2 * y + 1 - core, low:high, :] = other_ref[starts[k] : starts[k] + high - low, :]


def place_heads(at, own, pieces, other):
    return pl.pallas_call(
        heads_kernel,
        out_shape=jax.ShapeDtypeStruct((2 * NY, *own.shape), BF16),
        in_specs=[SMEM] + [VMEM] * (2 + len(pieces)),
        out_specs=VMEM,
        compiler_params=params(8),
        name="place_heads",
    )(at, own, *pieces, other)


def weights_kernel(grad_ref, inputs_ref, out_ref):
    quarters, wide = 4, inputs_ref.shape[1] // 4
    for head in range(2):
        grad = jnp.concatenate([grad_ref[x * 2 + head] for x in range(NX)])
        term = lax.dot_general(
            grad, inputs_ref[...], (((0,), (0,)), ((), ())), preferred_element_type=F32
        ).astype(BF16)
        for part in range(4):
            for quarter in range(quarters):
                out_ref[
                    head * 4 + part, quarter * 2 * PART : (quarter + 1) * 2 * PART, :
                ] = term[
                    part * 2 * PART : (part + 1) * 2 * PART, quarter * wide : (quarter + 1) * wide
                ]


def weight_terms(grad, inputs_x):
    return pl.pallas_call(
        weights_kernel,
        out_shape=jax.ShapeDtypeStruct((NZ, 4 * 2 * PART, inputs_x.shape[1] // 4), BF16),
        in_specs=[VMEM, VMEM],
        out_specs=VMEM,
        compiler_params=params(16),
        cost_estimate=pl.CostEstimate(flops=1 << 30, bytes_accessed=4 << 20, transcendentals=0),
        name="weight_terms",
    )(grad, inputs_x)


def weight_sum_kernel(terms_ref, key_ref, value_ref):
    total = terms_ref[0].astype(F32)
    for z in range(1, NZ):
        total += terms_ref[z].astype(F32)
    wide = total.shape[1]
    for quarter in range(4):
        low = quarter * 2 * PART
        key_ref[:, quarter * wide : (quarter + 1) * wide] = total[low : low + PART]
        value_ref[:, quarter * wide : (quarter + 1) * wide] = total[low + PART : low + 2 * PART]


def weight_sum(terms):
    out = jax.ShapeDtypeStruct((PART, 4 * terms.shape[2]), F32)
    return pl.pallas_call(
        weight_sum_kernel,
        out_shape=(out, out),
        in_specs=[VMEM],
        out_specs=(VMEM, VMEM),
        compiler_params=params(8),
        name="weight_sum",
    )(terms)


def input_kernel(at_ref, grad_ref, weights_ref, mine_ref, above_ref, low_ref, high_ref, below_ref):
    x_at = lax.div(at_ref[0], NZ)
    half = low_ref.shape[0]
    for steps in range(NX):
        x = lax.rem(x_at + steps, NX)
        grad = jnp.concatenate([grad_ref[2 * x], grad_ref[2 * x + 1]], axis=1)
        term = jnp.dot(grad, weights_ref[...], preferred_element_type=F32)
        if steps == 2:
            low_ref[...] = term[:half].astype(BF16)
            high_ref[...] = term[half:].astype(BF16)
        else:
            out_ref = (mine_ref, above_ref, None, below_ref)[steps]
            out_ref[...] = term.astype(out_ref.dtype)


def input_terms(at, grad, weights):
    rows, wide = grad.shape[1], weights.shape[1]
    send, half = (jax.ShapeDtypeStruct((size, wide), BF16) for size in (rows, rows // 2))
    return pl.pallas_call(
        input_kernel,
        out_shape=(jax.ShapeDtypeStruct((rows, wide), F32), send, half, half, send),
        in_specs=[SMEM, VMEM, VMEM],
        out_specs=(VMEM,) * 5,
        compiler_params=params(16),
        cost_estimate=pl.CostEstimate(flops=1 << 30, bytes_accessed=4 << 20, transcendentals=0),
        name="input_terms",
    )(at, grad, weights)


def added(term, arrived, low):
    high = low + arrived.shape[0]
    rows = (term[low:high].astype(F32) + arrived.astype(F32)).astype(BF16)
    return jnp.concatenate([term[:low], rows, term[high:]])


def local(
    queries, key_rows, value_rows, out_grad, inputs, key_weight, value_weight, far_blocks, far_count
):
    tokens = queries.shape[0]
    seq_index = lax.axis_index("seq").astype(jnp.int32)
    at = seq_index.reshape(1)
    own_index = lax.axis_index("own").astype(jnp.int32).reshape(1)
    own_kv = jnp.concatenate([key_rows, value_rows], axis=1).reshape(NB, BLK, 2 * DH)

    from_below, from_above = both_ways(own_kv, own_kv, "seq", Z_UP)
    across = [(x * NZ + z, (x + 2) % NX * NZ + z) for x in range(NX) for z in range(NZ)]
    list_across = lax.ppermute(far_blocks, "seq", across)
    from_below, from_above, list_across, listed = lax.optimization_barrier(
        (from_below, from_above, list_across, far_blocks)
    )
    plane = [from_below, from_above]
    for distance in range(2, NZ // 2 + 1):
        if distance == NZ // 2:
            from_below, from_above = from_below[: NB // 2], from_above[NB // 2 :]
        from_below, from_above = both_ways(from_below, from_above, "seq", Z_UP)
        plane += [from_below, from_above]
    prev_kv = shifted(own_kv, "seq", 1)
    plane, low, high = pick_across(at, list_across, own_kv, plane)
    low, high, listed, key_weight, value_weight = lax.optimization_barrier(
        (low, high, listed, key_weight, value_weight)
    )
    weights = jnp.concatenate([key_weight.T, value_weight.T])
    weights = lax.all_gather(weights, "seq", axis=0, axis_index_groups=Z_GROUPS, tiled=True)
    low, high = both_ways(low, high, "seq", X_UP)
    list_below, list_above = both_ways(listed, listed, "seq", X_UP)
    up, down = pick(at, list_above, list_below, plane, low, high)
    from_below, from_above = both_ways(up, down, "seq", X_UP)

    query_grad, window, far_grad = attend(
        at, far_blocks, far_count, queries, out_grad, prev_kv, own_kv, plane, from_below, from_above
    )
    back = shifted(window[:tokens].astype(BF16), "seq", -1)
    far_below, far_above = both_ways(far_grad, far_grad, "seq", X_UP)
    far_below, far_above, back, inputs = lax.optimization_barrier(
        (far_below, far_above, back, inputs)
    )
    far_across = both_ways(far_below[:FARS], far_above[FARS:], "seq", X_UP)
    far_all = (far_below, far_above, *far_across)
    inputs_x = lax.all_gather(inputs, "seq", axis=0, axis_index_groups=X_GROUPS, tiled=True)
    list_above, weights = lax.optimization_barrier((list_above, weights))
    lists = (far_blocks, list_above, list_across, list_below)
    dense = spread(at, lists, far_grad, far_all)
    dense = dense.reshape(NZ, tokens, 2 * DH)
    terms = lax.all_to_all(dense, "seq", 0, 0, axis_index_groups=Z_GROUPS, tiled=True)
    kv_grad = finish(terms, back, window)

    moved = lax.ppermute(kv_grad, ("seq", "own"), SWAP_XY)
    same_core = ring_gather(moved, "own", Y_UP, NY)
    other_core = lax.ppermute(jnp.concatenate([moved, *same_core]), "own", CORES)
    heads = place_heads(own_index, moved, same_core, other_core)

    mine, above, low, high, below = input_terms(at, heads, weights)
    from_below, from_above = both_ways(low, high, "seq", X_UP)
    pieces = weight_terms(heads, inputs_x)
    pieces = lax.all_to_all(pieces, "seq", 0, 0, axis_index_groups=Z_GROUPS, tiled=True)
    above, below = added(above, from_below, 0), added(below, from_above, tokens // 2)
    from_below, from_above = both_ways(above, below, "seq", X_UP)
    input_grad = mine + from_below.astype(F32) + from_above.astype(F32)
    key_weight_grad, value_weight_grad = weight_sum(pieces)
    return (query_grad, input_grad.astype(BF16), key_weight_grad.T, value_weight_grad.T)


def solution(mesh):
    return jax.shard_map(
        local,
        mesh=mesh,
        in_specs=(
            P("seq", "own"),
            P("seq", "own"),
            P("seq", "own"),
            P("seq", "own"),
            P("seq", "own"),
            P("own", "seq"),
            P("own", "seq"),
            P("seq", None),
            P("seq"),
        ),
        out_specs=(P("seq", "own"), P("seq", "own"), P("own", "seq"), P("own", "seq")),
        check_vma=False,
    )
```

```python
import functools
import math

import jax
import jax.numpy as jnp
from jax import lax
from jax.experimental import pallas as pl
from jax.experimental.pallas import tpu as pltpu
from jax.sharding import PartitionSpec as P

DH = 128
GQ = 8
BLK = 128
WIN = 3
FARS = 4
NX = 4
NZ = 8
NB = 2
PLANE = NB * NZ
SLOTS = NB * FARS
X_GROUPS = [[x * NZ + z for x in range(NX)] for z in range(NZ)]
Z_GROUPS = [[x * NZ + z for z in range(NZ)] for x in range(NX)]
Z_UP = [(x * NZ + z, x * NZ + (z + 1) % NZ) for x in range(NX) for z in range(NZ)]
X_UP = [(x * NZ + z, (x + 1) % NX * NZ + z) for x in range(NX) for z in range(NZ)]
NY = 4
Y_UP = [(2 * y + core, 2 * ((y + 1) % NY) + core) for y in range(NY) for core in range(2)]
CORES = [(own, own ^ 1) for own in range(2 * NY)]
SWAP_XY = [
    (((x * NZ + z) * NY + y) * 2 + core, ((y * NZ + z) * NY + x) * 2 + core)
    for x in range(NX)
    for z in range(NZ)
    for y in range(NY)
    for core in range(2)
]
PART = DH // 4
SCALE = 1.0 / math.sqrt(DH)
EXP2_SCALE = SCALE * math.log2(math.e)
NEG = -1e30

SMEM = pl.BlockSpec(memory_space=pltpu.SMEM)
VMEM = pl.BlockSpec(memory_space=pltpu.VMEM)
NT = (((1,), (1,)), ((), ()))
F32 = jnp.float32
BF16 = jnp.bfloat16


def params(mib):
    return pltpu.CompilerParams(vmem_limit_bytes=mib << 20)


def shifted(value, axis, steps):
    count = lax.axis_size(axis)
    leading, last = (max(0, -steps), min(count, count - steps))
    return lax.ppermute(value, axis, [(source, source + steps) for source in range(leading, last)])


def both_ways(upward, downward, axis, pairs):
    back = [(target, source) for source, target in pairs]
    return lax.ppermute(upward, axis, pairs), lax.ppermute(downward, axis, back)


def ring_gather(value, axis, pairs, count):
    half = value.shape[0] // 2
    from_below, from_above = value, value
    pieces = []
    for distance in range(1, count // 2 + 1):
        if distance == count // 2:
            from_below, from_above = from_below[:half], from_above[half:]
        from_below, from_above = both_ways(from_below, from_above, axis, pairs)
        pieces += [from_below, from_above]
    return pieces


def place_pieces(out_ref, at, own_ref, pieces, count, size):
    half = size // 2
    out_ref[pl.ds(at * size, size)] = own_ref[...]
    for distance in range(1, count // 2 + 1):
        below = lax.rem(at + (count - distance), count) * size
        above = lax.rem(at + distance, count) * size
        if distance == count // 2:
            out_ref[pl.ds(below, half)] = pieces[2 * distance - 2][...]
            out_ref[pl.ds(below + half, half)] = pieces[2 * distance - 1][...]
        else:
            out_ref[pl.ds(below, size)] = pieces[2 * distance - 2][...]
            out_ref[pl.ds(above, size)] = pieces[2 * distance - 1][...]


def across_kernel(at_ref, across_ref, own_ref, *refs):
    *pieces, plane_ref, low_ref, high_ref = refs
    place_pieces(plane_ref, lax.rem(at_ref[0], NZ), own_ref, pieces, NZ, NB)
    for b, out_ref in enumerate((low_ref, high_ref)):
        for j in range(FARS):
            out_ref[j] = plane_ref[lax.rem(across_ref[b, j], PLANE)]


def pick_across(at, across, own, pieces):
    half = jax.ShapeDtypeStruct((FARS, BLK, 2 * DH), BF16)
    return pl.pallas_call(
        across_kernel,
        out_shape=(jax.ShapeDtypeStruct((PLANE, BLK, 2 * DH), BF16), half, half),
        in_specs=[SMEM] * 2 + [VMEM] * (1 + len(pieces)),
        out_specs=(VMEM,) * 3,
        compiler_params=params(8),
        name="pick_across",
    )(at, across, own, *pieces)


def pick_kernel(at_ref, above_ref, below_ref, plane_ref, low_ref, high_ref, up_ref, down_ref):
    x_at = lax.div(at_ref[0], NZ)
    for list_ref, arrived_ref, behind, passed, out_ref in (
        (above_ref, low_ref, lax.rem(x_at + NX - 1, NX), 0, up_ref),
        (below_ref, high_ref, lax.rem(x_at + 1, NX), 1, down_ref),
    ):
        for b in range(NB):
            for j in range(FARS):
                listed = list_ref[b, j]
                slot = b * FARS + j
                if b == passed:
                    passes = lax.div(listed, PLANE) == behind

                    @pl.when(passes)
                    def _():
                        out_ref[slot] = arrived_ref[j]

                    @pl.when(jnp.logical_not(passes))
                    def _():
                        out_ref[slot] = plane_ref[lax.rem(listed, PLANE)]
                else:
                    out_ref[slot] = plane_ref[lax.rem(listed, PLANE)]


def pick(at, above, below, plane, low, high):
    out = jax.ShapeDtypeStruct((SLOTS, BLK, 2 * DH), BF16)
    return pl.pallas_call(
        pick_kernel,
        out_shape=(out, out),
        in_specs=[SMEM] * 3 + [VMEM] * 3,
        out_specs=(VMEM, VMEM),
        compiler_params=params(8),
        name="pick_far",
    )(at, above, below, plane, low, high)


def attend_kernel(
    at_ref, far_ref, count_ref, q_ref, g_ref, prev_ref, own_ref, plane_ref, below_ref, above_ref,
    qg_ref, win_ref, farg_ref, k_ref, v_ref, kt_ref, acc_ref, tri_ref,
):
    win_ref[...] = jnp.zeros_like(win_ref)
    key_at = lax.broadcasted_iota(jnp.int32, (BLK, 2 * BLK), 0)
    query_at = lax.broadcasted_iota(jnp.int32, (BLK, 2 * BLK), 1) % BLK
    tri_ref[...] = jnp.where(key_at <= query_at, 0.0, NEG)

    def block(b, carry):
        index = at_ref[0] * NB + b
        for w in range(WIN):
            local = b + w
            both = jnp.where(local < NB, prev_ref[lax.rem(local, NB)], own_ref[lax.rem(local, NB)])
            k_ref[w * BLK : (w + 1) * BLK, :] = both[:, :DH]
            v_ref[w * BLK : (w + 1) * BLK, :] = both[:, DH:]
        for j in range(FARS):
            slot = b * FARS + j
            steps = lax.rem(lax.div(far_ref[b, j], PLANE) + (NX - lax.div(at_ref[0], NZ)), NX)
            mine = plane_ref[lax.rem(far_ref[b, j], PLANE)]
            from_below = (steps == NX - 1) | ((steps == 2) & (b == 0))
            both = jnp.where(from_below, below_ref[slot], above_ref[slot])
            both = jnp.where(steps == 0, mine, both)
            k_ref[(WIN + j) * BLK : (WIN + j + 1) * BLK, :] = both[:, :DH]
            v_ref[(WIN + j) * BLK : (WIN + j + 1) * BLK, :] = both[:, DH:]
        kt_ref[...] = k_ref[...].astype(F32).T.astype(BF16)
        acc_ref[...] = jnp.zeros_like(acc_ref)
        biases = [
            jnp.where(index >= 2, 0.0, NEG).astype(F32),
            jnp.where(index >= 1, 0.0, NEG).astype(F32),
            None,
        ] + [jnp.where(j < count_ref[b], 0.0, NEG).astype(F32) for j in range(FARS)]
        rows = pl.ds(pl.multiple_of(b * BLK, BLK), BLK)
        for pair in range(GQ // 2):
            lo = pair * 2 * DH
            q2 = jnp.concatenate([q_ref[rows, lo : lo + DH], q_ref[rows, lo + DH : lo + 2 * DH]])
            g2 = jnp.concatenate([g_ref[rows, lo : lo + DH], g_ref[rows, lo + DH : lo + 2 * DH]])
            scores = lax.dot_general(k_ref[...], q2, NT, preferred_element_type=F32)
            parts = [scores[c * BLK : (c + 1) * BLK, :] for c in range(WIN + FARS)]
            parts[WIN - 1] = parts[WIN - 1] + tri_ref[...]
            tops = [
                jnp.max(part, axis=0, keepdims=True) + (0.0 if bias is None else bias)
                for part, bias in zip(parts, biases)
            ]
            top = functools.reduce(jnp.maximum, tops)
            expo = jnp.concatenate(
                [
                    jnp.exp2((part - (top if bias is None else top - bias)) * EXP2_SCALE)
                    for part, bias in zip(parts, biases)
                ]
            )
            inv = 1.0 / jnp.sum(expo, axis=0, keepdims=True)
            soft = expo * inv
            grad_p = lax.dot_general(v_ref[...], g2, NT, preferred_element_type=F32)
            delta = jnp.sum(soft * grad_p, axis=0, keepdims=True)
            soft_b = soft.astype(BF16)
            grad_s = (soft * (grad_p - delta)).astype(BF16)
            acc_ref[:, :DH] += jnp.dot(grad_s, q2, preferred_element_type=F32)
            acc_ref[:, DH:] += jnp.dot(soft_b, g2, preferred_element_type=F32)
            grad_q = jnp.dot(kt_ref[...], grad_s, preferred_element_type=F32).T * SCALE
            qg_ref[rows, lo : lo + DH] = grad_q[:BLK].astype(BF16)
            qg_ref[rows, lo + DH : lo + 2 * DH] = grad_q[BLK:].astype(BF16)
        acc_ref[:, :DH] = acc_ref[:, :DH] * SCALE
        window = pl.ds(pl.multiple_of(b * BLK, BLK), WIN * BLK)
        win_ref[window, :] += acc_ref[: WIN * BLK, :]
        for j in range(FARS):
            farg_ref[b * FARS + j] = acc_ref[(WIN + j) * BLK : (WIN + j + 1) * BLK, :].astype(BF16)
        return carry

    for b in range(NB):
        block(b, 0)


def attend(at, far, count, queries, out_grad, prev, own, plane, below, above):
    keys = (WIN + FARS) * BLK
    return pl.pallas_call(
        attend_kernel,
        out_shape=(
            jax.ShapeDtypeStruct((NB * BLK, GQ * DH), BF16),
            jax.ShapeDtypeStruct((2 * NB * BLK, 2 * DH), F32),
            jax.ShapeDtypeStruct((SLOTS, BLK, 2 * DH), BF16),
        ),
        in_specs=[SMEM, SMEM, SMEM] + [VMEM] * 7,
        out_specs=(VMEM, VMEM, VMEM),
        scratch_shapes=[
            pltpu.VMEM((keys, DH), BF16),
            pltpu.VMEM((keys, DH), BF16),
            pltpu.VMEM((DH, keys), BF16),
            pltpu.VMEM((keys, 2 * DH), F32),
            pltpu.VMEM((BLK, 2 * BLK), F32),
        ],
        compiler_params=params(24),
        cost_estimate=pl.CostEstimate(flops=2_400_000_000 * 4, bytes_accessed=6 << 20, transcendentals=2_000_000),
        name="attend",
    )(at, far, count, queries, out_grad, prev, own, plane, below, above)


def spread_kernel(at_ref, *refs):
    lists, pieces = refs[:NX], refs[NX:-2]
    out_ref, acc_ref = refs[-2:]
    mine, below, above, across_low, across_high = pieces
    x_at = lax.div(at_ref[0], NZ)
    acc_ref[...] = jnp.zeros_like(acc_ref)

    def add(listed, term_ref, j):
        @pl.when(lax.div(listed, PLANE) == x_at)
        def _():
            acc_ref[lax.rem(listed, PLANE)] += term_ref[j].astype(F32)

    half = SLOTS // 2
    for j in range(SLOTS):
        add(lists[0][j // FARS, j % FARS], mine, j)
        add(lists[1][j // FARS, j % FARS], above, j)
        add(lists[2][j // FARS, j % FARS], across_low if j < half else across_high, j % half)
        add(lists[3][j // FARS, j % FARS], below, j)
    out_ref[...] = acc_ref[...].astype(BF16)


def spread(at, lists, own, pieces):
    return pl.pallas_call(
        spread_kernel,
        out_shape=jax.ShapeDtypeStruct((PLANE, BLK, 2 * DH), BF16),
        in_specs=[SMEM] * (1 + NX) + [VMEM] * (1 + len(pieces)),
        out_specs=VMEM,
        scratch_shapes=[pltpu.VMEM((PLANE, BLK, 2 * DH), F32)],
        compiler_params=params(16),
        name="spread_far",
    )(at, *lists, own, *pieces)


def finish_kernel(terms_ref, back_ref, window_ref, out_ref):
    total = window_ref[NB * BLK :, :] + back_ref[...].astype(F32)
    for z in range(NZ):
        total += terms_ref[z].astype(F32)
    source = lax.broadcasted_iota(jnp.int32, (2 * DH, 2 * DH), 0)
    target = lax.broadcasted_iota(jnp.int32, (2 * DH, 2 * DH), 1)
    part, rest = target // (2 * PART), target % (2 * PART)
    wanted = (rest // PART) * DH + part * PART + rest % PART
    order = jnp.where(source == wanted, 1.0, 0.0).astype(BF16)
    out_ref[...] = jnp.dot(
        total.astype(BF16), order, preferred_element_type=F32
    ).astype(BF16)


def finish(terms, back, window):
    return pl.pallas_call(
        finish_kernel,
        out_shape=jax.ShapeDtypeStruct((NB * BLK, 2 * DH), BF16),
        in_specs=[VMEM] * 3,
        out_specs=VMEM,
        compiler_params=params(12),
        name="finish_kv",
    )(terms, back, window)


def heads_kernel(at_ref, own_ref, *refs):
    *pieces, other_ref, out_ref = refs
    at, core = lax.div(at_ref[0], 2), lax.rem(at_ref[0], 2)
    rows = NB * BLK
    half = rows // 2
    below, above = lax.rem(at + NY - 1, NY), lax.rem(at + 1, NY)
    across = lax.rem(at + 2, NY)
    starts = (0, rows, 2 * rows, 3 * rows, 3 * rows + half)
    for k, (y, low, high) in enumerate(
        ((at, 0, rows), (below, 0, rows), (above, 0, rows), (across, 0, half), (across, half, rows))
    ):
        mine = own_ref if k == 0 else pieces[k - 1]
        out_ref[2 * y + core, low:high, :] = mine[...]
        out_ref[2 * y + 1 - core, low:high, :] = other_ref[starts[k] : starts[k] + high - low, :]


def place_heads(at, own, pieces, other):
    return pl.pallas_call(
        heads_kernel,
        out_shape=jax.ShapeDtypeStruct((2 * NY, *own.shape), BF16),
        in_specs=[SMEM] + [VMEM] * (2 + len(pieces)),
        out_specs=VMEM,
        compiler_params=params(8),
        name="place_heads",
    )(at, own, *pieces, other)


def weights_kernel(grad_ref, inputs_ref, out_ref):
    quarters, wide = 4, inputs_ref.shape[1] // 4
    for head in range(2):
        grad = jnp.concatenate([grad_ref[x * 2 + head] for x in range(NX)])
        term = lax.dot_general(
            grad, inputs_ref[...], (((0,), (0,)), ((), ())), preferred_element_type=F32
        ).astype(BF16)
        for part in range(4):
            for quarter in range(quarters):
                out_ref[
                    head * 4 + part, quarter * 2 * PART : (quarter + 1) * 2 * PART, :
                ] = term[
                    part * 2 * PART : (part + 1) * 2 * PART, quarter * wide : (quarter + 1) * wide
                ]


def weight_terms(grad, inputs_x):
    return pl.pallas_call(
        weights_kernel,
        out_shape=jax.ShapeDtypeStruct((NZ, 4 * 2 * PART, inputs_x.shape[1] // 4), BF16),
        in_specs=[VMEM, VMEM],
        out_specs=VMEM,
        compiler_params=params(16),
        cost_estimate=pl.CostEstimate(flops=1 << 30, bytes_accessed=4 << 20, transcendentals=0),
        name="weight_terms",
    )(grad, inputs_x)


def weight_sum_kernel(terms_ref, key_ref, value_ref):
    total = terms_ref[0].astype(F32)
    for z in range(1, NZ):
        total += terms_ref[z].astype(F32)
    wide = total.shape[1]
    for quarter in range(4):
        low = quarter * 2 * PART
        key_ref[:, quarter * wide : (quarter + 1) * wide] = total[low : low + PART]
        value_ref[:, quarter * wide : (quarter + 1) * wide] = total[low + PART : low + 2 * PART]


def weight_sum(terms):
    out = jax.ShapeDtypeStruct((PART, 4 * terms.shape[2]), F32)
    return pl.pallas_call(
        weight_sum_kernel,
        out_shape=(out, out),
        in_specs=[VMEM],
        out_specs=(VMEM, VMEM),
        compiler_params=params(8),
        name="weight_sum",
    )(terms)


def input_kernel(at_ref, grad_ref, weights_ref, mine_ref, above_ref, low_ref, high_ref, below_ref):
    x_at = lax.div(at_ref[0], NZ)
    half = low_ref.shape[0]
    for steps in range(NX):
        x = lax.rem(x_at + steps, NX)
        grad = jnp.concatenate([grad_ref[2 * x], grad_ref[2 * x + 1]], axis=1)
        term = jnp.dot(grad, weights_ref[...], preferred_element_type=F32)
        if steps == 2:
            low_ref[...] = term[:half].astype(BF16)
            high_ref[...] = term[half:].astype(BF16)
        else:
            out_ref = (mine_ref, above_ref, None, below_ref)[steps]
            out_ref[...] = term.astype(out_ref.dtype)


def input_terms(at, grad, weights):
    rows, wide = grad.shape[1], weights.shape[1]
    send, half = (jax.ShapeDtypeStruct((size, wide), BF16) for size in (rows, rows // 2))
    return pl.pallas_call(
        input_kernel,
        out_shape=(jax.ShapeDtypeStruct((rows, wide), F32), send, half, half, send),
        in_specs=[SMEM, VMEM, VMEM],
        out_specs=(VMEM,) * 5,
        compiler_params=params(16),
        cost_estimate=pl.CostEstimate(flops=1 << 30, bytes_accessed=4 << 20, transcendentals=0),
        name="input_terms",
    )(at, grad, weights)


def added(term, arrived, low):
    high = low + arrived.shape[0]
    rows = (term[low:high].astype(F32) + arrived.astype(F32)).astype(BF16)
    return jnp.concatenate([term[:low], rows, term[high:]])


def local(
    queries, key_rows, value_rows, out_grad, inputs, key_weight, value_weight, far_blocks, far_count
):
    tokens = queries.shape[0]
    seq_index = lax.axis_index("seq").astype(jnp.int32)
    at = seq_index.reshape(1)
    own_index = lax.axis_index("own").astype(jnp.int32).reshape(1)
    own_kv = jnp.concatenate([key_rows, value_rows], axis=1).reshape(NB, BLK, 2 * DH)

    from_below, from_above = both_ways(own_kv, own_kv, "seq", Z_UP)
    across = [(x * NZ + z, (x + 2) % NX * NZ + z) for x in range(NX) for z in range(NZ)]
    list_across = lax.ppermute(far_blocks, "seq", across)
    from_below, from_above, list_across, listed = lax.optimization_barrier(
        (from_below, from_above, list_across, far_blocks)
    )
    plane = [from_below, from_above]
    for distance in range(2, NZ // 2 + 1):
        if distance == NZ // 2:
            from_below, from_above = from_below[: NB // 2], from_above[NB // 2 :]
        from_below, from_above = both_ways(from_below, from_above, "seq", Z_UP)
        plane += [from_below, from_above]
    prev_kv = shifted(own_kv, "seq", 1)
    plane, low, high = pick_across(at, list_across, own_kv, plane)
    low, high, listed, key_weight, value_weight = lax.optimization_barrier(
        (low, high, listed, key_weight, value_weight)
    )
    weights = jnp.concatenate([key_weight.T, value_weight.T])
    weights = lax.all_gather(weights, "seq", axis=0, axis_index_groups=Z_GROUPS, tiled=True)
    low, high = both_ways(low, high, "seq", X_UP)
    list_below, list_above = both_ways(listed, listed, "seq", X_UP)
    up, down = pick(at, list_above, list_below, plane, low, high)
    from_below, from_above = both_ways(up, down, "seq", X_UP)

    query_grad, window, far_grad = attend(
        at, far_blocks, far_count, queries, out_grad, prev_kv, own_kv, plane, from_below, from_above
    )
    back = shifted(window[:tokens].astype(BF16), "seq", -1)
    far_below, far_above = both_ways(far_grad, far_grad, "seq", X_UP)
    far_below, far_above, back, inputs = lax.optimization_barrier(
        (far_below, far_above, back, inputs)
    )
    far_across = both_ways(far_below[:FARS], far_above[FARS:], "seq", X_UP)
    far_all = (far_below, far_above, *far_across)
    inputs_x = lax.all_gather(inputs, "seq", axis=0, axis_index_groups=X_GROUPS, tiled=True)
    list_above, weights = lax.optimization_barrier((list_above, weights))
    lists = (far_blocks, list_above, list_across, list_below)
    dense = spread(at, lists, far_grad, far_all)
    dense = dense.reshape(NZ, tokens, 2 * DH)
    terms = lax.all_to_all(dense, "seq", 0, 0, axis_index_groups=Z_GROUPS, tiled=True)
    kv_grad = finish(terms, back, window)

    moved = lax.ppermute(kv_grad, ("seq", "own"), SWAP_XY)
    moved, inputs_x = lax.optimization_barrier((moved, inputs_x))
    same_core = ring_gather(moved, "own", Y_UP, NY)
    other_core = lax.ppermute(jnp.concatenate([moved, *same_core]), "own", CORES)
    heads = place_heads(own_index, moved, same_core, other_core)

    mine, above, low, high, below = input_terms(at, heads, weights)
    from_below, from_above = both_ways(low, high, "seq", X_UP)
    pieces = weight_terms(heads, inputs_x)
    pieces = lax.all_to_all(pieces, "seq", 0, 0, axis_index_groups=Z_GROUPS, tiled=True)
    above, below = added(above, from_below, 0), added(below, from_above, tokens // 2)
    from_below, from_above = both_ways(above, below, "seq", X_UP)
    input_grad = mine + from_below.astype(F32) + from_above.astype(F32)
    key_weight_grad, value_weight_grad = weight_sum(pieces)
    return (query_grad, input_grad.astype(BF16), key_weight_grad.T, value_weight_grad.T)


def solution(mesh):
    return jax.shard_map(
        local,
        mesh=mesh,
        in_specs=(
            P("seq", "own"),
            P("seq", "own"),
            P("seq", "own"),
            P("seq", "own"),
            P("seq", "own"),
            P("own", "seq"),
            P("own", "seq"),
            P("seq", None),
            P("seq"),
        ),
        out_specs=(P("seq", "own"), P("seq", "own"), P("own", "seq"), P("own", "seq")),
        check_vma=False,
    )
```

```python
import functools
import math

import jax
import jax.numpy as jnp
from jax import lax
from jax.experimental import pallas as pl
from jax.experimental.pallas import tpu as pltpu
from jax.sharding import PartitionSpec as P

DH = 128
GQ = 8
BLK = 128
WIN = 3
FARS = 4
NX = 4
NZ = 8
NB = 2
PLANE = NB * NZ
SLOTS = NB * FARS
X_GROUPS = [[x * NZ + z for x in range(NX)] for z in range(NZ)]
Z_GROUPS = [[x * NZ + z for z in range(NZ)] for x in range(NX)]
Z_UP = [(x * NZ + z, x * NZ + (z + 1) % NZ) for x in range(NX) for z in range(NZ)]
X_UP = [(x * NZ + z, (x + 1) % NX * NZ + z) for x in range(NX) for z in range(NZ)]
NY = 4
Y_UP = [(2 * y + core, 2 * ((y + 1) % NY) + core) for y in range(NY) for core in range(2)]
CORES = [(own, own ^ 1) for own in range(2 * NY)]
SWAP_XY = [
    (((x * NZ + z) * NY + y) * 2 + core, ((y * NZ + z) * NY + x) * 2 + core)
    for x in range(NX)
    for z in range(NZ)
    for y in range(NY)
    for core in range(2)
]
PART = DH // 4
SCALE = 1.0 / math.sqrt(DH)
EXP2_SCALE = SCALE * math.log2(math.e)
NEG = -1e30

SMEM = pl.BlockSpec(memory_space=pltpu.SMEM)
VMEM = pl.BlockSpec(memory_space=pltpu.VMEM)
NT = (((1,), (1,)), ((), ()))
F32 = jnp.float32
BF16 = jnp.bfloat16


def params(mib):
    return pltpu.CompilerParams(vmem_limit_bytes=mib << 20)


def shifted(value, axis, steps):
    count = lax.axis_size(axis)
    leading, last = (max(0, -steps), min(count, count - steps))
    return lax.ppermute(value, axis, [(source, source + steps) for source in range(leading, last)])


def both_ways(upward, downward, axis, pairs):
    back = [(target, source) for source, target in pairs]
    return lax.ppermute(upward, axis, pairs), lax.ppermute(downward, axis, back)


def ring_gather(value, axis, pairs, count):
    half = value.shape[0] // 2
    from_below, from_above = value, value
    pieces = []
    for distance in range(1, count // 2 + 1):
        if distance == count // 2:
            from_below, from_above = from_below[:half], from_above[half:]
        from_below, from_above = both_ways(from_below, from_above, axis, pairs)
        pieces += [from_below, from_above]
    return pieces


def place_pieces(out_ref, at, own_ref, pieces, count, size):
    half = size // 2
    out_ref[pl.ds(at * size, size)] = own_ref[...]
    for distance in range(1, count // 2 + 1):
        below = lax.rem(at + (count - distance), count) * size
        above = lax.rem(at + distance, count) * size
        if distance == count // 2:
            out_ref[pl.ds(below, half)] = pieces[2 * distance - 2][...]
            out_ref[pl.ds(below + half, half)] = pieces[2 * distance - 1][...]
        else:
            out_ref[pl.ds(below, size)] = pieces[2 * distance - 2][...]
            out_ref[pl.ds(above, size)] = pieces[2 * distance - 1][...]


def across_kernel(at_ref, across_ref, own_ref, *refs):
    *pieces, plane_ref, low_ref, high_ref = refs
    place_pieces(plane_ref, lax.rem(at_ref[0], NZ), own_ref, pieces, NZ, NB)
    for b, out_ref in enumerate((low_ref, high_ref)):
        for j in range(FARS):
            out_ref[j] = plane_ref[lax.rem(across_ref[b, j], PLANE)]


def pick_across(at, across, own, pieces):
    half = jax.ShapeDtypeStruct((FARS, BLK, 2 * DH), BF16)
    return pl.pallas_call(
        across_kernel,
        out_shape=(jax.ShapeDtypeStruct((PLANE, BLK, 2 * DH), BF16), half, half),
        in_specs=[SMEM] * 2 + [VMEM] * (1 + len(pieces)),
        out_specs=(VMEM,) * 3,
        compiler_params=params(8),
        name="pick_across",
    )(at, across, own, *pieces)


def pick_kernel(at_ref, above_ref, below_ref, plane_ref, low_ref, high_ref, up_ref, down_ref):
    x_at = lax.div(at_ref[0], NZ)
    for list_ref, arrived_ref, behind, passed, out_ref in (
        (above_ref, low_ref, lax.rem(x_at + NX - 1, NX), 0, up_ref),
        (below_ref, high_ref, lax.rem(x_at + 1, NX), 1, down_ref),
    ):
        for b in range(NB):
            for j in range(FARS):
                listed = list_ref[b, j]
                slot = b * FARS + j
                if b == passed:
                    passes = lax.div(listed, PLANE) == behind

                    @pl.when(passes)
                    def _():
                        out_ref[slot] = arrived_ref[j]

                    @pl.when(jnp.logical_not(passes))
                    def _():
                        out_ref[slot] = plane_ref[lax.rem(listed, PLANE)]
                else:
                    out_ref[slot] = plane_ref[lax.rem(listed, PLANE)]


def pick(at, above, below, plane, low, high):
    out = jax.ShapeDtypeStruct((SLOTS, BLK, 2 * DH), BF16)
    return pl.pallas_call(
        pick_kernel,
        out_shape=(out, out),
        in_specs=[SMEM] * 3 + [VMEM] * 3,
        out_specs=(VMEM, VMEM),
        compiler_params=params(8),
        name="pick_far",
    )(at, above, below, plane, low, high)


def attend_kernel(
    at_ref, far_ref, count_ref, q_ref, g_ref, prev_ref, own_ref, plane_ref, below_ref, above_ref,
    qg_ref, win_ref, farg_ref, k_ref, v_ref, kt_ref, acc_ref, tri_ref,
):
    win_ref[...] = jnp.zeros_like(win_ref)
    key_at = lax.broadcasted_iota(jnp.int32, (BLK, 2 * BLK), 0)
    query_at = lax.broadcasted_iota(jnp.int32, (BLK, 2 * BLK), 1) % BLK
    tri_ref[...] = jnp.where(key_at <= query_at, 0.0, NEG)

    def block(b, carry):
        index = at_ref[0] * NB + b
        for w in range(WIN):
            local = b + w
            both = jnp.where(local < NB, prev_ref[lax.rem(local, NB)], own_ref[lax.rem(local, NB)])
            k_ref[w * BLK : (w + 1) * BLK, :] = both[:, :DH]
            v_ref[w * BLK : (w + 1) * BLK, :] = both[:, DH:]
        for j in range(FARS):
            slot = b * FARS + j
            steps = lax.rem(lax.div(far_ref[b, j], PLANE) + (NX - lax.div(at_ref[0], NZ)), NX)
            mine = plane_ref[lax.rem(far_ref[b, j], PLANE)]
            from_below = (steps == NX - 1) | ((steps == 2) & (b == 0))
            both = jnp.where(from_below, below_ref[slot], above_ref[slot])
            both = jnp.where(steps == 0, mine, both)
            k_ref[(WIN + j) * BLK : (WIN + j + 1) * BLK, :] = both[:, :DH]
            v_ref[(WIN + j) * BLK : (WIN + j + 1) * BLK, :] = both[:, DH:]
        kt_ref[...] = k_ref[...].astype(F32).T.astype(BF16)
        acc_ref[...] = jnp.zeros_like(acc_ref)
        biases = [
            jnp.where(index >= 2, 0.0, NEG).astype(F32),
            jnp.where(index >= 1, 0.0, NEG).astype(F32),
            None,
        ] + [jnp.where(j < count_ref[b], 0.0, NEG).astype(F32) for j in range(FARS)]
        rows = pl.ds(pl.multiple_of(b * BLK, BLK), BLK)
        for pair in range(GQ // 2):
            lo = pair * 2 * DH
            q2 = jnp.concatenate([q_ref[rows, lo : lo + DH], q_ref[rows, lo + DH : lo + 2 * DH]])
            g2 = jnp.concatenate([g_ref[rows, lo : lo + DH], g_ref[rows, lo + DH : lo + 2 * DH]])
            scores = lax.dot_general(k_ref[...], q2, NT, preferred_element_type=F32)
            parts = [scores[c * BLK : (c + 1) * BLK, :] for c in range(WIN + FARS)]
            parts[WIN - 1] = parts[WIN - 1] + tri_ref[...]
            tops = [
                jnp.max(part, axis=0, keepdims=True) + (0.0 if bias is None else bias)
                for part, bias in zip(parts, biases)
            ]
            top = functools.reduce(jnp.maximum, tops)
            expo = jnp.concatenate(
                [
                    jnp.exp2((part - (top if bias is None else top - bias)) * EXP2_SCALE)
                    for part, bias in zip(parts, biases)
                ]
            )
            inv = 1.0 / jnp.sum(expo, axis=0, keepdims=True)
            soft = expo * inv
            grad_p = lax.dot_general(v_ref[...], g2, NT, preferred_element_type=F32)
            delta = jnp.sum(soft * grad_p, axis=0, keepdims=True)
            soft_b = soft.astype(BF16)
            grad_s = (soft * (grad_p - delta)).astype(BF16)
            acc_ref[:, :DH] += jnp.dot(grad_s, q2, preferred_element_type=F32)
            acc_ref[:, DH:] += jnp.dot(soft_b, g2, preferred_element_type=F32)
            grad_q = jnp.dot(kt_ref[...], grad_s, preferred_element_type=F32).T * SCALE
            qg_ref[rows, lo : lo + DH] = grad_q[:BLK].astype(BF16)
            qg_ref[rows, lo + DH : lo + 2 * DH] = grad_q[BLK:].astype(BF16)
        acc_ref[:, :DH] = acc_ref[:, :DH] * SCALE
        window = pl.ds(pl.multiple_of(b * BLK, BLK), WIN * BLK)
        win_ref[window, :] += acc_ref[: WIN * BLK, :]
        for j in range(FARS):
            farg_ref[b * FARS + j] = acc_ref[(WIN + j) * BLK : (WIN + j + 1) * BLK, :].astype(BF16)
        return carry

    for b in range(NB):
        block(b, 0)


def attend(at, far, count, queries, out_grad, prev, own, plane, below, above):
    keys = (WIN + FARS) * BLK
    return pl.pallas_call(
        attend_kernel,
        out_shape=(
            jax.ShapeDtypeStruct((NB * BLK, GQ * DH), BF16),
            jax.ShapeDtypeStruct((2 * NB * BLK, 2 * DH), F32),
            jax.ShapeDtypeStruct((SLOTS, BLK, 2 * DH), BF16),
        ),
        in_specs=[SMEM, SMEM, SMEM] + [VMEM] * 7,
        out_specs=(VMEM, VMEM, VMEM),
        scratch_shapes=[
            pltpu.VMEM((keys, DH), BF16),
            pltpu.VMEM((keys, DH), BF16),
            pltpu.VMEM((DH, keys), BF16),
            pltpu.VMEM((keys, 2 * DH), F32),
            pltpu.VMEM((BLK, 2 * BLK), F32),
        ],
        compiler_params=params(24),
        cost_estimate=pl.CostEstimate(flops=2_400_000_000 * 4, bytes_accessed=6 << 20, transcendentals=2_000_000),
        name="attend",
    )(at, far, count, queries, out_grad, prev, own, plane, below, above)


def spread_kernel(at_ref, *refs):
    lists, pieces = refs[:NX], refs[NX:-2]
    out_ref, acc_ref = refs[-2:]
    mine, below, above, across_low, across_high = pieces
    x_at = lax.div(at_ref[0], NZ)
    acc_ref[...] = jnp.zeros_like(acc_ref)

    def add(listed, term_ref, j):
        @pl.when(lax.div(listed, PLANE) == x_at)
        def _():
            acc_ref[lax.rem(listed, PLANE)] += term_ref[j].astype(F32)

    half = SLOTS // 2
    for j in range(SLOTS):
        add(lists[0][j // FARS, j % FARS], mine, j)
        add(lists[1][j // FARS, j % FARS], above, j)
        add(lists[2][j // FARS, j % FARS], across_low if j < half else across_high, j % half)
        add(lists[3][j // FARS, j % FARS], below, j)
    out_ref[...] = acc_ref[...].astype(BF16)


def spread(at, lists, own, pieces):
    return pl.pallas_call(
        spread_kernel,
        out_shape=jax.ShapeDtypeStruct((PLANE, BLK, 2 * DH), BF16),
        in_specs=[SMEM] * (1 + NX) + [VMEM] * (1 + len(pieces)),
        out_specs=VMEM,
        scratch_shapes=[pltpu.VMEM((PLANE, BLK, 2 * DH), F32)],
        compiler_params=params(16),
        name="spread_far",
    )(at, *lists, own, *pieces)


def finish_kernel(terms_ref, back_ref, window_ref, out_ref):
    total = window_ref[NB * BLK :, :] + back_ref[...].astype(F32)
    for z in range(NZ):
        total += terms_ref[z].astype(F32)
    source = lax.broadcasted_iota(jnp.int32, (2 * DH, 2 * DH), 0)
    target = lax.broadcasted_iota(jnp.int32, (2 * DH, 2 * DH), 1)
    part, rest = target // (2 * PART), target % (2 * PART)
    wanted = (rest // PART) * DH + part * PART + rest % PART
    order = jnp.where(source == wanted, 1.0, 0.0).astype(BF16)
    out_ref[...] = jnp.dot(
        total.astype(BF16), order, preferred_element_type=F32
    ).astype(BF16)


def finish(terms, back, window):
    return pl.pallas_call(
        finish_kernel,
        out_shape=jax.ShapeDtypeStruct((NB * BLK, 2 * DH), BF16),
        in_specs=[VMEM] * 3,
        out_specs=VMEM,
        compiler_params=params(12),
        name="finish_kv",
    )(terms, back, window)


def heads_kernel(at_ref, own_ref, *refs):
    *pieces, other_ref, out_ref = refs
    at, core = lax.div(at_ref[0], 2), lax.rem(at_ref[0], 2)
    rows = NB * BLK
    half = rows // 2
    below, above = lax.rem(at + NY - 1, NY), lax.rem(at + 1, NY)
    across = lax.rem(at + 2, NY)
    starts = (0, rows, 2 * rows, 3 * rows, 3 * rows + half)
    for k, (y, low, high) in enumerate(
        ((at, 0, rows), (below, 0, rows), (above, 0, rows), (across, 0, half), (across, half, rows))
    ):
        mine = own_ref if k == 0 else pieces[k - 1]
        out_ref[2 * y + core, low:high, :] = mine[...]
        out_ref[2 * y + 1 - core, low:high, :] = other_ref[starts[k] : starts[k] + high - low, :]


def place_heads(at, own, pieces, other):
    return pl.pallas_call(
        heads_kernel,
        out_shape=jax.ShapeDtypeStruct((2 * NY, *own.shape), BF16),
        in_specs=[SMEM] + [VMEM] * (2 + len(pieces)),
        out_specs=VMEM,
        compiler_params=params(8),
        name="place_heads",
    )(at, own, *pieces, other)


def weights_kernel(grad_ref, inputs_ref, out_ref):
    quarters, wide = 4, inputs_ref.shape[1] // 4
    for head in range(2):
        grad = jnp.concatenate([grad_ref[x * 2 + head] for x in range(NX)])
        term = lax.dot_general(
            grad, inputs_ref[...], (((0,), (0,)), ((), ())), preferred_element_type=F32
        ).astype(BF16)
        for part in range(4):
            for quarter in range(quarters):
                out_ref[
                    head * 4 + part, quarter * 2 * PART : (quarter + 1) * 2 * PART, :
                ] = term[
                    part * 2 * PART : (part + 1) * 2 * PART, quarter * wide : (quarter + 1) * wide
                ]


def weight_terms(grad, inputs_x):
    return pl.pallas_call(
        weights_kernel,
        out_shape=jax.ShapeDtypeStruct((NZ, 4 * 2 * PART, inputs_x.shape[1] // 4), BF16),
        in_specs=[VMEM, VMEM],
        out_specs=VMEM,
        compiler_params=params(16),
        cost_estimate=pl.CostEstimate(flops=1 << 30, bytes_accessed=4 << 20, transcendentals=0),
        name="weight_terms",
    )(grad, inputs_x)


def weight_sum_kernel(terms_ref, key_ref, value_ref):
    total = terms_ref[0].astype(F32)
    for z in range(1, NZ):
        total += terms_ref[z].astype(F32)
    wide = total.shape[1]
    for quarter in range(4):
        low = quarter * 2 * PART
        key_ref[:, quarter * wide : (quarter + 1) * wide] = total[low : low + PART]
        value_ref[:, quarter * wide : (quarter + 1) * wide] = total[low + PART : low + 2 * PART]


def weight_sum(terms):
    out = jax.ShapeDtypeStruct((PART, 4 * terms.shape[2]), F32)
    return pl.pallas_call(
        weight_sum_kernel,
        out_shape=(out, out),
        in_specs=[VMEM],
        out_specs=(VMEM, VMEM),
        compiler_params=params(8),
        name="weight_sum",
    )(terms)


def input_kernel(at_ref, grad_ref, weights_ref, mine_ref, above_ref, low_ref, high_ref, below_ref):
    x_at = lax.div(at_ref[0], NZ)
    half = low_ref.shape[0]
    for steps in range(NX):
        x = lax.rem(x_at + steps, NX)
        grad = jnp.concatenate([grad_ref[2 * x], grad_ref[2 * x + 1]], axis=1)
        term = jnp.dot(grad, weights_ref[...], preferred_element_type=F32)
        if steps == 2:
            low_ref[...] = term[:half].astype(BF16)
            high_ref[...] = term[half:].astype(BF16)
        else:
            out_ref = (mine_ref, above_ref, None, below_ref)[steps]
            out_ref[...] = term.astype(out_ref.dtype)


def input_terms(at, grad, weights):
    rows, wide = grad.shape[1], weights.shape[1]
    send, half = (jax.ShapeDtypeStruct((size, wide), BF16) for size in (rows, rows // 2))
    return pl.pallas_call(
        input_kernel,
        out_shape=(jax.ShapeDtypeStruct((rows, wide), F32), send, half, half, send),
        in_specs=[SMEM, VMEM, VMEM],
        out_specs=(VMEM,) * 5,
        compiler_params=params(16),
        cost_estimate=pl.CostEstimate(flops=1 << 30, bytes_accessed=4 << 20, transcendentals=0),
        name="input_terms",
    )(at, grad, weights)


def added(term, arrived, low):
    high = low + arrived.shape[0]
    rows = (term[low:high].astype(F32) + arrived.astype(F32)).astype(BF16)
    return jnp.concatenate([term[:low], rows, term[high:]])


def local(
    queries, key_rows, value_rows, out_grad, inputs, key_weight, value_weight, far_blocks, far_count
):
    tokens = queries.shape[0]
    seq_index = lax.axis_index("seq").astype(jnp.int32)
    at = seq_index.reshape(1)
    own_index = lax.axis_index("own").astype(jnp.int32).reshape(1)
    own_kv = jnp.concatenate([key_rows, value_rows], axis=1).reshape(NB, BLK, 2 * DH)

    from_below, from_above = both_ways(own_kv, own_kv, "seq", Z_UP)
    across = [(x * NZ + z, (x + 2) % NX * NZ + z) for x in range(NX) for z in range(NZ)]
    list_across = lax.ppermute(far_blocks, "seq", across)
    from_below, from_above, list_across, listed = lax.optimization_barrier(
        (from_below, from_above, list_across, far_blocks)
    )
    plane = [from_below, from_above]
    for distance in range(2, NZ // 2 + 1):
        if distance == NZ // 2:
            from_below, from_above = from_below[: NB // 2], from_above[NB // 2 :]
        from_below, from_above = both_ways(from_below, from_above, "seq", Z_UP)
        plane += [from_below, from_above]
    prev_kv = shifted(own_kv, "seq", 1)
    plane, low, high = pick_across(at, list_across, own_kv, plane)
    low, high, listed, key_weight, value_weight = lax.optimization_barrier(
        (low, high, listed, key_weight, value_weight)
    )
    weights = jnp.concatenate([key_weight.T, value_weight.T])
    weights = lax.all_gather(weights, "seq", axis=0, axis_index_groups=Z_GROUPS, tiled=True)
    low, high = both_ways(low, high, "seq", X_UP)
    list_below, list_above = both_ways(listed, listed, "seq", X_UP)
    up, down = pick(at, list_above, list_below, plane, low, high)
    from_below, from_above = both_ways(up, down, "seq", X_UP)

    query_grad, window, far_grad = attend(
        at, far_blocks, far_count, queries, out_grad, prev_kv, own_kv, plane, from_below, from_above
    )
    back = shifted(window[:tokens].astype(BF16), "seq", -1)
    far_below, far_above = both_ways(far_grad, far_grad, "seq", X_UP)
    far_below, far_above, back, inputs = lax.optimization_barrier(
        (far_below, far_above, back, inputs)
    )
    far_across = both_ways(far_below[:FARS], far_above[FARS:], "seq", X_UP)
    far_all = (far_below, far_above, *far_across)
    inputs_x = lax.all_gather(inputs, "seq", axis=0, axis_index_groups=X_GROUPS, tiled=True)
    lists = (far_blocks, list_above, list_across, list_below)
    dense = spread(at, lists, far_grad, far_all)
    dense = dense.reshape(NZ, tokens, 2 * DH)
    terms = lax.all_to_all(dense, "seq", 0, 0, axis_index_groups=Z_GROUPS, tiled=True)
    kv_grad = finish(terms, back, window)

    moved = lax.ppermute(kv_grad, ("seq", "own"), SWAP_XY)
    moved, inputs_x, weights = lax.optimization_barrier((moved, inputs_x, weights))
    same_core = ring_gather(moved, "own", Y_UP, NY)
    other_core = lax.ppermute(jnp.concatenate([moved, *same_core]), "own", CORES)
    heads = place_heads(own_index, moved, same_core, other_core)

    mine, above, low, high, below = input_terms(at, heads, weights)
    from_below, from_above = both_ways(low, high, "seq", X_UP)
    pieces = weight_terms(heads, inputs_x)
    pieces = lax.all_to_all(pieces, "seq", 0, 0, axis_index_groups=Z_GROUPS, tiled=True)
    above, below = added(above, from_below, 0), added(below, from_above, tokens // 2)
    from_below, from_above = both_ways(above, below, "seq", X_UP)
    input_grad = mine + from_below.astype(F32) + from_above.astype(F32)
    key_weight_grad, value_weight_grad = weight_sum(pieces)
    return (query_grad, input_grad.astype(BF16), key_weight_grad.T, value_weight_grad.T)


def solution(mesh):
    return jax.shard_map(
        local,
        mesh=mesh,
        in_specs=(
            P("seq", "own"),
            P("seq", "own"),
            P("seq", "own"),
            P("seq", "own"),
            P("seq", "own"),
            P("own", "seq"),
            P("own", "seq"),
            P("seq", None),
            P("seq"),
        ),
        out_specs=(P("seq", "own"), P("seq", "own"), P("own", "seq"), P("own", "seq")),
        check_vma=False,
    )
```
